256 devices in a mesh: batch: 4 (over x), tm: 16 (over z, core), label: 4 (over y).
Axes of the slice: x: 4, y: 4, z: 8, core: 2. Of those that a mesh axis runs over, the one named last changes fastest.
Arguments:
- enc_joint: bfloat16 [4, 384, 640], P('batch', 'tm'), may hold values from -6 to 6
- pred_joint: bfloat16 [4, 320, 640], P('batch', 'label'), may hold values from -6 to 6
- out_weight: bfloat16 [640, 4096], P('batch', 'tm'), may hold values from -1.1953125 to 1.1953125
- labels: int32 [4, 320], P('batch', 'label'), may hold values from 0 to 4095
- frame_len: int32 [4], P('batch'), may hold values from 192 to 384, as said below
- label_len: int32 [4], P('batch'), may hold values from 80 to 319, as said below
Outputs:
- log_blank: float32 [4, 384, 320], P('batch', 'tm', 'label')
- log_label: float32 [4, 384, 320], P('batch', 'tm', 'label')
- loss: float32 [4], P('batch')
The draws below stay inside these ranges and needn't reach their ends.
Inputs may be any that keep to these rules, and one draw needn't show every extreme that they name: `frame_len`: some utterance has 384 frames. `label_len`: some utterance has 319 labels.
All inputs are finite; a program needn't handle non-finite values.
Results may differ from the reference program's by a relative error of at most 0.00063.
Values may be sent and summed in bfloat16 or wider, within the bound.
No kernel may reach another device: no remote copies, remote signals or barrier semaphores. Data moves between devices by JAX's collectives and lax.ppermute only.
A program may use at most 128 MiB of HBM per device.

```python
import math
import jax
import jax.numpy as jnp
import numpy as np
from jax import lax

J = 640
V = 4096
BATCH = 4
FRAMES = 384
POS = 320


def draw_frame_len(key, part):
    key = jax.random.fold_in(key, 11)
    values = jax.random.randint(key, (BATCH,), FRAMES // 2, FRAMES + 1)
    return values.at[0].set(FRAMES).astype(jnp.int32)


def draw_label_len(key, part):
    key = jax.random.fold_in(key, 23)
    values = jax.random.randint(key, (BATCH,), POS // 4, POS)
    return values.at[BATCH - 1].set(POS - 1).astype(jnp.int32)


def with_ends(array, key, low, largest):
    shape = array.shape
    place = [jax.random.randint(jax.random.fold_in(key, axis), (), 0, shape[axis]) for axis in range(len(shape))]
    array = array.at[tuple(place)].set(low)
    longest = shape.index(max(shape))
    place[longest] = (place[longest] + 1) % shape[longest]
    return array.at[tuple(place)].set(largest)


def shard_levels(stream_key, shape, shards, least, top_value):
    def one(position, shards_of):
        steps = jax.random.uniform(jax.random.fold_in(jax.random.fold_in(stream_key, 6), position), (shards_of,), jnp.float32, least / len(shards), top_value / len(shards))
        return jnp.repeat(jnp.exp(steps), shape[position] // shards_of).reshape((-1,) + (1,) * (len(shape) - position - 1))

    gain = one(*shards[0])
    for cut in shards[1:]:
        gain = gain * one(*cut)
    return gain


def rank_bounds(amount, slope):
    weights = [(1 << 20) // math.isqrt(grade ** slope) + 1 for grade in range(1, amount + 1)]
    spread = 1 + sum(weights) // (1 << 30)
    return np.cumsum(np.array([max(1, weight // spread) for weight in weights]))


def ranked_ids(key, dims, count, skew):
    table = rank_bounds(count, skew)
    ticket = jax.random.randint(jax.random.fold_in(key, 1), dims, 0, int(table[count - 1]))
    grade = jnp.searchsorted(jnp.asarray(table, jnp.int32), ticket, side="right")
    return jax.random.permutation(jax.random.fold_in(key, 2), count)[grade].astype(jnp.int32)


def normal_values(rng, shape, spread, most, split=(), kind=jnp.bfloat16):
    level = shard_levels(rng, shape, split, -0.22, 0.18) if split else 1.0
    entries = jax.random.normal(rng, shape, jnp.float32) * spread * level
    return jnp.minimum(jnp.maximum(entries, -most), most).astype(kind)


def setup_inputs(seed: int = 0) -> dict:
    streams_of = jax.random.split(jax.random.key(seed), 7)
    enc_joint = normal_values(streams_of[0], (BATCH, FRAMES, J), 1.0, 6.0, ((0, 4), (1, 16)))
    pred_joint = normal_values(streams_of[1], (BATCH, POS, J), 1.0, 6.0, ((0, 4), (1, 4)))
    out_weight = normal_values(streams_of[2], (J, V), 0.2, 1.1953125, ((0, 4), (1, 16)))
    labels = with_ends(ranked_ids(streams_of[3], (BATCH, POS), V, 2), jax.random.fold_in(streams_of[3], 3), 0, V - 1).astype(jnp.int32)
    frame_len = draw_frame_len(jax.random.fold_in(streams_of[6], 71), 0)
    label_len = draw_label_len(jax.random.fold_in(streams_of[6], 71), 0)
    return dict(enc_joint=enc_joint, pred_joint=pred_joint, out_weight=out_weight, labels=labels, frame_len=frame_len, label_len=label_len)


NEG = -1.0e30


def frame_probs(enc_row, pred, weight, label_row):
    hidden = jnp.tanh(enc_row.astype(jnp.float32)[None, :] + pred.astype(jnp.float32)).astype(jnp.bfloat16)
    logits = jnp.dot(hidden, weight, preferred_element_type=jnp.float32)
    lse = jax.nn.logsumexp(logits, axis=1)
    blank = logits[:, 0] - lse
    picked = jnp.take_along_axis(logits, label_row[:, None], axis=1)[:, 0] - lse
    return blank, picked


def lattice(blank, picked):
    zeros = jnp.zeros((blank.shape[0], 1), blank.dtype)
    costs = jnp.cumsum(jnp.concatenate([zeros, picked[:, :-1]], axis=1), axis=1)
    start = jnp.full((blank.shape[1],), NEG, blank.dtype).at[0].set(0.0)

    def row(carry, inputs):
        cost_row, blank_row = inputs
        xs = cost_row + lax.cumlogsumexp(carry - cost_row)
        return xs + blank_row, xs

    final, alpha = lax.scan(row, start, (costs, blank))
    return alpha


def reference(enc_joint, pred_joint, out_weight, labels, frame_len, label_len):
    def utterance(inputs):
        enc, pred, label_row, flen, ulen = inputs
        blank, picked = lax.map(lambda e: frame_probs(e, pred, out_weight, label_row), enc)
        alpha = lattice(blank, picked)
        value = alpha[flen - 1, ulen] + blank[flen - 1, ulen]
        return blank, picked, -value / flen.astype(blank.dtype)

    log_blank, log_label, loss = lax.map(utterance, (enc_joint, pred_joint, labels, frame_len, label_len))
    return log_blank, log_label, loss
```

```python
import functools

import jax
import jax.numpy as jnp
from jax import lax
from jax.experimental import pallas as pl
from jax.experimental.pallas import tpu as pltpu
from jax.sharding import PartitionSpec as P

NEG = -1e30
F32 = jnp.float32
BF16 = jnp.bfloat16
SPAN = 8
GROUP = 4


def joint_kernel(
    ids_ref, enc_ref, pred_ref, weight_ref,
    lse_ref, blank_ref, picked_ref,
    enc, pred, chosen, picks, hidden_a, hidden_b, logits_a, logits_b, top, total,
):
    frames = enc_ref.shape[0]
    positions, width = pred_ref.shape
    share = weight_ref.shape[0]
    chunk = share // GROUP
    enc[...] = enc_ref[...].astype(F32)
    pred[...] = pred_ref[...].astype(F32)
    columns = lax.broadcasted_iota(jnp.int32, (positions, share), 1)
    one_hot = (columns == ids_ref[...]).astype(F32).astype(BF16)
    chosen[...] = jnp.dot(one_hot, weight_ref[...], preferred_element_type=F32)
    picks[...] = jnp.zeros_like(picks)
    lanes = lax.broadcasted_iota(jnp.int32, picks.shape, 1)

    def make_hidden(frame, part, out):
        rounded = jnp.tanh(pred[...] + enc[pl.ds(frame, 1), :]).astype(BF16)
        out[part * positions:(part + 1) * positions, :] = rounded
        picked = jnp.sum(rounded.astype(F32) * chosen[...], axis=1, keepdims=True)
        picks[...] = jnp.where(lanes == frame, picked, picks[...])

    def multiply(part, hidden, out):
        out[...] = lax.dot_general(
            weight_ref[part * chunk:(part + 1) * chunk, :], hidden[...],
            (((1,), (1,)), ((), ())), preferred_element_type=F32,
        )

    def gather_terms(part, group, logits):
        values = logits[...]
        high = jnp.max(values, axis=0, keepdims=True)
        if part == 0:
            blank_ref[pl.ds(group, 1), :] = logits[0:1, :]
            total[...] = jnp.sum(jnp.exp(values - high), axis=0, keepdims=True)
            top[...] = high
        else:
            high = jnp.maximum(high, top[...])
            total[...] = total[...] * jnp.exp(top[...] - high) + jnp.sum(
                jnp.exp(values - high), axis=0, keepdims=True
            )
            top[...] = high
        if part == GROUP - 1:
            lse_ref[pl.ds(group, 1), :] = top[...] + jnp.log(total[...])

    groups = frames // GROUP
    for part in range(GROUP):
        make_hidden(part, part, hidden_a)
    logits_b[...] = jnp.zeros_like(logits_b)
    top[...] = jnp.zeros_like(top)
    total[...] = jnp.ones_like(total)

    def half(group, now, later):
        for part in range(GROUP):
            fresh, old = (logits_a, logits_b) if part % 2 == 0 else (logits_b, logits_a)
            multiply(part, now, fresh)
            make_hidden(jnp.minimum(group + 1, groups - 1) * GROUP + part, part, later)
            if part == 0:
                gather_terms(GROUP - 1, jnp.maximum(group - 1, 0), old)
            else:
                gather_terms(part - 1, group, old)

    def step(pair, carry):
        half(2 * pair, hidden_a, hidden_b)
        half(2 * pair + 1, hidden_b, hidden_a)
        return carry

    lax.fori_loop(0, groups // 2, step, 0)
    gather_terms(GROUP - 1, groups - 1, logits_b)
    picked_ref[...] = picks[...].T[:frames, :]


def joint_terms(ids, enc, pred, weight):
    frames = enc.shape[0]
    positions, width = pred.shape
    share = weight.shape[0]
    wide = GROUP * positions
    grouped = jax.ShapeDtypeStruct((frames // GROUP, wide), F32)
    vmem = pl.BlockSpec(memory_space=pltpu.VMEM)
    flops = 2 * frames * positions * width * share
    return pl.pallas_call(
        joint_kernel,
        out_shape=(grouped, grouped, jax.ShapeDtypeStruct((frames, positions), F32)),
        in_specs=[vmem] * 4,
        out_specs=(vmem,) * 3,
        scratch_shapes=[
            pltpu.VMEM((frames, width), F32),
            pltpu.VMEM((positions, width), F32),
            pltpu.VMEM((positions, width), F32),
            pltpu.VMEM((positions, 128), F32),
            pltpu.VMEM((wide, width), BF16),
            pltpu.VMEM((wide, width), BF16),
            pltpu.VMEM((share // GROUP, wide), F32),
            pltpu.VMEM((share // GROUP, wide), F32),
            pltpu.VMEM((1, wide), F32),
            pltpu.VMEM((1, wide), F32),
        ],
        compiler_params=pltpu.CompilerParams(vmem_limit_bytes=40 << 20),
        cost_estimate=pl.CostEstimate(flops=flops, bytes_accessed=2 << 20, transcendentals=0),
        name="joint",
    )(ids, enc, pred, weight)


def log_sum(terms):
    if len(terms) == 1:
        return terms[0]
    top = functools.reduce(jnp.maximum, terms)
    return top + jnp.log(functools.reduce(jnp.add, [jnp.exp(term - top) for term in terms]))


def shift_lanes(values, by):
    by = by % values.shape[1]
    return values if by == 0 else pltpu.roll(values, by, 1)


def compose(first, then):
    terms = []
    for count in range(len(first) + len(then) - 1):
        parts = [
            then[late] + shift_lanes(first[count - late], late)
            for late in range(len(then))
            if 0 <= count - late < len(first)
        ]
        terms.append(log_sum(parts))
    return terms


def shear(values, lead):
    rows = values.shape[0]
    lanes = lax.broadcasted_iota(jnp.int32, values.shape, 1)
    if lead:
        values = pltpu.roll(values, rows - lead, 0)
    for bit in (64, 32, 16, 8, 4, 2, 1):
        values = jnp.where((lanes & bit) != 0, pltpu.roll(values, bit, 0), values)
    return values


def lattice_kernel(frame_len_ref, label_len_ref, grid_ref, loss_ref, stay, move, ahead, back):
    blocks, _, frames_dev, positions = grid_ref.shape
    frames = blocks * frames_dev
    strips, diagonals, _ = stay.shape
    lanes_all = 128 * strips
    flen = frame_len_ref[0]
    ulen = label_len_ref[0]
    spare = jnp.full((frames, lanes_all - positions), NEG, F32)
    depth = frames + 128
    pad = jnp.full((depth - frames, 128), NEG, F32)

    def whole(which):
        rows = jnp.concatenate([grid_ref[block, which] for block in range(blocks)], axis=0)
        return jnp.concatenate([rows, spare], axis=1)

    blank = whole(0)
    label = shift_lanes(whole(1), 1)
    stay[...] = jnp.full(stay.shape, NEG, F32)
    move[...] = jnp.full(move.shape, NEG, F32)
    for part in range(strips):
        start = 128 * part
        rows = min(depth, diagonals - start)
        for source, out, lead in ((blank, stay, 0), (label, move, 1)):
            strip = jnp.concatenate([source[:, start:start + 128], pad], axis=0)
            out[part, start:start + rows, :] = shear(strip, lead)[:rows]

    row = lax.broadcasted_iota(jnp.int32, (SPAN, lanes_all), 0)
    lane = lax.broadcasted_iota(jnp.int32, (SPAN, lanes_all), 1)
    in_row = lane < positions
    moves_in = in_row & (lane > 0)
    rest = jnp.where(lane == ulen, 0.0, NEG)

    def every_eighth(table, start):
        at = pl.ds(start, SPAN, stride=SPAN)
        return jnp.concatenate([table[part, at, :] for part in range(strips)], axis=1)

    def build(group, carry):
        base = group * SPAN * SPAN
        steps = []
        for step in range(SPAN):
            time = base + row * SPAN + step - lane
            held = every_eighth(stay, base + step)
            moved = every_eighth(move, base + step)
            held = jnp.where(in_row & (time < flen), held, rest)
            moved = jnp.where(moves_in & (time + 1 < flen), moved, NEG)
            steps.append([held, moved])
        while len(steps) > 1:
            steps = [compose(steps[i], steps[i + 1]) for i in range(0, len(steps), 2)]
        at = pl.multiple_of(group * SPAN, SPAN)
        for count, values in enumerate(steps[0]):
            ahead[count, pl.ds(at, SPAN), :] = values
            back[count, pl.ds(at, SPAN), :] = shift_lanes(values, -count)
        return carry

    lax.fori_loop(0, diagonals // (SPAN * SPAN), build, 0)

    spans = diagonals // SPAN
    place = lax.broadcasted_iota(jnp.int32, (1, lanes_all), 1)

    def sweep(index, carry):
        alpha, beta = carry
        last = spans - 1 - index
        alpha = log_sum(
            [ahead[count, pl.ds(index, 1), :] + shift_lanes(alpha, count) for count in range(SPAN + 1)]
        )
        beta = log_sum(
            [back[count, pl.ds(last, 1), :] + shift_lanes(beta, -count) for count in range(SPAN + 1)]
        )
        return alpha, beta

    alpha = jnp.where(place == 0, 0.0, NEG)
    beta = jnp.where(place == ulen, 0.0, NEG)
    alpha, beta = lax.fori_loop(0, spans // 2, sweep, (alpha, beta))
    both = alpha + beta
    top = jnp.max(both, axis=1, keepdims=True)
    value = top + jnp.log(jnp.sum(jnp.exp(both - top), axis=1, keepdims=True))
    loss_ref[...] = -value / jnp.full((1, 1), flen, jnp.int32).astype(F32)


def lattice_loss(frame_len, label_len, grid):
    blocks, _, frames_dev, positions = grid.shape
    lanes = -(-positions // 128) * 128
    diagonals = -(-(blocks * frames_dev + positions) // (SPAN * SPAN)) * SPAN * SPAN
    assert (diagonals // SPAN) % 2 == 0
    strip = pltpu.VMEM((lanes // 128, diagonals, 128), F32)
    table = pltpu.VMEM((SPAN + 1, diagonals // SPAN, lanes), F32)
    vmem = pl.BlockSpec(memory_space=pltpu.VMEM)
    smem = pl.BlockSpec(memory_space=pltpu.SMEM)
    return pl.pallas_call(
        lattice_kernel,
        out_shape=jax.ShapeDtypeStruct((1, 1), F32),
        in_specs=[smem, smem, vmem],
        out_specs=vmem,
        scratch_shapes=[
            strip,
            strip,
            table,
            table,
        ],
        compiler_params=pltpu.CompilerParams(vmem_limit_bytes=40 << 20),
        name="lattice",
    )(frame_len, label_len, grid)


def shards(enc_joint, pred_joint, out_weight, labels, frame_len, label_len):
    frames = enc_joint.shape[1]
    positions = pred_joint.shape[1]
    n_label = lax.axis_size("label")
    mine = lax.axis_index("label")
    columns = out_weight.shape[1]
    piece = columns // n_label
    with jax.named_scope("gather_inputs"):
        own = lax.dynamic_slice_in_dim(out_weight, mine * piece, piece, axis=1)
        rows = lax.all_gather(own, "batch", axis=0, tiled=True)
        weight = lax.all_gather(rows.T, "tm", axis=0, tiled=True)
        pred = lax.all_gather(pred_joint[0], "label", axis=0, tiled=True)
        ids = lax.all_gather(labels, "label", axis=0, tiled=False).reshape(-1)
    held = (ids // piece) % n_label == mine
    spots = jnp.where(held, ids // columns * piece + ids % piece, -1)
    lse, blank, picked = joint_terms(spots[:, None], enc_joint[0], pred, weight)
    with jax.named_scope("combine_vocab"):
        parts = jnp.stack([lse.reshape(picked.shape), blank.reshape(picked.shape), picked])
        parts = lax.all_gather(parts, "label", axis=0, tiled=False)
        top = jnp.max(parts[:, 0], axis=0)
        norm = top + jnp.log(jnp.sum(jnp.exp(parts[:, 0] - top), axis=0))
        log_blank = parts[0, 1] - norm
        log_label = jnp.sum(parts[:, 2], axis=0) - norm
    out_blank = lax.dynamic_slice_in_dim(log_blank, mine * positions, positions, axis=1)
    out_label = lax.dynamic_slice_in_dim(log_label, mine * positions, positions, axis=1)
    with jax.named_scope("gather_grid"):
        grid = lax.all_gather(jnp.stack([log_blank, log_label]), "tm", axis=0, tiled=False)
    loss = lattice_loss(frame_len, label_len, grid).reshape(1)
    return out_blank[None], out_label[None], loss


def solution(mesh):
    return jax.shard_map(
        shards,
        mesh=mesh,
        in_specs=(
            P("batch", "tm", None),
            P("batch", "label", None),
            P("batch", "tm"),
            P("batch", "label"),
            P("batch"),
            P("batch"),
        ),
        out_specs=(P("batch", "tm", "label"), P("batch", "tm", "label"), P("batch")),
        check_vma=False,
    )
```

```python
import functools

import jax
import jax.numpy as jnp
from jax import lax
from jax.experimental import pallas as pl
from jax.experimental.pallas import tpu as pltpu
from jax.sharding import PartitionSpec as P

NEG = -1e30
F32 = jnp.float32
BF16 = jnp.bfloat16
SPAN = 8
GROUP = 4
CHUNKS = 2
LABEL_WAYS = 4
BATCH_WAYS = 4


def joint_kernel(
    place_ref, enc_ref, *refs,
):
    mine, batch = place_ref[0], place_ref[1]
    preds, refs = refs[:LABEL_WAYS], refs[LABEL_WAYS:]
    pieces, refs = refs[:BATCH_WAYS], refs[BATCH_WAYS:]
    lse_ref, blank_ref, picked_ref = refs[:3]
    enc, pred, ids, chosen, picks, columns_first, weight, hidden_a, hidden_b, logits_a, logits_b, top, total = refs[3:]
    frames, width = enc_ref.shape
    positions = pred.shape[0]
    share = weight.shape[0]
    chunk = share // CHUNKS
    enc[...] = enc_ref[...].astype(F32)

    held = positions // LABEL_WAYS
    for shift, ref in enumerate(preds):
        at = pl.multiple_of(lax.rem(mine - shift + LABEL_WAYS, LABEL_WAYS) * held, 8)
        values = ref[...].astype(F32)
        pred[pl.ds(at, held), :] = values[:, :width]
        ids[pl.ds(at, held), :] = values[:, width:]

    blocks, half_rows, _ = pieces[0].shape
    lane = lax.broadcasted_iota(jnp.int32, (half_rows, 128), 1)
    for shift, ref in enumerate(pieces):
        at = pl.multiple_of(lax.rem(batch - shift + BATCH_WAYS, BATCH_WAYS) * 2 * half_rows, 8)
        for pair in range(blocks // 2):
            left = ref[2 * pair].astype(F32)
            right = ref[2 * pair + 1].astype(F32)
            upper = jnp.where(lane < 64, left, pltpu.roll(right, 64, 1))
            lower = jnp.where(lane < 64, pltpu.roll(left, 64, 1), right)
            columns_first[pl.ds(at, half_rows), 128 * pair:128 * pair + 128] = upper
            columns_first[pl.ds(at + half_rows, half_rows), 128 * pair:128 * pair + 128] = lower
    for tile in range(share // 128):
        weight[128 * tile:128 * tile + 128, :] = columns_first[:, 128 * tile:128 * tile + 128].T.astype(BF16)

    high = ids[:, 0:1].astype(jnp.int32)
    low = ids[:, 1:2].astype(jnp.int32)
    spot = jnp.where((high & 3) == mine, (high >> 2) * 64 + low, -1)
    columns = lax.broadcasted_iota(jnp.int32, (positions, share), 1)
    one_hot = (columns == spot).astype(F32).astype(BF16)
    chosen[...] = jnp.dot(one_hot, weight[...], preferred_element_type=F32)
    picks[...] = jnp.zeros_like(picks)
    lanes = lax.broadcasted_iota(jnp.int32, picks.shape, 1)

    def make_hidden(frame, part, out):
        rounded = jnp.tanh(pred[...] + enc[pl.ds(frame, 1), :]).astype(BF16)
        out[part * positions:(part + 1) * positions, :] = rounded
        picked = jnp.sum(rounded.astype(F32) * chosen[...], axis=1, keepdims=True)
        picks[...] = jnp.where(lanes == frame, picked, picks[...])

    def multiply(part, hidden, out):
        out[...] = lax.dot_general(
            weight[part * chunk:(part + 1) * chunk, :], hidden[...],
            (((1,), (1,)), ((), ())), preferred_element_type=F32,
        )

    def gather_terms(part, group, logits):
        values = logits[...]
        high = jnp.max(values, axis=0, keepdims=True)
        if part == 0:
            blank_ref[pl.ds(group, 1), :] = logits[0:1, :]
            total[...] = jnp.sum(jnp.exp(values - high), axis=0, keepdims=True)
            top[...] = high
        else:
            high = jnp.maximum(high, top[...])
            total[...] = total[...] * jnp.exp(top[...] - high) + jnp.sum(
                jnp.exp(values - high), axis=0, keepdims=True
            )
            top[...] = high
        if part == CHUNKS - 1:
            lse_ref[pl.ds(group, 1), :] = top[...] + jnp.log(total[...])

    groups = frames // GROUP
    for part in range(GROUP):
        make_hidden(part, part, hidden_a)
    logits_b[...] = jnp.zeros_like(logits_b)
    top[...] = jnp.zeros_like(top)
    total[...] = jnp.ones_like(total)
    each = GROUP // CHUNKS

    def half(group, now, later):
        for part in range(CHUNKS):
            fresh, old = (logits_a, logits_b) if part % 2 == 0 else (logits_b, logits_a)
            multiply(part, now, fresh)
            for which in range(part * each, (part + 1) * each):
                make_hidden(jnp.minimum(group + 1, groups - 1) * GROUP + which, which, later)
            if part == 0:
                gather_terms(CHUNKS - 1, jnp.maximum(group - 1, 0), old)
            else:
                gather_terms(part - 1, group, old)

    def step(pair, carry):
        half(2 * pair, hidden_a, hidden_b)
        half(2 * pair + 1, hidden_b, hidden_a)
        return carry

    lax.fori_loop(0, groups // 2, step, 0)
    gather_terms(CHUNKS - 1, groups - 1, logits_b)
    picked_ref[...] = picks[...].T[:frames, :]


def joint_terms(place, enc, preds, pieces):
    frames, width = enc.shape
    positions = LABEL_WAYS * preds[0].shape[0]
    blocks, half_rows, _ = pieces[0].shape
    share = 64 * blocks
    wide = GROUP * positions
    grouped = jax.ShapeDtypeStruct((frames // GROUP, wide), F32)
    vmem = pl.BlockSpec(memory_space=pltpu.VMEM)
    smem = pl.BlockSpec(memory_space=pltpu.SMEM)
    flops = 2 * frames * positions * width * share
    return pl.pallas_call(
        joint_kernel,
        out_shape=(grouped, grouped, jax.ShapeDtypeStruct((frames, positions), F32)),
        in_specs=[smem] + [vmem] * (1 + len(preds) + len(pieces)),
        out_specs=(vmem,) * 3,
        scratch_shapes=[
            pltpu.VMEM((frames, width), F32),
            pltpu.VMEM((positions, width), F32),
            pltpu.VMEM((positions, 128), F32),
            pltpu.VMEM((positions, width), F32),
            pltpu.VMEM((positions, 128), F32),
            pltpu.VMEM((width, share), F32),
            pltpu.VMEM((share, width), BF16),
            pltpu.VMEM((wide, width), BF16),
            pltpu.VMEM((wide, width), BF16),
            pltpu.VMEM((share // CHUNKS, wide), F32),
            pltpu.VMEM((share // CHUNKS, wide), F32),
            pltpu.VMEM((1, wide), F32),
            pltpu.VMEM((1, wide), F32),
        ],
        compiler_params=pltpu.CompilerParams(vmem_limit_bytes=48 << 20),
        cost_estimate=pl.CostEstimate(flops=flops, bytes_accessed=2 << 20, transcendentals=0),
        name="joint",
    )(place, enc, *preds, *pieces)


def log_sum(terms):
    if len(terms) == 1:
        return terms[0]
    top = functools.reduce(jnp.maximum, terms)
    return top + jnp.log(functools.reduce(jnp.add, [jnp.exp(term - top) for term in terms]))


def shift_lanes(values, by):
    by = by % values.shape[1]
    return values if by == 0 else pltpu.roll(values, by, 1)


def compose(first, then):
    terms = []
    for count in range(len(first) + len(then) - 1):
        parts = [
            then[late] + shift_lanes(first[count - late], late)
            for late in range(len(then))
            if 0 <= count - late < len(first)
        ]
        terms.append(log_sum(parts))
    return terms


def shear(values, lead):
    rows = values.shape[0]
    lanes = lax.broadcasted_iota(jnp.int32, values.shape, 1)
    if lead:
        values = pltpu.roll(values, rows - lead, 0)
    for bit in (64, 32, 16, 8, 4, 2, 1):
        values = jnp.where((lanes & bit) != 0, pltpu.roll(values, bit, 0), values)
    return values


def lattice_kernel(frame_len_ref, label_len_ref, grid_ref, loss_ref, stay, move, ahead, back):
    blocks, _, frames_dev, positions = grid_ref.shape
    frames = blocks * frames_dev
    strips, diagonals, _ = stay.shape
    lanes_all = 128 * strips
    flen = frame_len_ref[0]
    ulen = label_len_ref[0]
    spare = jnp.full((frames, lanes_all - positions), NEG, F32)
    depth = frames + 128
    pad = jnp.full((depth - frames, 128), NEG, F32)

    def whole(which):
        rows = jnp.concatenate([grid_ref[block, which] for block in range(blocks)], axis=0)
        return jnp.concatenate([rows, spare], axis=1)

    blank = whole(0)
    label = shift_lanes(whole(1), 1)
    stay[...] = jnp.full(stay.shape, NEG, F32)
    move[...] = jnp.full(move.shape, NEG, F32)
    for part in range(strips):
        start = 128 * part
        rows = min(depth, diagonals - start)
        for source, out, lead in ((blank, stay, 0), (label, move, 1)):
            strip = jnp.concatenate([source[:, start:start + 128], pad], axis=0)
            out[part, start:start + rows, :] = shear(strip, lead)[:rows]

    row = lax.broadcasted_iota(jnp.int32, (SPAN, lanes_all), 0)
    lane = lax.broadcasted_iota(jnp.int32, (SPAN, lanes_all), 1)
    in_row = lane < positions
    moves_in = in_row & (lane > 0)
    rest = jnp.where(lane == ulen, 0.0, NEG)

    def every_eighth(table, start):
        at = pl.ds(start, SPAN, stride=SPAN)
        return jnp.concatenate([table[part, at, :] for part in range(strips)], axis=1)

    def build(group, carry):
        base = group * SPAN * SPAN
        steps = []
        for step in range(SPAN):
            time = base + row * SPAN + step - lane
            held = every_eighth(stay, base + step)
            moved = every_eighth(move, base + step)
            held = jnp.where(in_row & (time < flen), held, rest)
            moved = jnp.where(moves_in & (time + 1 < flen), moved, NEG)
            steps.append([held, moved])
        while len(steps) > 1:
            steps = [compose(steps[i], steps[i + 1]) for i in range(0, len(steps), 2)]
        at = pl.multiple_of(group * SPAN, SPAN)
        for count, values in enumerate(steps[0]):
            ahead[count, pl.ds(at, SPAN), :] = values
            back[count, pl.ds(at, SPAN), :] = shift_lanes(values, -count)
        return carry

    lax.fori_loop(0, diagonals // (SPAN * SPAN), build, 0)

    spans = diagonals // SPAN
    place = lax.broadcasted_iota(jnp.int32, (1, lanes_all), 1)

    def sweep(index, carry):
        alpha, beta = carry
        last = spans - 1 - index
        alpha = log_sum(
            [ahead[count, pl.ds(index, 1), :] + shift_lanes(alpha, count) for count in range(SPAN + 1)]
        )
        beta = log_sum(
            [back[count, pl.ds(last, 1), :] + shift_lanes(beta, -count) for count in range(SPAN + 1)]
        )
        return alpha, beta

    alpha = jnp.where(place == 0, 0.0, NEG)
    beta = jnp.where(place == ulen, 0.0, NEG)
    alpha, beta = lax.fori_loop(0, spans // 2, sweep, (alpha, beta))
    both = alpha + beta
    top = jnp.max(both, axis=1, keepdims=True)
    value = top + jnp.log(jnp.sum(jnp.exp(both - top), axis=1, keepdims=True))
    loss_ref[...] = -value / jnp.full((1, 1), flen, jnp.int32).astype(F32)


def lattice_loss(frame_len, label_len, grid):
    blocks, _, frames_dev, positions = grid.shape
    lanes = -(-positions // 128) * 128
    diagonals = -(-(blocks * frames_dev + positions) // (SPAN * SPAN)) * SPAN * SPAN
    assert (diagonals // SPAN) % 2 == 0
    strip = pltpu.VMEM((lanes // 128, diagonals, 128), F32)
    table = pltpu.VMEM((SPAN + 1, diagonals // SPAN, lanes), F32)
    vmem = pl.BlockSpec(memory_space=pltpu.VMEM)
    smem = pl.BlockSpec(memory_space=pltpu.SMEM)
    return pl.pallas_call(
        lattice_kernel,
        out_shape=jax.ShapeDtypeStruct((1, 1), F32),
        in_specs=[smem, smem, vmem],
        out_specs=vmem,
        scratch_shapes=[
            strip,
            strip,
            table,
            table,
        ],
        compiler_params=pltpu.CompilerParams(vmem_limit_bytes=40 << 20),
        name="lattice",
    )(frame_len, label_len, grid)


def around(array, axis):
    size = lax.axis_size(axis)
    moved = [
        lax.ppermute(array, axis, [(i, (i + by) % size) for i in range(size)])
        for by in range(1, size)
    ]
    return [array] + moved


def shards(enc_joint, pred_joint, out_weight, labels, frame_len, label_len):
    positions = pred_joint.shape[1]
    mine = lax.axis_index("label")
    rows, columns = out_weight.shape
    piece = columns // LABEL_WAYS
    with jax.named_scope("gather_weight"):
        own = lax.dynamic_slice_in_dim(out_weight, mine * piece, piece, axis=1)
        own = jnp.concatenate([own[:rows // 2], own[rows // 2:]], axis=1)
        blocks = lax.all_gather(own, "tm", axis=0, tiled=False)
        pieces = around(blocks, "batch")
    with jax.named_scope("gather_positions"):
        digits = jnp.stack([labels[0] // piece, labels[0] % piece], axis=1).astype(BF16)
        digits = jnp.pad(digits, ((0, 0), (0, 126)))
        packed = jnp.concatenate([pred_joint[0], digits], axis=1)
        preds = around(packed, "label")
    place = jnp.stack([mine, lax.axis_index("batch")]).astype(jnp.int32)
    lse, blank, picked = joint_terms(place, enc_joint[0], preds, pieces)
    with jax.named_scope("combine_vocab"):
        blank = jnp.where(mine == 0, blank, 0.0)
        parts = jnp.stack([lse.reshape(picked.shape), blank.reshape(picked.shape), picked])
        parts = around(parts, "label")
        top = functools.reduce(jnp.maximum, [part[0] for part in parts])
        norm = top + jnp.log(sum(jnp.exp(part[0] - top) for part in parts))
        log_blank = sum(part[1] for part in parts) - norm
        log_label = sum(part[2] for part in parts) - norm
    out_blank = lax.dynamic_slice_in_dim(log_blank, mine * positions, positions, axis=1)
    out_label = lax.dynamic_slice_in_dim(log_label, mine * positions, positions, axis=1)
    with jax.named_scope("gather_grid"):
        grid = lax.all_gather(jnp.stack([log_blank, log_label]), "tm", axis=0, tiled=False)
    loss = lattice_loss(frame_len, label_len, grid).reshape(1)
    return out_blank[None], out_label[None], loss


def solution(mesh):
    return jax.shard_map(
        shards,
        mesh=mesh,
        in_specs=(
            P("batch", "tm", None),
            P("batch", "label", None),
            P("batch", "tm"),
            P("batch", "label"),
            P("batch"),
            P("batch"),
        ),
        out_specs=(P("batch", "tm", "label"), P("batch", "tm", "label"), P("batch")),
        check_vma=False,
    )
```

```python
import functools

import jax
import jax.numpy as jnp
from jax import lax
from jax.experimental import pallas as pl
from jax.experimental.pallas import tpu as pltpu
from jax.sharding import PartitionSpec as P

NEG = -1e30
F32 = jnp.float32
BF16 = jnp.bfloat16
SPAN = 8
GROUP = 4
CHUNKS = 2
LABEL_WAYS = 4
BATCH_WAYS = 4


def joint_kernel(
    place_ref, enc_ref, *refs
):
    mine, batch = place_ref[0], place_ref[1]
    preds, refs = refs[:LABEL_WAYS], refs[LABEL_WAYS:]
    own_ref, fetched_ref, lse_ref, blank_ref, picked_ref = refs[:5]
    enc, pred, ids, chosen, picks, columns_first, weight, hidden_a, hidden_b, logits_a, logits_b, top, total = refs[5:]
    frames, width = enc_ref.shape
    positions = pred.shape[0]
    share = weight.shape[0]
    chunk = share // CHUNKS
    enc[...] = enc_ref[...].astype(F32)

    held = positions // LABEL_WAYS
    for shift, ref in enumerate(preds):
        at = pl.multiple_of(lax.rem(mine - shift + LABEL_WAYS, LABEL_WAYS) * held, 8)
        values = ref[...].astype(F32)
        pred[pl.ds(at, held), :] = values[:, :width]
        ids[pl.ds(at, held), :] = values[:, width:]

    blocks, half_rows, _ = own_ref.shape
    lane = lax.broadcasted_iota(jnp.int32, (half_rows, 128), 1)
    for shift in range(BATCH_WAYS):
        at = pl.multiple_of(lax.rem(batch - shift + BATCH_WAYS, BATCH_WAYS) * 2 * half_rows, 8)

        def block(index):
            if shift == 0:
                return own_ref[index].astype(F32)
            some = blocks // 2
            return fetched_ref[index // some, shift - 1, index % some].astype(F32)

        for pair in range(blocks // 2):
            left = block(2 * pair)
            right = block(2 * pair + 1)
            upper = jnp.where(lane < 64, left, pltpu.roll(right, 64, 1))
            lower = jnp.where(lane < 64, pltpu.roll(left, 64, 1), right)
            columns_first[pl.ds(at, half_rows), 128 * pair:128 * pair + 128] = upper
            columns_first[pl.ds(at + half_rows, half_rows), 128 * pair:128 * pair + 128] = lower
    for tile in range(share // 128):
        weight[128 * tile:128 * tile + 128, :] = columns_first[:, 128 * tile:128 * tile + 128].T.astype(BF16)

    high = ids[:, 0:1].astype(jnp.int32)
    low = ids[:, 1:2].astype(jnp.int32)
    spot = jnp.where((high & 3) == mine, (high >> 2) * 64 + low, -1)
    columns = lax.broadcasted_iota(jnp.int32, (positions, share), 1)
    one_hot = (columns == spot).astype(F32).astype(BF16)
    chosen[...] = jnp.dot(one_hot, weight[...], preferred_element_type=F32)
    picks[...] = jnp.zeros_like(picks)
    lanes = lax.broadcasted_iota(jnp.int32, picks.shape, 1)

    def make_hidden(frame, part, out):
        rounded = jnp.tanh(pred[...] + enc[pl.ds(frame, 1), :]).astype(BF16)
        out[part * positions:(part + 1) * positions, :] = rounded
        picked = jnp.sum(rounded.astype(F32) * chosen[...], axis=1, keepdims=True)
        picks[...] = jnp.where(lanes == frame, picked, picks[...])

    def multiply(part, hidden, out):
        out[...] = lax.dot_general(
            weight[part * chunk:(part + 1) * chunk, :], hidden[...],
            (((1,), (1,)), ((), ())), preferred_element_type=F32,
        )

    def gather_terms(part, group, logits):
        values = logits[...]
        high = jnp.max(values, axis=0, keepdims=True)
        if part == 0:
            blank_ref[pl.ds(group, 1), :] = logits[0:1, :]
            total[...] = jnp.sum(jnp.exp(values - high), axis=0, keepdims=True)
            top[...] = high
        else:
            high = jnp.maximum(high, top[...])
            total[...] = total[...] * jnp.exp(top[...] - high) + jnp.sum(
                jnp.exp(values - high), axis=0, keepdims=True
            )
            top[...] = high
        if part == CHUNKS - 1:
            lse_ref[pl.ds(group, 1), :] = top[...] + jnp.log(total[...])

    groups = frames // GROUP
    for part in range(GROUP):
        make_hidden(part, part, hidden_a)
    logits_b[...] = jnp.zeros_like(logits_b)
    top[...] = jnp.zeros_like(top)
    total[...] = jnp.ones_like(total)
    each = GROUP // CHUNKS

    def half(group, now, later):
        for part in range(CHUNKS):
            fresh, old = (logits_a, logits_b) if part % 2 == 0 else (logits_b, logits_a)
            multiply(part, now, fresh)
            for which in range(part * each, (part + 1) * each):
                make_hidden(jnp.minimum(group + 1, groups - 1) * GROUP + which, which, later)
            if part == 0:
                gather_terms(CHUNKS - 1, jnp.maximum(group - 1, 0), old)
            else:
                gather_terms(part - 1, group, old)

    def step(pair, carry):
        half(2 * pair, hidden_a, hidden_b)
        half(2 * pair + 1, hidden_b, hidden_a)
        return carry

    lax.fori_loop(0, groups // 2, step, 0)
    gather_terms(CHUNKS - 1, groups - 1, logits_b)
    picked_ref[...] = picks[...].T[:frames, :]


def joint_terms(place, enc, preds, own, fetched):
    frames, width = enc.shape
    positions = LABEL_WAYS * preds[0].shape[0]
    share = 64 * own.shape[0]
    wide = GROUP * positions
    grouped = jax.ShapeDtypeStruct((frames // GROUP, wide), F32)
    vmem = pl.BlockSpec(memory_space=pltpu.VMEM)
    smem = pl.BlockSpec(memory_space=pltpu.SMEM)
    flops = 2 * frames * positions * width * share
    return pl.pallas_call(
        joint_kernel,
        out_shape=(grouped, grouped, jax.ShapeDtypeStruct((frames, positions), F32)),
        in_specs=[smem] + [vmem] * (3 + len(preds)),
        out_specs=(vmem,) * 3,
        scratch_shapes=[
            pltpu.VMEM((frames, width), F32),
            pltpu.VMEM((positions, width), F32),
            pltpu.VMEM((positions, 128), F32),
            pltpu.VMEM((positions, width), F32),
            pltpu.VMEM((positions, 128), F32),
            pltpu.VMEM((width, share), F32),
            pltpu.VMEM((share, width), BF16),
            pltpu.VMEM((wide, width), BF16),
            pltpu.VMEM((wide, width), BF16),
            pltpu.VMEM((share // CHUNKS, wide), F32),
            pltpu.VMEM((share // CHUNKS, wide), F32),
            pltpu.VMEM((1, wide), F32),
            pltpu.VMEM((1, wide), F32),
        ],
        compiler_params=pltpu.CompilerParams(vmem_limit_bytes=48 << 20),
        cost_estimate=pl.CostEstimate(flops=flops, bytes_accessed=2 << 20, transcendentals=0),
        name="joint",
    )(place, enc, *preds, own, fetched)


def tree(combine, terms):
    while len(terms) > 1:
        pairs = [combine(a, b) for a, b in zip(terms[::2], terms[1::2])]
        terms = pairs + terms[len(terms) - len(terms) % 2:]
    return terms[0]


def log_sum(terms):
    if len(terms) == 1:
        return terms[0]
    if len(terms) == 2:
        gap = jnp.minimum(*terms) - jnp.maximum(*terms)
        return jnp.maximum(*terms) + jnp.log(1.0 + jnp.exp(gap))
    top = tree(jnp.maximum, terms)
    return top + jnp.log(tree(jnp.add, [jnp.exp(term - top) for term in terms]))


def shift_lanes(values, by):
    by = by % values.shape[1]
    return values if by == 0 else pltpu.roll(values, by, 1)


def compose(first, then):
    terms = []
    for count in range(len(first) + len(then) - 1):
        parts = [
            then[late] + shift_lanes(first[count - late], late)
            for late in range(len(then))
            if 0 <= count - late < len(first)
        ]
        terms.append(log_sum(parts))
    return terms


def shear(values, lead):
    rows = values.shape[0]
    lanes = lax.broadcasted_iota(jnp.int32, values.shape, 1)
    if lead:
        values = pltpu.roll(values, rows - lead, 0)
    for bit in (64, 32, 16, 8, 4, 2, 1):
        values = jnp.where((lanes & bit) != 0, pltpu.roll(values, bit, 0), values)
    return values


def lattice_kernel(
    frame_len_ref, label_len_ref, grid_ref, loss_ref, stay, move, ahead, back, ahead_far, back_far
):
    blocks, _, frames_dev, positions = grid_ref.shape
    frames = blocks * frames_dev
    strips, diagonals, _ = stay.shape
    lanes_all = 128 * strips
    flen = frame_len_ref[0]
    ulen = label_len_ref[0]
    spare = jnp.full((frames, lanes_all - positions), NEG, F32)
    tall = frames + 128
    pad = jnp.full((tall - frames, 128), NEG, F32)

    def whole(which):
        rows = jnp.concatenate([grid_ref[block, which] for block in range(blocks)], axis=0)
        return jnp.concatenate([rows, spare], axis=1)

    blank = whole(0)
    label = shift_lanes(whole(1), 1)
    stay[...] = jnp.full(stay.shape, NEG, F32)
    move[...] = jnp.full(move.shape, NEG, F32)
    for part in range(strips):
        start = 128 * part
        rows = min(tall, diagonals - start)
        for source, out, lead in ((blank, stay, 0), (label, move, 1)):
            strip = jnp.concatenate([source[:, start:start + 128], pad], axis=0)
            out[part, start:start + rows, :] = shear(strip, lead)[:rows]

    depth = SPAN * SPAN
    for group in range(diagonals // depth):
        base = group * depth
        live = [p for p in range(strips) if 128 * p <= base + depth and base < 128 * p + 128 + frames]
        first, count_live = live[0], len(live)
        row = lax.broadcasted_iota(jnp.int32, (SPAN, 128 * count_live), 0)
        lane = lax.broadcasted_iota(jnp.int32, (SPAN, 128 * count_live), 1) + 128 * first
        in_row = lane < positions
        moves_in = in_row & (lane > 0)
        rest = jnp.where(lane == ulen, 0.0, NEG)
        steps = []
        for step in range(SPAN):
            time = base + row * SPAN + step - lane
            at = pl.ds(base + step, SPAN, stride=SPAN)
            held = jnp.concatenate([stay[part, at, :] for part in live], axis=1)
            moved = jnp.concatenate([move[part, at, :] for part in live], axis=1)
            held = jnp.where(in_row & (time < flen), held, rest)
            moved = jnp.where(moves_in & (time + 1 < flen), moved, NEG)
            steps.append([held, moved])
        while len(steps) > 1:
            steps = [compose(steps[i], steps[i + 1]) for i in range(0, len(steps), 2)]
        at = group * SPAN
        for count, values in enumerate(steps[0]):
            moved = shift_lanes(values, -count)
            for part in range(strips):
                if part in live:
                    strip = slice(128 * (part - first), 128 * (part - first) + 128)
                    forth, from_back = values[:, strip], moved[:, strip]
                else:
                    forth = jnp.full((SPAN, 128), NEG, F32)
                    if count == 0:
                        lane = lax.broadcasted_iota(jnp.int32, (SPAN, 128), 1) + 128 * part
                        forth = jnp.where(lane == ulen, 0.0, NEG)
                    from_back = forth
                if count < SPAN:
                    ahead[part, pl.ds(at * SPAN + count, SPAN, stride=SPAN), :] = forth
                    back[part, pl.ds(at * SPAN + SPAN - 1 - count, SPAN, stride=SPAN), :] = from_back
                else:
                    ahead_far[at:at + SPAN, 128 * part:128 * part + 128] = forth
                    back_far[at:at + SPAN, 128 * part:128 * part + 128] = from_back

    spans = diagonals // SPAN
    place = lax.broadcasted_iota(jnp.int32, (1, lanes_all), 1)

    def advance(state, shift, table, far, block, far_shift):
        rows = pl.ds(pl.multiple_of(block * SPAN, SPAN), SPAN)
        weights = jnp.concatenate([table[part, rows, :] for part in range(strips)], axis=1)
        spread = jnp.broadcast_to(state, (SPAN, lanes_all))
        near = weights + pltpu.roll(spread, shift, 1, stride=1, stride_axis=0)
        last = far[pl.ds(block, 1), :] + shift_lanes(state, far_shift)
        top = jnp.maximum(jnp.max(near, axis=0, keepdims=True), last)
        total = jnp.sum(jnp.exp(near - top), axis=0, keepdims=True) + jnp.exp(last - top)
        return top + jnp.log(total)

    def sweep(index, carry):
        alpha, beta = carry
        alpha = advance(alpha, 0, ahead, ahead_far, index, SPAN)
        beta = advance(beta, lanes_all - SPAN + 1, back, back_far, spans - 1 - index, -SPAN)
        return alpha, beta

    alpha = jnp.where(place == 0, 0.0, NEG)
    beta = jnp.where(place == ulen, 0.0, NEG)
    alpha, beta = lax.fori_loop(0, spans // 2, sweep, (alpha, beta))
    both = alpha + beta
    top = jnp.max(both, axis=1, keepdims=True)
    value = top + jnp.log(jnp.sum(jnp.exp(both - top), axis=1, keepdims=True))
    loss_ref[...] = -value / jnp.full((1, 1), flen, jnp.int32).astype(F32)


def lattice_loss(frame_len, label_len, grid):
    blocks, _, frames_dev, positions = grid.shape
    lanes = -(-positions // 128) * 128
    diagonals = -(-(blocks * frames_dev + positions) // (SPAN * SPAN)) * SPAN * SPAN
    assert (diagonals // SPAN) % 2 == 0
    strip = pltpu.VMEM((lanes // 128, diagonals, 128), F32)
    table = pltpu.VMEM((lanes // 128, diagonals, 128), F32)
    far = pltpu.VMEM((diagonals // SPAN, lanes), F32)
    vmem = pl.BlockSpec(memory_space=pltpu.VMEM)
    smem = pl.BlockSpec(memory_space=pltpu.SMEM)
    return pl.pallas_call(
        lattice_kernel,
        out_shape=jax.ShapeDtypeStruct((1, 1), F32),
        in_specs=[smem, smem, vmem],
        out_specs=vmem,
        scratch_shapes=[
            strip,
            strip,
            table,
            table,
            far,
            far,
        ],
        compiler_params=pltpu.CompilerParams(vmem_limit_bytes=40 << 20),
        name="lattice",
    )(frame_len, label_len, grid)


def around(array, axis):
    size = lax.axis_size(axis)
    moved = [
        lax.ppermute(array, axis, [(i, (i + by) % size) for i in range(size)])
        for by in range(1, size)
    ]
    return [array] + moved


def shards(enc_joint, pred_joint, out_weight, labels, frame_len, label_len):
    positions = pred_joint.shape[1]
    mine = lax.axis_index("label")
    rows, columns = out_weight.shape
    piece = columns // LABEL_WAYS
    with jax.named_scope("gather_weight"):
        own = lax.dynamic_slice_in_dim(out_weight, mine * piece, piece, axis=1)
        own = jnp.concatenate([own[:rows // 2], own[rows // 2:]], axis=1)
        blocks = lax.all_gather(own, "tm", axis=0, tiled=False)
        core = lax.axis_index("tm") % 2
        some = blocks.shape[0] // 2
        half = lax.dynamic_slice_in_dim(blocks, core * some, some, axis=0)
        fetched = jnp.stack(around(half, "batch")[1:])
        pairs = [[i, i + 1] for i in range(0, lax.axis_size("tm"), 2)]
        fetched = lax.all_gather(fetched, "tm", axis=0, tiled=False, axis_index_groups=pairs)
    with jax.named_scope("gather_positions"):
        digits = jnp.stack([labels[0] // piece, labels[0] % piece], axis=1).astype(BF16)
        digits = jnp.pad(digits, ((0, 0), (0, 126)))
        packed = jnp.concatenate([pred_joint[0], digits], axis=1)
        preds = around(packed, "label")
    place = jnp.stack([mine, lax.axis_index("batch")]).astype(jnp.int32)
    lse, blank, picked = joint_terms(place, enc_joint[0], preds, blocks, fetched)
    with jax.named_scope("combine_vocab"):
        blank = jnp.where(mine == 0, blank, 0.0)
        parts = jnp.stack([lse.reshape(picked.shape), blank.reshape(picked.shape), picked])
        parts = around(parts, "label")
        top = functools.reduce(jnp.maximum, [part[0] for part in parts])
        norm = top + jnp.log(sum(jnp.exp(part[0] - top) for part in parts))
        log_blank = sum(part[1] for part in parts) - norm
        log_label = sum(part[2] for part in parts) - norm
    out_blank = lax.dynamic_slice_in_dim(log_blank, mine * positions, positions, axis=1)
    out_label = lax.dynamic_slice_in_dim(log_label, mine * positions, positions, axis=1)
    with jax.named_scope("gather_grid"):
        grid = lax.all_gather(jnp.stack([log_blank, log_label]), "tm", axis=0, tiled=False)
    loss = lattice_loss(frame_len, label_len, grid).reshape(1)
    return out_blank[None], out_label[None], loss


def solution(mesh):
    return jax.shard_map(
        shards,
        mesh=mesh,
        in_specs=(
            P("batch", "tm", None),
            P("batch", "label", None),
            P("batch", "tm"),
            P("batch", "label"),
            P("batch"),
            P("batch"),
        ),
        out_specs=(P("batch", "tm", "label"), P("batch", "tm", "label"), P("batch")),
        check_vma=False,
    )
```

```python
import functools

import jax
import jax.numpy as jnp
from jax import lax
from jax.experimental import pallas as pl
from jax.experimental.pallas import tpu as pltpu
from jax.sharding import PartitionSpec as P

NEG = -1e30
F32 = jnp.float32
BF16 = jnp.bfloat16
SPAN = 8
GROUP = 4
CHUNKS = 2
LABEL_WAYS = 4
BATCH_WAYS = 4


def joint_kernel(
    place_ref, enc_ref, own_ref, own_pred_ref, mine_ref, theirs_ref,
    lse_ref, blank_ref, picked_ref,
    enc, pred, chosen, picks, columns_first, weight, hidden_a, hidden_b, logits_a, logits_b, top, total,
):
    mine, batch, core = place_ref[0], place_ref[1], place_ref[2]
    frames, width = enc_ref.shape
    tiles, positions, _ = pred.shape
    share = weight.shape[0]
    chunk = share // CHUNKS
    enc[...] = enc_ref[...].astype(F32)
    blocks, half_rows, _ = own_ref.shape
    some = blocks // 2
    lane = lax.broadcasted_iota(jnp.int32, (half_rows, 128), 1)

    def put_rows(ref, start, count, source, first_pair):
        at = pl.multiple_of(source * 2 * half_rows, 8)
        for pair in range(count // 2):
            left = ref[start + 2 * pair].astype(F32)
            right = ref[start + 2 * pair + 1].astype(F32)
            columns_first[first_pair + pair, pl.ds(at, half_rows), :] = jnp.where(lane < 64, left, right)
            columns_first[first_pair + pair, pl.ds(at + half_rows, half_rows), :] = jnp.where(lane < 64, right, left)

    def put_positions(ref, start, count, source, first):
        at = pl.multiple_of(source * half_rows, 8)
        for index in range(count):
            pred[first + index, pl.ds(at, half_rows), :] = ref[start + index].astype(F32)

    def wrap(value, ways):
        return lax.rem(value + ways, ways)

    put_rows(own_ref, 0, blocks, batch, 0)
    put_positions(own_pred_ref, 0, tiles, mine, 0)
    for ref, side in ((mine_ref, core), (theirs_ref, 1 - core)):
        step = 2 * side - 1
        put_rows(ref, 0, blocks, wrap(batch + step, BATCH_WAYS), 0)
        put_rows(ref, blocks, some, wrap(batch + 2, BATCH_WAYS), side * (some // 2))
        put_positions(ref, blocks + some, tiles, wrap(mine + step, LABEL_WAYS), 0)
        put_positions(ref, blocks + some + tiles, tiles // 2, wrap(mine + 2, LABEL_WAYS), side * (tiles // 2))
    depth = lax.broadcasted_iota(jnp.int32, (128, width), 1)
    upper = lax.rem(depth, 2 * half_rows) < half_rows
    for tile in range(share // 128):
        turned = columns_first[tile].T
        swapped = jnp.concatenate([turned[64:], turned[:64]], axis=0)
        weight[128 * tile:128 * tile + 128, :] = jnp.where(upper, turned, swapped).astype(BF16)

    digits = pred[tiles - 1]
    high = digits[:, 0:1].astype(jnp.int32)
    low = digits[:, 1:2].astype(jnp.int32)
    spot = jnp.where((high & 3) == mine, (high >> 2) * 64 + low, -1)
    columns = lax.broadcasted_iota(jnp.int32, (positions, share), 1)
    one_hot = (columns == spot).astype(F32).astype(BF16)
    chosen[...] = jnp.dot(one_hot, weight[...], preferred_element_type=F32)
    picks[...] = jnp.zeros_like(picks)
    lanes = lax.broadcasted_iota(jnp.int32, picks.shape, 1)

    def make_hidden(frame, part, out):
        rows = slice(part * positions, (part + 1) * positions)
        picked = jnp.zeros((positions, 128), F32)
        frame_row = enc[pl.ds(frame, 1), :]
        for tile in range(tiles - 1):
            strip = slice(128 * tile, 128 * tile + 128)
            rounded = jnp.tanh(pred[tile] + frame_row[:, strip]).astype(BF16)
            out[rows, strip] = rounded
            picked = picked + rounded.astype(F32) * chosen[:, strip]
        picked = jnp.sum(picked, axis=1, keepdims=True)
        picks[...] = jnp.where(lanes == frame, picked, picks[...])

    def multiply(part, hidden, out):
        out[...] = lax.dot_general(
            weight[part * chunk:(part + 1) * chunk, :], hidden[...],
            (((1,), (1,)), ((), ())), preferred_element_type=F32,
        )

    def gather_terms(part, group, logits):
        values = logits[...]
        high = jnp.max(values, axis=0, keepdims=True)
        if part == 0:
            blank_ref[pl.ds(group, 1), :] = logits[0:1, :]
            total[...] = jnp.sum(jnp.exp(values - high), axis=0, keepdims=True)
            top[...] = high
        else:
            high = jnp.maximum(high, top[...])
            total[...] = total[...] * jnp.exp(top[...] - high) + jnp.sum(
                jnp.exp(values - high), axis=0, keepdims=True
            )
            top[...] = high
        if part == CHUNKS - 1:
            lse_ref[pl.ds(group, 1), :] = top[...] + jnp.log(total[...])

    groups = frames // GROUP
    for part in range(GROUP):
        make_hidden(part, part, hidden_a)
    logits_b[...] = jnp.zeros_like(logits_b)
    top[...] = jnp.zeros_like(top)
    total[...] = jnp.ones_like(total)
    each = GROUP // CHUNKS

    def half(group, now, later):
        for part in range(CHUNKS):
            fresh, old = (logits_a, logits_b) if part % 2 == 0 else (logits_b, logits_a)
            multiply(part, now, fresh)
            for which in range(part * each, (part + 1) * each):
                make_hidden(jnp.minimum(group + 1, groups - 1) * GROUP + which, which, later)
            if part == 0:
                gather_terms(CHUNKS - 1, jnp.maximum(group - 1, 0), old)
            else:
                gather_terms(part - 1, group, old)

    def step(pair, carry):
        half(2 * pair, hidden_a, hidden_b)
        half(2 * pair + 1, hidden_b, hidden_a)
        return carry

    lax.fori_loop(0, groups // 2, step, 0)
    gather_terms(CHUNKS - 1, groups - 1, logits_b)
    picked_ref[...] = picks[...].T[:frames, :]


def joint_terms(place, enc, own, own_pred, mine, theirs):
    frames, width = enc.shape
    tiles = own_pred.shape[0]
    positions = LABEL_WAYS * own_pred.shape[1]
    share = 64 * own.shape[0]
    wide = GROUP * positions
    grouped = jax.ShapeDtypeStruct((frames // GROUP, wide), F32)
    vmem = pl.BlockSpec(memory_space=pltpu.VMEM)
    smem = pl.BlockSpec(memory_space=pltpu.SMEM)
    flops = 2 * frames * positions * width * share
    return pl.pallas_call(
        joint_kernel,
        out_shape=(grouped, grouped, jax.ShapeDtypeStruct((frames, positions), F32)),
        in_specs=[smem] + [vmem] * 5,
        out_specs=(vmem,) * 3,
        scratch_shapes=[
            pltpu.VMEM((frames, width), F32),
            pltpu.VMEM((tiles, positions, 128), F32),
            pltpu.VMEM((positions, width), F32),
            pltpu.VMEM((positions, 128), F32),
            pltpu.VMEM((share // 128, width, 128), F32),
            pltpu.VMEM((share, width), BF16),
            pltpu.VMEM((wide, width), BF16),
            pltpu.VMEM((wide, width), BF16),
            pltpu.VMEM((share // CHUNKS, wide), F32),
            pltpu.VMEM((share // CHUNKS, wide), F32),
            pltpu.VMEM((1, wide), F32),
            pltpu.VMEM((1, wide), F32),
        ],
        compiler_params=pltpu.CompilerParams(vmem_limit_bytes=48 << 20),
        cost_estimate=pl.CostEstimate(flops=flops, bytes_accessed=2 << 20, transcendentals=0),
        name="joint",
    )(place, enc, own, own_pred, mine, theirs)


def tree(combine, terms):
    while len(terms) > 1:
        pairs = [combine(a, b) for a, b in zip(terms[::2], terms[1::2])]
        terms = pairs + terms[len(terms) - len(terms) % 2:]
    return terms[0]


def log_sum(terms):
    if len(terms) == 1:
        return terms[0]
    if len(terms) == 2:
        gap = jnp.minimum(*terms) - jnp.maximum(*terms)
        return jnp.maximum(*terms) + jnp.log(1.0 + jnp.exp(gap))
    top = tree(jnp.maximum, terms)
    return top + jnp.log(tree(jnp.add, [jnp.exp(term - top) for term in terms]))


def shift_lanes(values, by):
    by = by % values.shape[1]
    return values if by == 0 else pltpu.roll(values, by, 1)


def compose(first, then):
    terms = []
    for count in range(len(first) + len(then) - 1):
        parts = [
            then[late] + shift_lanes(first[count - late], late)
            for late in range(len(then))
            if 0 <= count - late < len(first)
        ]
        terms.append(log_sum(parts))
    return terms


def shear(values, lead):
    rows = values.shape[0]
    lanes = lax.broadcasted_iota(jnp.int32, values.shape, 1)
    if lead:
        values = pltpu.roll(values, rows - lead, 0)
    for bit in (64, 32, 16, 8, 4, 2, 1):
        values = jnp.where((lanes & bit) != 0, pltpu.roll(values, bit, 0), values)
    return values


def lattice_kernel(
    frame_len_ref, label_len_ref, grid_ref, loss_ref, stay, move, ahead, back, ahead_far, back_far
):
    blocks, _, frames_dev, positions = grid_ref.shape
    frames = blocks * frames_dev
    strips, diagonals, _ = stay.shape
    lanes_all = 128 * strips
    flen = frame_len_ref[0]
    ulen = label_len_ref[0]
    spare = jnp.full((frames, lanes_all - positions), NEG, F32)
    tall = frames + 128
    pad = jnp.full((tall - frames, 128), NEG, F32)

    def whole(which):
        rows = jnp.concatenate([grid_ref[block, which] for block in range(blocks)], axis=0)
        return jnp.concatenate([rows, spare], axis=1)

    blank = whole(0)
    label = shift_lanes(whole(1), 1)
    stay[...] = jnp.full(stay.shape, NEG, F32)
    move[...] = jnp.full(move.shape, NEG, F32)
    for part in range(strips):
        start = 128 * part
        rows = min(tall, diagonals - start)
        for source, out, lead in ((blank, stay, 0), (label, move, 1)):
            strip = jnp.concatenate([source[:, start:start + 128], pad], axis=0)
            out[part, start:start + rows, :] = shear(strip, lead)[:rows]

    depth = SPAN * SPAN
    for group in range(diagonals // depth):
        base = group * depth
        live = [p for p in range(strips) if 128 * p <= base + depth and base < 128 * p + 128 + frames]
        first, count_live = live[0], len(live)
        row = lax.broadcasted_iota(jnp.int32, (SPAN, 128 * count_live), 0)
        lane = lax.broadcasted_iota(jnp.int32, (SPAN, 128 * count_live), 1) + 128 * first
        in_row = lane < positions
        moves_in = in_row & (lane > 0)
        rest = jnp.where(lane == ulen, 0.0, NEG)
        steps = []
        for step in range(SPAN):
            time = base + row * SPAN + step - lane
            at = pl.ds(base + step, SPAN, stride=SPAN)
            held = jnp.concatenate([stay[part, at, :] for part in live], axis=1)
            moved = jnp.concatenate([move[part, at, :] for part in live], axis=1)
            held = jnp.where(in_row & (time < flen), held, rest)
            moved = jnp.where(moves_in & (time + 1 < flen), moved, NEG)
            steps.append([held, moved])
        while len(steps) > 1:
            steps = [compose(steps[i], steps[i + 1]) for i in range(0, len(steps), 2)]
        at = group * SPAN
        for count, values in enumerate(steps[0]):
            moved = shift_lanes(values, -count)
            for part in range(strips):
                if part in live:
                    strip = slice(128 * (part - first), 128 * (part - first) + 128)
                    forth, from_back = values[:, strip], moved[:, strip]
                else:
                    forth = jnp.full((SPAN, 128), NEG, F32)
                    if count == 0:
                        lane = lax.broadcasted_iota(jnp.int32, (SPAN, 128), 1) + 128 * part
                        forth = jnp.where(lane == ulen, 0.0, NEG)
                    from_back = forth
                if count < SPAN:
                    ahead[part, pl.ds(at * SPAN + count, SPAN, stride=SPAN), :] = forth
                    back[part, pl.ds(at * SPAN + SPAN - 1 - count, SPAN, stride=SPAN), :] = from_back
                else:
                    ahead_far[at:at + SPAN, 128 * part:128 * part + 128] = forth
                    back_far[at:at + SPAN, 128 * part:128 * part + 128] = from_back

    spans = diagonals // SPAN
    place = lax.broadcasted_iota(jnp.int32, (1, lanes_all), 1)

    def advance(state, shift, table, far, block, far_shift):
        rows = pl.ds(pl.multiple_of(block * SPAN, SPAN), SPAN)
        weights = jnp.concatenate([table[part, rows, :] for part in range(strips)], axis=1)
        spread = jnp.broadcast_to(state, (SPAN, lanes_all))
        near = weights + pltpu.roll(spread, shift, 1, stride=1, stride_axis=0)
        last = far[pl.ds(block, 1), :] + shift_lanes(state, far_shift)
        top = jnp.maximum(jnp.max(near, axis=0, keepdims=True), last)
        total = jnp.sum(jnp.exp(near - top), axis=0, keepdims=True) + jnp.exp(last - top)
        return top + jnp.log(total)

    def sweep(index, carry):
        alpha, beta = carry
        alpha = advance(alpha, 0, ahead, ahead_far, index, SPAN)
        beta = advance(beta, lanes_all - SPAN + 1, back, back_far, spans - 1 - index, -SPAN)
        return alpha, beta

    alpha = jnp.where(place == 0, 0.0, NEG)
    beta = jnp.where(place == ulen, 0.0, NEG)
    alpha, beta = lax.fori_loop(0, spans // 2, sweep, (alpha, beta))
    both = alpha + beta
    top = jnp.max(both, axis=1, keepdims=True)
    value = top + jnp.log(jnp.sum(jnp.exp(both - top), axis=1, keepdims=True))
    loss_ref[...] = -value / jnp.full((1, 1), flen, jnp.int32).astype(F32)


def lattice_loss(frame_len, label_len, grid):
    blocks, _, frames_dev, positions = grid.shape
    lanes = -(-positions // 128) * 128
    diagonals = -(-(blocks * frames_dev + positions) // (SPAN * SPAN)) * SPAN * SPAN
    assert (diagonals // SPAN) % 2 == 0
    strip = pltpu.VMEM((lanes // 128, diagonals, 128), F32)
    table = pltpu.VMEM((lanes // 128, diagonals, 128), F32)
    far = pltpu.VMEM((diagonals // SPAN, lanes), F32)
    vmem = pl.BlockSpec(memory_space=pltpu.VMEM)
    smem = pl.BlockSpec(memory_space=pltpu.SMEM)
    return pl.pallas_call(
        lattice_kernel,
        out_shape=jax.ShapeDtypeStruct((1, 1), F32),
        in_specs=[smem, smem, vmem],
        out_specs=vmem,
        scratch_shapes=[
            strip,
            strip,
            table,
            table,
            far,
            far,
        ],
        compiler_params=pltpu.CompilerParams(vmem_limit_bytes=40 << 20),
        name="lattice",
    )(frame_len, label_len, grid)


def both_ways(array, axis):
    ways, cores = lax.axis_size(axis), lax.axis_size("tm")
    axes = ("batch", "tm") if axis == "batch" else ("tm", "label")

    def device(way, at):
        return way % ways * cores + at if axis == "batch" else at * ways + way % ways

    near, opposite = [], []
    for way in range(ways):
        for at in range(cores):
            near.append((device(way, at), device(way + (1 if at % 2 == 0 else -1), at)))
            opposite.append((device(way, at), device(way + 2, at)))
    some = array.shape[0] // 2
    half = lax.dynamic_slice_in_dim(array, lax.axis_index("tm") % 2 * some, some, axis=0)
    return lax.ppermute(array, axes, near), lax.ppermute(half, axes, opposite)


def shards(enc_joint, pred_joint, out_weight, labels, frame_len, label_len):
    positions, width = pred_joint.shape[1:]
    mine = lax.axis_index("label")
    here = lax.axis_index("tm")
    rows, columns = out_weight.shape
    piece = columns // LABEL_WAYS
    with jax.named_scope("gather_weight"):
        upper, lower = [
            lax.dynamic_slice(out_weight, (side * (rows // 2), mine * piece), (rows // 2, piece))
            for side in (here % 2, 1 - here % 2)
        ]
        own = lax.all_gather(jnp.concatenate([upper, lower], axis=1), "tm", axis=0, tiled=False)
    with jax.named_scope("gather_positions"):
        digits = jnp.stack([labels[0] // piece, labels[0] % piece], axis=1).astype(BF16)
        digits = jnp.pad(digits, ((0, 0), (0, 126)))
        own_pred = jnp.stack(jnp.split(pred_joint[0], width // 128, axis=1) + [digits])
    with jax.named_scope("fetch"):
        from_others = jnp.concatenate([*both_ways(own, "batch"), *both_ways(own_pred, "label")], axis=0)
        swap = [(i, i ^ 1) for i in range(lax.axis_size("tm"))]
        theirs = lax.ppermute(from_others, "tm", swap)
    place = jnp.stack([mine, lax.axis_index("batch"), here % 2]).astype(jnp.int32)
    lse, blank, picked = joint_terms(place, enc_joint[0], own, own_pred, from_others, theirs)
    with jax.named_scope("combine_vocab"):
        blank = jnp.where(mine == 0, blank, 0.0)
        norm, log_blank, log_label = lse.reshape(picked.shape), blank.reshape(picked.shape), picked
        for flip in (1, 3):
            pairs = [(i, i ^ flip) for i in range(LABEL_WAYS)]
            other = lax.ppermute(jnp.stack([norm, log_blank, log_label]), "label", pairs)
            norm = jnp.logaddexp(norm, other[0])
            log_blank, log_label = log_blank + other[1], log_label + other[2]
        log_blank, log_label = log_blank - norm, log_label - norm
    out_blank = lax.dynamic_slice_in_dim(log_blank, mine * positions, positions, axis=1)
    out_label = lax.dynamic_slice_in_dim(log_label, mine * positions, positions, axis=1)
    with jax.named_scope("gather_grid"):
        grid = lax.all_gather(jnp.stack([log_blank, log_label]), "tm", axis=0, tiled=False)
    loss = lattice_loss(frame_len, label_len, grid).reshape(1)
    return out_blank[None], out_label[None], loss


def solution(mesh):
    return jax.shard_map(
        shards,
        mesh=mesh,
        in_specs=(
            P("batch", "tm", None),
            P("batch", "label", None),
            P("batch", "tm"),
            P("batch", "label"),
            P("batch"),
            P("batch"),
        ),
        out_specs=(P("batch", "tm", "label"), P("batch", "tm", "label"), P("batch")),
        check_vma=False,
    )
```

```python
import functools

import jax
import jax.numpy as jnp
from jax import lax
from jax.experimental import pallas as pl
from jax.experimental.pallas import tpu as pltpu
from jax.sharding import PartitionSpec as P

NEG = -1e30
F32 = jnp.float32
BF16 = jnp.bfloat16
SPAN = 8
GROUP = 4
CHUNKS = 2
LABEL_WAYS = 4
BATCH_WAYS = 4


def pack_kernel(place_ref, weight_ref, pred_ref, labels_ref, block_ref, packed_ref):
    mine, odd_block = place_ref[0], lax.rem(place_ref[3], 2) == 1
    tiles, positions, _ = packed_ref.shape
    rows = block_ref.shape[0]
    lane = lax.broadcasted_iota(jnp.int32, (rows, 128), 1)
    values = jnp.where(mine < 2, weight_ref[:, :128].astype(F32), weight_ref[:, 128:].astype(F32))
    left = jnp.where(odd_block, values[rows:], values[:rows])
    right = jnp.where(odd_block, values[:rows], values[rows:])
    second = lax.rem(mine, 2) == 1
    left = jnp.where(second, pltpu.roll(left, 64, 1), left)
    right = jnp.where(second, right, pltpu.roll(right, 64, 1))
    block_ref[...] = jnp.where(lane < 64, left, right).astype(BF16)
    for tile in range(tiles - 1):
        packed_ref[tile] = pred_ref[:, 128 * tile:128 * tile + 128]
    labels = jnp.broadcast_to(labels_ref[...], (positions, positions))
    across = lax.broadcasted_iota(jnp.int32, (positions, positions), 0)
    along = lax.broadcasted_iota(jnp.int32, (positions, positions), 1)
    own = jnp.where(across == along, labels, 0)
    high = jnp.sum((own >> 6).astype(F32), axis=1, keepdims=True)
    low = jnp.sum((own & 63).astype(F32), axis=1, keepdims=True)
    lane = lax.broadcasted_iota(jnp.int32, (positions, 128), 1)
    packed_ref[tiles - 1] = jnp.where(lane == 0, high, jnp.where(lane == 1, low, 0.0)).astype(BF16)


def pack(place, weight, pred, labels):
    positions, width = pred.shape
    vmem = pl.BlockSpec(memory_space=pltpu.VMEM)
    return pl.pallas_call(
        pack_kernel,
        out_shape=(
            jax.ShapeDtypeStruct((weight.shape[0] // 2, 128), BF16),
            jax.ShapeDtypeStruct((width // 128 + 1, positions, 128), BF16),
        ),
        in_specs=[pl.BlockSpec(memory_space=pltpu.SMEM)] + [vmem] * 3,
        out_specs=(vmem, vmem),
        name="pack",
    )(place, weight, pred, labels)


def joint_kernel(
    place_ref, enc_ref, own_ref, own_pred_ref, mine_ref, theirs_ref,
    lse_ref, blank_ref, picked_ref,
    enc, pred, chosen, picks, columns_first, weight, hidden_a, hidden_b, logits_a, logits_b, top, total, top_a, top_b,
):
    mine, batch, core = place_ref[0], place_ref[1], place_ref[2]
    frames, width = enc_ref.shape
    tiles, positions, _ = pred.shape
    share = weight.shape[0]
    chunk = share // CHUNKS
    enc[...] = enc_ref[...].astype(F32)
    blocks, half_rows, _ = own_ref.shape
    some = blocks // 2
    lane = lax.broadcasted_iota(jnp.int32, (half_rows, 128), 1)

    def put_rows(ref, start, count, source, first_pair):
        at = pl.multiple_of(source * 2 * half_rows, 8)
        for pair in range(count // 2):
            left = ref[start + 2 * pair].astype(F32)
            right = ref[start + 2 * pair + 1].astype(F32)
            columns_first[first_pair + pair, pl.ds(at, half_rows), :] = jnp.where(lane < 64, left, right)
            columns_first[first_pair + pair, pl.ds(at + half_rows, half_rows), :] = jnp.where(lane < 64, right, left)

    def put_positions(ref, start, count, source, first):
        at = pl.multiple_of(source * half_rows, 8)
        for index in range(count):
            pred[first + index, pl.ds(at, half_rows), :] = ref[start + index].astype(F32)

    def wrap(value, ways):
        return lax.rem(value + ways, ways)

    put_rows(own_ref, 0, blocks, batch, 0)
    put_positions(own_pred_ref, 0, tiles, mine, 0)
    for ref, side in ((mine_ref, core), (theirs_ref, 1 - core)):
        step = 2 * side - 1
        put_rows(ref, 0, blocks, wrap(batch + step, BATCH_WAYS), 0)
        put_rows(ref, blocks, some, wrap(batch + 2, BATCH_WAYS), side * (some // 2))
        put_positions(ref, blocks + some, tiles, wrap(mine + step, LABEL_WAYS), 0)
        put_positions(ref, blocks + some + tiles, tiles // 2, wrap(mine + 2, LABEL_WAYS), side * (tiles // 2))
    depth = lax.broadcasted_iota(jnp.int32, (128, width), 1)
    upper = lax.rem(depth, 2 * half_rows) < half_rows
    for tile in range(share // 128):
        turned = columns_first[tile].T
        swapped = jnp.concatenate([turned[64:], turned[:64]], axis=0)
        weight[128 * tile:128 * tile + 128, :] = jnp.where(upper, turned, swapped).astype(BF16)

    digits = pred[tiles - 1]
    high = digits[:, 0:1].astype(jnp.int32)
    low = digits[:, 1:2].astype(jnp.int32)
    spot = jnp.where((high & 3) == mine, (high >> 2) * 64 + low, -1)
    columns = lax.broadcasted_iota(jnp.int32, (positions, share), 1)
    one_hot = (columns == spot).astype(F32).astype(BF16)
    chosen[...] = jnp.dot(one_hot, weight[...], preferred_element_type=F32)
    picks[...] = jnp.zeros_like(picks)
    lanes = lax.broadcasted_iota(jnp.int32, picks.shape, 1)

    def make_hidden(frame, part, out):
        rows = slice(part * positions, (part + 1) * positions)
        picked = jnp.zeros((positions, 128), F32)
        frame_row = enc[pl.ds(frame, 1), :]
        for tile in range(tiles - 1):
            strip = slice(128 * tile, 128 * tile + 128)
            rounded = jnp.tanh(pred[tile] + frame_row[:, strip]).astype(BF16)
            out[rows, strip] = rounded
            picked = picked + rounded.astype(F32) * chosen[:, strip]
        picked = jnp.sum(picked, axis=1, keepdims=True)
        picks[...] = jnp.where(lanes == frame, picked, picks[...])

    def multiply(part, hidden, out, chunk_top):
        acc = lax.dot_general(
            weight[part * chunk:(part + 1) * chunk, :], hidden[...],
            (((1,), (1,)), ((), ())), preferred_element_type=F32,
        )
        out[...] = acc
        chunk_top[...] = jnp.max(acc, axis=0, keepdims=True)

    def gather_terms(part, group, logits, chunk_top):
        values = logits[...]
        high = chunk_top[...]
        if part == 0:
            blank_ref[pl.ds(group, 1), :] = logits[0:1, :]
            total[...] = jnp.sum(jnp.exp(values - high), axis=0, keepdims=True)
            top[...] = high
        else:
            high = jnp.maximum(high, top[...])
            total[...] = total[...] * jnp.exp(top[...] - high) + jnp.sum(
                jnp.exp(values - high), axis=0, keepdims=True
            )
            top[...] = high
        if part == CHUNKS - 1:
            lse_ref[pl.ds(group, 1), :] = top[...] + jnp.log(total[...])

    groups = frames // GROUP
    for part in range(GROUP):
        make_hidden(part, part, hidden_a)
    logits_b[...] = jnp.zeros_like(logits_b)
    top[...] = jnp.zeros_like(top)
    top_b[...] = jnp.zeros_like(top)
    total[...] = jnp.ones_like(total)
    each = GROUP // CHUNKS

    def half(group, now, later):
        for part in range(CHUNKS):
            fresh, old = (logits_a, logits_b) if part % 2 == 0 else (logits_b, logits_a)
            fresh_top, old_top = (top_a, top_b) if part % 2 == 0 else (top_b, top_a)
            multiply(part, now, fresh, fresh_top)
            for which in range(part * each, (part + 1) * each):
                make_hidden(jnp.minimum(group + 1, groups - 1) * GROUP + which, which, later)
            if part == 0:
                gather_terms(CHUNKS - 1, jnp.maximum(group - 1, 0), old, old_top)
            else:
                gather_terms(part - 1, group, old, old_top)

    def step(pair, carry):
        half(2 * pair, hidden_a, hidden_b)
        half(2 * pair + 1, hidden_b, hidden_a)
        return carry

    lax.fori_loop(0, groups // 2, step, 0)
    gather_terms(CHUNKS - 1, groups - 1, logits_b, top_b)
    picked_ref[...] = picks[...].T[:frames, :]


def joint_terms(place, enc, own, own_pred, mine, theirs):
    frames, width = enc.shape
    tiles = own_pred.shape[0]
    positions = LABEL_WAYS * own_pred.shape[1]
    share = 64 * own.shape[0]
    wide = GROUP * positions
    grouped = jax.ShapeDtypeStruct((frames // GROUP, wide), F32)
    vmem = pl.BlockSpec(memory_space=pltpu.VMEM)
    smem = pl.BlockSpec(memory_space=pltpu.SMEM)
    flops = 2 * frames * positions * width * share
    return pl.pallas_call(
        joint_kernel,
        out_shape=(grouped, grouped, jax.ShapeDtypeStruct((frames, positions), F32)),
        in_specs=[smem] + [vmem] * 5,
        out_specs=(vmem,) * 3,
        scratch_shapes=[
            pltpu.VMEM((frames, width), F32),
            pltpu.VMEM((tiles, positions, 128), F32),
            pltpu.VMEM((positions, width), F32),
            pltpu.VMEM((positions, 128), F32),
            pltpu.VMEM((share // 128, width, 128), F32),
            pltpu.VMEM((share, width), BF16),
            pltpu.VMEM((wide, width), BF16),
            pltpu.VMEM((wide, width), BF16),
            pltpu.VMEM((share // CHUNKS, wide), F32),
            pltpu.VMEM((share // CHUNKS, wide), F32),
            pltpu.VMEM((1, wide), F32),
            pltpu.VMEM((1, wide), F32),
            pltpu.VMEM((1, wide), F32),
            pltpu.VMEM((1, wide), F32),
        ],
        compiler_params=pltpu.CompilerParams(vmem_limit_bytes=48 << 20),
        cost_estimate=pl.CostEstimate(flops=flops, bytes_accessed=2 << 20, transcendentals=0),
        name="joint",
    )(place, enc, own, own_pred, mine, theirs)


def tree(combine, terms):
    while len(terms) > 1:
        pairs = [combine(a, b) for a, b in zip(terms[::2], terms[1::2])]
        terms = pairs + terms[len(terms) - len(terms) % 2:]
    return terms[0]


def log_sum(terms):
    if len(terms) == 1:
        return terms[0]
    if len(terms) == 2:
        gap = jnp.minimum(*terms) - jnp.maximum(*terms)
        return jnp.maximum(*terms) + jnp.log(1.0 + jnp.exp(gap))
    top = tree(jnp.maximum, terms)
    return top + jnp.log(tree(jnp.add, [jnp.exp(term - top) for term in terms]))


def shift_lanes(values, by):
    by = by % values.shape[1]
    return values if by == 0 else pltpu.roll(values, by, 1)


def compose(first, then):
    terms = []
    for count in range(len(first) + len(then) - 1):
        parts = [
            then[late] + shift_lanes(first[count - late], late)
            for late in range(len(then))
            if 0 <= count - late < len(first)
        ]
        terms.append(log_sum(parts))
    return terms


def shear(values, lead):
    rows = values.shape[0]
    lanes = lax.broadcasted_iota(jnp.int32, values.shape, 1)
    if lead:
        values = pltpu.roll(values, rows - lead, 0)
    for bit in (64, 32, 16, 8, 4, 2, 1):
        values = jnp.where((lanes & bit) != 0, pltpu.roll(values, bit, 0), values)
    return values


def lattice_kernel(
    frame_len_ref, label_len_ref, grid_ref, loss_ref, stay, move, ahead, back, ahead_far, back_far
):
    blocks, _, frames_dev, positions = grid_ref.shape
    frames = blocks * frames_dev
    strips, diagonals, _ = stay.shape
    lanes_all = 128 * strips
    flen = frame_len_ref[0]
    ulen = label_len_ref[0]
    spare = jnp.full((frames, lanes_all - positions), NEG, F32)
    tall = frames + 128
    pad = jnp.full((tall - frames, 128), NEG, F32)

    def whole(which):
        rows = jnp.concatenate([grid_ref[block, which] for block in range(blocks)], axis=0)
        return jnp.concatenate([rows, spare], axis=1)

    blank = whole(0)
    label = shift_lanes(whole(1), 1)
    stay[...] = jnp.full(stay.shape, NEG, F32)
    move[...] = jnp.full(move.shape, NEG, F32)
    for part in range(strips):
        start = 128 * part
        rows = min(tall, diagonals - start)
        for source, out, lead in ((blank, stay, 0), (label, move, 1)):
            strip = jnp.concatenate([source[:, start:start + 128], pad], axis=0)
            out[part, start:start + rows, :] = shear(strip, lead)[:rows]

    depth = SPAN * SPAN
    for group in range(diagonals // depth):
        base = group * depth
        live = [p for p in range(strips) if 128 * p <= base + depth and base < 128 * p + 128 + frames]
        first, count_live = live[0], len(live)
        row = lax.broadcasted_iota(jnp.int32, (SPAN, 128 * count_live), 0)
        lane = lax.broadcasted_iota(jnp.int32, (SPAN, 128 * count_live), 1) + 128 * first
        in_row = lane < positions
        moves_in = in_row & (lane > 0)
        rest = jnp.where(lane == ulen, 0.0, NEG)
        steps = []
        for step in range(SPAN):
            time = base + row * SPAN + step - lane
            at = pl.ds(base + step, SPAN, stride=SPAN)
            held = jnp.concatenate([stay[part, at, :] for part in live], axis=1)
            moved = jnp.concatenate([move[part, at, :] for part in live], axis=1)
            held = jnp.where(in_row & (time < flen), held, rest)
            moved = jnp.where(moves_in & (time + 1 < flen), moved, NEG)
            steps.append([held, moved])
        while len(steps) > 1:
            steps = [compose(steps[i], steps[i + 1]) for i in range(0, len(steps), 2)]
        at = group * SPAN
        for count, values in enumerate(steps[0]):
            moved = shift_lanes(values, -count)
            for part in range(strips):
                if part in live:
                    strip = slice(128 * (part - first), 128 * (part - first) + 128)
                    forth, from_back = values[:, strip], moved[:, strip]
                else:
                    forth = jnp.full((SPAN, 128), NEG, F32)
                    if count == 0:
                        lane = lax.broadcasted_iota(jnp.int32, (SPAN, 128), 1) + 128 * part
                        forth = jnp.where(lane == ulen, 0.0, NEG)
                    from_back = forth
                if count < SPAN:
                    ahead[part, pl.ds(at * SPAN + count, SPAN, stride=SPAN), :] = forth
                    back[part, pl.ds(at * SPAN + SPAN - 1 - count, SPAN, stride=SPAN), :] = from_back
                else:
                    ahead_far[at:at + SPAN, 128 * part:128 * part + 128] = forth
                    back_far[at:at + SPAN, 128 * part:128 * part + 128] = from_back

    spans = diagonals // SPAN
    place = lax.broadcasted_iota(jnp.int32, (1, lanes_all), 1)

    def advance(state, shift, table, far, block, far_shift):
        rows = pl.ds(pl.multiple_of(block * SPAN, SPAN), SPAN)
        weights = jnp.concatenate([table[part, rows, :] for part in range(strips)], axis=1)
        spread = jnp.broadcast_to(state, (SPAN, lanes_all))
        near = weights + pltpu.roll(spread, shift, 1, stride=1, stride_axis=0)
        last = far[pl.ds(block, 1), :] + shift_lanes(state, far_shift)
        top = jnp.maximum(jnp.max(near, axis=0, keepdims=True), last)
        total = jnp.sum(jnp.exp(near - top), axis=0, keepdims=True) + jnp.exp(last - top)
        return top + jnp.log(total)

    def sweep(index, carry):
        alpha, beta = carry
        alpha = advance(alpha, 0, ahead, ahead_far, index, SPAN)
        beta = advance(beta, lanes_all - SPAN + 1, back, back_far, spans - 1 - index, -SPAN)
        return alpha, beta

    alpha = jnp.where(place == 0, 0.0, NEG)
    beta = jnp.where(place == ulen, 0.0, NEG)
    alpha, beta = lax.fori_loop(0, spans // 2, sweep, (alpha, beta))
    both = alpha + beta
    top = jnp.max(both, axis=1, keepdims=True)
    value = top + jnp.log(jnp.sum(jnp.exp(both - top), axis=1, keepdims=True))
    loss_ref[...] = -value / jnp.full((1, 1), flen, jnp.int32).astype(F32)


def lattice_loss(frame_len, label_len, grid):
    blocks, _, frames_dev, positions = grid.shape
    lanes = -(-positions // 128) * 128
    diagonals = -(-(blocks * frames_dev + positions) // (SPAN * SPAN)) * SPAN * SPAN
    assert (diagonals // SPAN) % 2 == 0
    strip = pltpu.VMEM((lanes // 128, diagonals, 128), F32)
    table = pltpu.VMEM((lanes // 128, diagonals, 128), F32)
    far = pltpu.VMEM((diagonals // SPAN, lanes), F32)
    vmem = pl.BlockSpec(memory_space=pltpu.VMEM)
    smem = pl.BlockSpec(memory_space=pltpu.SMEM)
    return pl.pallas_call(
        lattice_kernel,
        out_shape=jax.ShapeDtypeStruct((1, 1), F32),
        in_specs=[smem, smem, vmem],
        out_specs=vmem,
        scratch_shapes=[
            strip,
            strip,
            table,
            table,
            far,
            far,
        ],
        compiler_params=pltpu.CompilerParams(vmem_limit_bytes=40 << 20),
        name="lattice",
    )(frame_len, label_len, grid)


def around(array, axis):
    size = lax.axis_size(axis)
    moved = [
        lax.ppermute(array, axis, [(i, (i + by) % size) for i in range(size)])
        for by in range(1, size)
    ]
    return [array] + moved


def both_ways(array, axis):
    ways, cores = lax.axis_size(axis), lax.axis_size("tm")
    axes = ("batch", "tm") if axis == "batch" else ("tm", "label")

    def device(way, at):
        return way % ways * cores + at if axis == "batch" else at * ways + way % ways

    near, opposite = [], []
    for way in range(ways):
        for at in range(cores):
            near.append((device(way, at), device(way + (1 if at % 2 == 0 else -1), at)))
            opposite.append((device(way, at), device(way + 2, at)))
    some = array.shape[0] // 2
    half = lax.dynamic_slice_in_dim(array, lax.axis_index("tm") % 2 * some, some, axis=0)
    return lax.ppermute(array, axes, near), lax.ppermute(half, axes, opposite)


def shards(enc_joint, pred_joint, out_weight, labels, frame_len, label_len):
    positions = pred_joint.shape[1]
    mine = lax.axis_index("label")
    here = lax.axis_index("tm")
    place = jnp.stack([mine, lax.axis_index("batch"), here % 2, here]).astype(jnp.int32)
    own, own_pred = pack(place, out_weight, pred_joint[0], labels)
    with jax.named_scope("gather_weight"):
        own = lax.all_gather(own, "tm", axis=0, tiled=False)
    with jax.named_scope("fetch"):
        from_others = jnp.concatenate([*both_ways(own, "batch"), *both_ways(own_pred, "label")], axis=0)
        swap = [(i, i ^ 1) for i in range(lax.axis_size("tm"))]
        theirs = lax.ppermute(from_others, "tm", swap)
    lse, blank, picked = joint_terms(place, enc_joint[0], own, own_pred, from_others, theirs)
    with jax.named_scope("combine_vocab"):
        blank = jnp.where(mine == 0, blank, 0.0)
        parts = jnp.stack([lse.reshape(picked.shape), blank.reshape(picked.shape), picked])
        parts = around(parts, "label")
        top = functools.reduce(jnp.maximum, [part[0] for part in parts])
        norm = top + jnp.log(sum(jnp.exp(part[0] - top) for part in parts))
        log_blank = sum(part[1] for part in parts) - norm
        log_label = sum(part[2] for part in parts) - norm
    out_blank = lax.dynamic_slice_in_dim(log_blank, mine * positions, positions, axis=1)
    out_label = lax.dynamic_slice_in_dim(log_label, mine * positions, positions, axis=1)
    with jax.named_scope("gather_grid"):
        grid = lax.all_gather(jnp.stack([log_blank, log_label]), "tm", axis=0, tiled=False)
    loss = lattice_loss(frame_len, label_len, grid).reshape(1)
    return out_blank[None], out_label[None], loss


def solution(mesh):
    return jax.shard_map(
        shards,
        mesh=mesh,
        in_specs=(
            P("batch", "tm", None),
            P("batch", "label", None),
            P("batch", "tm"),
            P("batch", "label"),
            P("batch"),
            P("batch"),
        ),
        out_specs=(P("batch", "tm", "label"), P("batch", "tm", "label"), P("batch")),
        check_vma=False,
    )
```

```python
import functools

import jax
import jax.numpy as jnp
from jax import lax
from jax.experimental import pallas as pl
from jax.experimental.pallas import tpu as pltpu
from jax.sharding import PartitionSpec as P

NEG = -1e30
F32 = jnp.float32
BF16 = jnp.bfloat16
SPAN = 16
SIDE = 8
GROUP = 4
CHUNKS = 2
LABEL_WAYS = 4
BATCH_WAYS = 4


def pack_kernel(weight_ref, pred_ref, labels_ref, block_ref, packed_ref):
    mine, odd_block = lax.axis_index("label"), lax.rem(lax.axis_index("tm"), 2) == 1
    tiles, positions, _ = packed_ref.shape
    rows = block_ref.shape[0]
    lane = lax.broadcasted_iota(jnp.int32, (rows, 128), 1)
    values = jnp.where(mine < 2, weight_ref[:, :128].astype(F32), weight_ref[:, 128:].astype(F32))
    left = jnp.where(odd_block, values[rows:], values[:rows])
    right = jnp.where(odd_block, values[:rows], values[rows:])
    second = lax.rem(mine, 2) == 1
    left = jnp.where(second, pltpu.roll(left, 64, 1), left)
    right = jnp.where(second, right, pltpu.roll(right, 64, 1))
    block_ref[...] = jnp.where(lane < 64, left, right).astype(BF16)
    for tile in range(tiles - 1):
        packed_ref[tile] = pred_ref[:, 128 * tile:128 * tile + 128]
    labels = jnp.broadcast_to(labels_ref[...], (positions, positions))
    across = lax.broadcasted_iota(jnp.int32, (positions, positions), 0)
    along = lax.broadcasted_iota(jnp.int32, (positions, positions), 1)
    own = jnp.where(across == along, labels, 0)
    high = jnp.sum((own >> 6).astype(F32), axis=1, keepdims=True)
    low = jnp.sum((own & 63).astype(F32), axis=1, keepdims=True)
    lane = lax.broadcasted_iota(jnp.int32, (positions, 128), 1)
    packed_ref[tiles - 1] = jnp.where(lane == 0, high, jnp.where(lane == 1, low, 0.0)).astype(BF16)


def pack(weight, pred, labels):
    positions, width = pred.shape
    vmem = pl.BlockSpec(memory_space=pltpu.VMEM)
    return pl.pallas_call(
        pack_kernel,
        out_shape=(
            jax.ShapeDtypeStruct((weight.shape[0] // 2, 128), BF16),
            jax.ShapeDtypeStruct((width // 128 + 1, positions, 128), BF16),
        ),
        in_specs=[vmem] * 3,
        out_specs=(vmem, vmem),
        name="pack",
    )(weight, pred, labels)


def joint_kernel(
    enc_ref, own_ref, own_pred_ref, mine_ref, theirs_ref,
    lse_ref, blank_ref, picked_ref,
    enc, pred, chosen, picks, columns_first, weight, hidden_a, hidden_b, logits_a, logits_b, top, total, top_a, top_b,
):
    mine, batch, core = lax.axis_index("label"), lax.axis_index("batch"), lax.rem(lax.axis_index("tm"), 2)
    frames, width = enc_ref.shape
    tiles, positions, _ = pred.shape
    share = weight.shape[0]
    chunk = share // CHUNKS
    enc[...] = enc_ref[...].astype(F32)
    blocks, half_rows, _ = own_ref.shape
    some = blocks // 2
    lane = lax.broadcasted_iota(jnp.int32, (half_rows, 128), 1)

    def put_rows(ref, start, count, source, first_pair):
        at = pl.multiple_of(source * 2 * half_rows, 8)
        for pair in range(count // 2):
            left = ref[start + 2 * pair].astype(F32)
            right = ref[start + 2 * pair + 1].astype(F32)
            columns_first[first_pair + pair, pl.ds(at, half_rows), :] = jnp.where(lane < 64, left, right)
            columns_first[first_pair + pair, pl.ds(at + half_rows, half_rows), :] = jnp.where(lane < 64, right, left)

    def put_positions(ref, start, count, source, first):
        at = pl.multiple_of(source * half_rows, 8)
        for index in range(count):
            pred[first + index, pl.ds(at, half_rows), :] = ref[start + index].astype(F32)

    def wrap(value, ways):
        return lax.rem(value + ways, ways)

    put_rows(own_ref, 0, blocks, batch, 0)
    put_positions(own_pred_ref, 0, tiles, mine, 0)
    for ref, side in ((mine_ref, core), (theirs_ref, 1 - core)):
        step = 2 * side - 1
        put_rows(ref, 0, blocks, wrap(batch + step, BATCH_WAYS), 0)
        put_rows(ref, blocks, some, wrap(batch + 2, BATCH_WAYS), side * (some // 2))
        put_positions(ref, blocks + some, tiles, wrap(mine + step, LABEL_WAYS), 0)
        put_positions(ref, blocks + some + tiles, tiles // 2, wrap(mine + 2, LABEL_WAYS), side * (tiles // 2))
    depth = lax.broadcasted_iota(jnp.int32, (128, width), 1)
    upper = lax.rem(depth, 2 * half_rows) < half_rows
    for tile in range(share // 128):
        turned = columns_first[tile].T
        swapped = jnp.concatenate([turned[64:], turned[:64]], axis=0)
        weight[128 * tile:128 * tile + 128, :] = jnp.where(upper, turned, swapped).astype(BF16)

    digits = pred[tiles - 1]
    high = digits[:, 0:1].astype(jnp.int32)
    low = digits[:, 1:2].astype(jnp.int32)
    spot = jnp.where((high & 3) == mine, (high >> 2) * 64 + low, -1)
    columns = lax.broadcasted_iota(jnp.int32, (positions, share), 1)
    one_hot = (columns == spot).astype(F32).astype(BF16)
    chosen[...] = jnp.dot(one_hot, weight[...], preferred_element_type=F32)
    picks[...] = jnp.zeros_like(picks)
    lanes = lax.broadcasted_iota(jnp.int32, picks.shape, 1)

    def make_hidden(frame, part, out):
        rows = slice(part * positions, (part + 1) * positions)
        picked = jnp.zeros((positions, 128), F32)
        frame_row = enc[pl.ds(frame, 1), :]
        for tile in range(tiles - 1):
            strip = slice(128 * tile, 128 * tile + 128)
            rounded = jnp.tanh(pred[tile] + frame_row[:, strip]).astype(BF16)
            out[rows, strip] = rounded
            picked = picked + rounded.astype(F32) * chosen[:, strip]
        picked = jnp.sum(picked, axis=1, keepdims=True)
        picks[...] = jnp.where(lanes == frame, picked, picks[...])

    def multiply(part, hidden, out, chunk_top):
        acc = lax.dot_general(
            weight[part * chunk:(part + 1) * chunk, :], hidden[...],
            (((1,), (1,)), ((), ())), preferred_element_type=F32,
        )
        out[...] = acc
        chunk_top[...] = jnp.max(acc, axis=0, keepdims=True)

    def gather_terms(part, group, logits, chunk_top):
        values = logits[...]
        high = chunk_top[...]
        if part == 0:
            blank_ref[pl.ds(group, 1), :] = logits[0:1, :]
            total[...] = jnp.sum(jnp.exp(values - high), axis=0, keepdims=True)
            top[...] = high
        else:
            high = jnp.maximum(high, top[...])
            total[...] = total[...] * jnp.exp(top[...] - high) + jnp.sum(
                jnp.exp(values - high), axis=0, keepdims=True
            )
            top[...] = high
        if part == CHUNKS - 1:
            lse_ref[pl.ds(group, 1), :] = top[...] + jnp.log(total[...])

    groups = frames // GROUP
    for part in range(GROUP):
        make_hidden(part, part, hidden_a)
    logits_b[...] = jnp.zeros_like(logits_b)
    top[...] = jnp.zeros_like(top)
    top_b[...] = jnp.zeros_like(top)
    total[...] = jnp.ones_like(total)
    each = GROUP // CHUNKS

    def half(group, now, later):
        for part in range(CHUNKS):
            fresh, old = (logits_a, logits_b) if part % 2 == 0 else (logits_b, logits_a)
            fresh_top, old_top = (top_a, top_b) if part % 2 == 0 else (top_b, top_a)
            multiply(part, now, fresh, fresh_top)
            for which in range(part * each, (part + 1) * each):
                make_hidden(jnp.minimum(group + 1, groups - 1) * GROUP + which, which, later)
            if part == 0:
                gather_terms(CHUNKS - 1, jnp.maximum(group - 1, 0), old, old_top)
            else:
                gather_terms(part - 1, group, old, old_top)

    def step(pair, carry):
        half(2 * pair, hidden_a, hidden_b)
        half(2 * pair + 1, hidden_b, hidden_a)
        return carry

    lax.fori_loop(0, groups // 2, step, 0)
    gather_terms(CHUNKS - 1, groups - 1, logits_b, top_b)
    picked_ref[...] = picks[...].T[:frames, :]


def joint_terms(enc, own, own_pred, mine, theirs):
    frames, width = enc.shape
    tiles = own_pred.shape[0]
    positions = LABEL_WAYS * own_pred.shape[1]
    share = 64 * own.shape[0]
    wide = GROUP * positions
    grouped = jax.ShapeDtypeStruct((frames // GROUP, wide), F32)
    vmem = pl.BlockSpec(memory_space=pltpu.VMEM)
    smem = pl.BlockSpec(memory_space=pltpu.SMEM)
    flops = 2 * frames * positions * width * share
    return pl.pallas_call(
        joint_kernel,
        out_shape=(grouped, grouped, jax.ShapeDtypeStruct((frames, positions), F32)),
        in_specs=[vmem] * 5,
        out_specs=(vmem,) * 3,
        scratch_shapes=[
            pltpu.VMEM((frames, width), F32),
            pltpu.VMEM((tiles, positions, 128), F32),
            pltpu.VMEM((positions, width), F32),
            pltpu.VMEM((positions, 128), F32),
            pltpu.VMEM((share // 128, width, 128), F32),
            pltpu.VMEM((share, width), BF16),
            pltpu.VMEM((wide, width), BF16),
            pltpu.VMEM((wide, width), BF16),
            pltpu.VMEM((share // CHUNKS, wide), F32),
            pltpu.VMEM((share // CHUNKS, wide), F32),
            pltpu.VMEM((1, wide), F32),
            pltpu.VMEM((1, wide), F32),
            pltpu.VMEM((1, wide), F32),
            pltpu.VMEM((1, wide), F32),
        ],
        compiler_params=pltpu.CompilerParams(vmem_limit_bytes=48 << 20),
        cost_estimate=pl.CostEstimate(flops=flops, bytes_accessed=2 << 20, transcendentals=0),
        name="joint",
    )(enc, own, own_pred, mine, theirs)


def tree(combine, terms):
    while len(terms) > 1:
        pairs = [combine(a, b) for a, b in zip(terms[::2], terms[1::2])]
        terms = pairs + terms[len(terms) - len(terms) % 2:]
    return terms[0]


def log_sum(terms):
    if len(terms) == 1:
        return terms[0]
    if len(terms) == 2:
        gap = jnp.minimum(*terms) - jnp.maximum(*terms)
        return jnp.maximum(*terms) + jnp.log(1.0 + jnp.exp(gap))
    top = tree(jnp.maximum, terms)
    return top + jnp.log(tree(jnp.add, [jnp.exp(term - top) for term in terms]))


def strips_of(values):
    return [values[:, start:start + 128] for start in range(0, values.shape[1], 128)]


def merge(strips, crossed, step):
    parts = [jnp.where(crossed, strips[(p - step) % len(strips)], strips[p]) for p in range(len(strips))]
    return jnp.concatenate(parts, axis=1)


def shift_lanes(values, by):
    if by == 0:
        return values
    lane = lax.broadcasted_iota(jnp.int32, (values.shape[0], 128), 1)
    turned = [pltpu.roll(strip, by % 128, 1) for strip in strips_of(values)]
    return merge(turned, lane < by, 1) if by > 0 else merge(turned, lane >= 128 + by, -1)


def compose(first, then):
    terms = []
    for count in range(len(first) + len(then) - 1):
        parts = [
            then[late] + shift_lanes(first[count - late], late)
            for late in range(len(then))
            if 0 <= count - late < len(first)
        ]
        terms.append(log_sum(parts))
    return terms


def shear(values, lead):
    rows = values.shape[0]
    lanes = lax.broadcasted_iota(jnp.int32, values.shape, 1)
    if lead:
        values = pltpu.roll(values, rows - lead, 0)
    for bit in (64, 32, 16, 8, 4, 2, 1):
        values = jnp.where((lanes & bit) != 0, pltpu.roll(values, bit, 0), values)
    return values


def lattice_kernel(
    frame_len_ref, label_len_ref, grid_ref, loss_ref, blank_ref, label_ref, stay, move, ahead, back, ahead_far, back_far
):
    blocks, _, frames_dev, positions = grid_ref.shape
    frames = blocks * frames_dev
    strips, diagonals, _ = stay.shape
    lanes_all = 128 * strips
    flen = frame_len_ref[0]
    ulen = label_len_ref[0]
    mine, held = lax.axis_index("label"), blank_ref.shape[1]
    for which, ref in enumerate((blank_ref, label_ref)):
        rows = grid_ref[lax.axis_index("tm"), which]
        own = rows[:, :held]
        for index in range(1, LABEL_WAYS):
            own = jnp.where(mine == index, rows[:, index * held:(index + 1) * held], own)
        ref[...] = own
    spare = jnp.full((frames, lanes_all - positions), NEG, F32)
    tall = frames + 128
    pad = jnp.full((tall - frames, 128), NEG, F32)

    def whole(which):
        rows = jnp.concatenate([grid_ref[block, which] for block in range(blocks)], axis=0)
        return jnp.concatenate([rows, spare], axis=1)

    blank = whole(0)
    label = shift_lanes(whole(1), 1)
    stay[...] = jnp.full(stay.shape, NEG, F32)
    move[...] = jnp.full(move.shape, NEG, F32)
    for part in range(strips):
        start = 128 * part
        rows = min(tall, diagonals - start)
        for source, out, lead in ((blank, stay, 0), (label, move, 1)):
            strip = jnp.concatenate([source[:, start:start + 128], pad], axis=0)
            out[part, start:start + rows, :] = shear(strip, lead)[:rows]

    depth = SIDE * SPAN
    for group in range(diagonals // depth):
        base = group * depth
        live = [p for p in range(strips) if 128 * p <= base + depth and base < 128 * p + 128 + frames]
        first, count_live = live[0], len(live)
        row = lax.broadcasted_iota(jnp.int32, (SIDE, 128 * count_live), 0)
        lane = lax.broadcasted_iota(jnp.int32, (SIDE, 128 * count_live), 1) + 128 * first
        in_row = lane < positions
        moves_in = in_row & (lane > 0)
        rest = jnp.where(lane == ulen, 0.0, NEG)
        steps = []
        for step in range(SPAN):
            time = base + row * SPAN + step - lane
            at = pl.ds(base + step, SIDE, stride=SPAN)
            held = jnp.concatenate([stay[part, at, :] for part in live], axis=1)
            moved = jnp.concatenate([move[part, at, :] for part in live], axis=1)
            held = jnp.where(in_row & (time < flen), held, rest)
            moved = jnp.where(moves_in & (time + 1 < flen), moved, NEG)
            steps.append([held, moved])
        while len(steps) > 1:
            steps = [compose(steps[i], steps[i + 1]) for i in range(0, len(steps), 2)]
        at = group * SIDE
        for count, values in enumerate(steps[0]):
            moved = shift_lanes(values, -count)
            for part in range(strips):
                if part in live:
                    strip = slice(128 * (part - first), 128 * (part - first) + 128)
                    forth, from_back = values[:, strip], moved[:, strip]
                else:
                    forth = jnp.full((SIDE, 128), NEG, F32)
                    if count == 0:
                        lane = lax.broadcasted_iota(jnp.int32, (SIDE, 128), 1) + 128 * part
                        forth = jnp.where(lane == ulen, 0.0, NEG)
                    from_back = forth
                if count < SPAN:
                    ahead[part, pl.ds(at * SPAN + count, SIDE, stride=SPAN), :] = forth
                    back[part, pl.ds(at * SPAN + SPAN - 1 - count, SIDE, stride=SPAN), :] = from_back
                else:
                    ahead_far[at:at + SIDE, 128 * part:128 * part + 128] = forth
                    back_far[at:at + SIDE, 128 * part:128 * part + 128] = from_back

    spans = diagonals // SPAN
    place = lax.broadcasted_iota(jnp.int32, (1, lanes_all), 1)

    def advance(state, step, table, far, block):
        rows = pl.ds(pl.multiple_of(block * SPAN, SPAN), SPAN)
        weights = jnp.concatenate([table[part, rows, :] for part in range(strips)], axis=1)
        first = 0 if step > 0 else 128 - SPAN + 1
        turned = [
            pltpu.roll(jnp.broadcast_to(strip, (SPAN, 128)), first, 1, stride=1, stride_axis=0)
            for strip in strips_of(state)
        ]
        lane = lax.broadcasted_iota(jnp.int32, (SPAN, 128), 1)
        row = lax.broadcasted_iota(jnp.int32, (SPAN, 128), 0)
        crossed = lane < row if step > 0 else lane >= first + row
        near = weights + merge(turned, crossed, step)
        last = far[pl.ds(block, 1), :] + shift_lanes(state, step * SPAN)
        top = jnp.maximum(jnp.max(near, axis=0, keepdims=True), last)
        total = jnp.sum(jnp.exp(near - top), axis=0, keepdims=True) + jnp.exp(last - top)
        return top + jnp.log(total)

    def sweep(index, carry):
        alpha, beta = carry
        alpha = advance(alpha, 1, ahead, ahead_far, index)
        beta = advance(beta, -1, back, back_far, spans - 1 - index)
        return alpha, beta

    alpha = jnp.where(place == 0, 0.0, NEG)
    beta = jnp.where(place == ulen, 0.0, NEG)
    alpha, beta = lax.fori_loop(0, spans // 2, sweep, (alpha, beta))
    both = alpha + beta
    top = jnp.max(both, axis=1, keepdims=True)
    value = top + jnp.log(jnp.sum(jnp.exp(both - top), axis=1, keepdims=True))
    loss_ref[...] = -value / jnp.full((1, 1), flen, jnp.int32).astype(F32)


def lattice_loss(frame_len, label_len, grid):
    blocks, _, frames_dev, positions = grid.shape
    lanes = -(-positions // 128) * 128
    diagonals = -(-(blocks * frames_dev + positions) // (SIDE * SPAN)) * SIDE * SPAN
    assert (diagonals // SPAN) % 2 == 0
    strip = pltpu.VMEM((lanes // 128, diagonals, 128), F32)
    block = jax.ShapeDtypeStruct((frames_dev, positions // LABEL_WAYS), F32)
    table = pltpu.VMEM((lanes // 128, diagonals, 128), F32)
    far = pltpu.VMEM((diagonals // SPAN, lanes), F32)
    vmem = pl.BlockSpec(memory_space=pltpu.VMEM)
    smem = pl.BlockSpec(memory_space=pltpu.SMEM)
    return pl.pallas_call(
        lattice_kernel,
        out_shape=(jax.ShapeDtypeStruct((1, 1), F32), block, block),
        in_specs=[smem, smem, vmem],
        out_specs=(vmem,) * 3,
        scratch_shapes=[
            strip,
            strip,
            table,
            table,
            far,
            far,
        ],
        compiler_params=pltpu.CompilerParams(vmem_limit_bytes=40 << 20),
        name="lattice",
    )(frame_len, label_len, grid)


def around(array, axis):
    size = lax.axis_size(axis)
    moved = [
        lax.ppermute(array, axis, [(i, (i + by) % size) for i in range(size)])
        for by in range(size - 1, 0, -1)
    ]
    return [array] + moved


def both_ways(array, axis):
    ways, cores = lax.axis_size(axis), lax.axis_size("tm")
    axes = ("batch", "tm") if axis == "batch" else ("tm", "label")

    def device(way, at):
        return way % ways * cores + at if axis == "batch" else at * ways + way % ways

    near, opposite = [], []
    for way in range(ways):
        for at in range(cores):
            near.append((device(way, at), device(way + (1 if at % 2 == 0 else -1), at)))
            opposite.append((device(way, at), device(way + 2, at)))
    some = array.shape[0] // 2
    half = lax.dynamic_slice_in_dim(array, lax.axis_index("tm") % 2 * some, some, axis=0)
    return lax.ppermute(array, axes, near), lax.ppermute(half, axes, opposite)


def shards(enc_joint, pred_joint, out_weight, labels, frame_len, label_len):
    mine = lax.axis_index("label")
    own, own_pred = pack(out_weight, pred_joint[0], labels)
    with jax.named_scope("gather_weight"):
        own = lax.all_gather(own, "tm", axis=0, tiled=False)
    with jax.named_scope("fetch"):
        from_others = jnp.concatenate([*both_ways(own, "batch"), *both_ways(own_pred, "label")], axis=0)
        swap = [(i, i ^ 1) for i in range(lax.axis_size("tm"))]
        theirs = lax.ppermute(from_others, "tm", swap)
    lse, blank, picked = joint_terms(enc_joint[0], own, own_pred, from_others, theirs)
    with jax.named_scope("combine_vocab"):
        blank = jnp.where(mine == 0, blank, 0.0)
        parts = jnp.stack([lse.reshape(picked.shape), blank.reshape(picked.shape), picked])
        parts = around(parts, "label")
        top = functools.reduce(jnp.maximum, [part[0] for part in parts])
        norm = top + jnp.log(sum(jnp.exp(part[0] - top) for part in parts))
        log_blank = sum(part[1] for part in parts) - norm
        log_label = sum(part[2] for part in parts) - norm
    with jax.named_scope("gather_grid"):
        grid = lax.all_gather(jnp.stack([log_blank, log_label]), "tm", axis=0, tiled=False)
    loss, out_blank, out_label = lattice_loss(frame_len, label_len, grid)
    return out_blank[None], out_label[None], loss.reshape(1)


def solution(mesh):
    return jax.shard_map(
        shards,
        mesh=mesh,
        in_specs=(
            P("batch", "tm", None),
            P("batch", "label", None),
            P("batch", "tm"),
            P("batch", "label"),
            P("batch"),
            P("batch"),
        ),
        out_specs=(P("batch", "tm", "label"), P("batch", "tm", "label"), P("batch")),
        check_vma=False,
    )
```

```python
import functools

import jax
import jax.numpy as jnp
from jax import lax
from jax.experimental import pallas as pl
from jax.experimental.pallas import tpu as pltpu
from jax.sharding import PartitionSpec as P

NEG = -1e30
F32 = jnp.float32
BF16 = jnp.bfloat16
SPAN = 16
SIDE = 8
GROUP = 4
CHUNKS = 2
LABEL_WAYS = 4
BATCH_WAYS = 4


def pack_kernel(weight_ref, pred_ref, labels_ref, block_ref, packed_ref):
    mine, odd_block = lax.axis_index("label"), lax.rem(lax.axis_index("tm"), 2) == 1
    tiles, positions, _ = packed_ref.shape
    rows = block_ref.shape[0]
    lane = lax.broadcasted_iota(jnp.int32, (rows, 128), 1)
    values = jnp.where(mine < 2, weight_ref[:, :128].astype(F32), weight_ref[:, 128:].astype(F32))
    left = jnp.where(odd_block, values[rows:], values[:rows])
    right = jnp.where(odd_block, values[:rows], values[rows:])
    second = lax.rem(mine, 2) == 1
    left = jnp.where(second, pltpu.roll(left, 64, 1), left)
    right = jnp.where(second, right, pltpu.roll(right, 64, 1))
    block_ref[...] = jnp.where(lane < 64, left, right).astype(BF16)
    for tile in range(tiles - 1):
        packed_ref[tile] = pred_ref[:, 128 * tile:128 * tile + 128]
    labels = jnp.broadcast_to(labels_ref[...], (positions, positions))
    across = lax.broadcasted_iota(jnp.int32, (positions, positions), 0)
    along = lax.broadcasted_iota(jnp.int32, (positions, positions), 1)
    own = jnp.where(across == along, labels, 0)
    high = jnp.sum((own >> 6).astype(F32), axis=1, keepdims=True)
    low = jnp.sum((own & 63).astype(F32), axis=1, keepdims=True)
    lane = lax.broadcasted_iota(jnp.int32, (positions, 128), 1)
    packed_ref[tiles - 1] = jnp.where(lane == 0, high, jnp.where(lane == 1, low, 0.0)).astype(BF16)


def pack(weight, pred, labels):
    positions, width = pred.shape
    vmem = pl.BlockSpec(memory_space=pltpu.VMEM)
    return pl.pallas_call(
        pack_kernel,
        out_shape=(
            jax.ShapeDtypeStruct((weight.shape[0] // 2, 128), BF16),
            jax.ShapeDtypeStruct((width // 128 + 1, positions, 128), BF16),
        ),
        in_specs=[vmem] * 3,
        out_specs=(vmem, vmem),
        name="pack",
    )(weight, pred, labels)


def joint_kernel(
    enc_ref, own_ref, own_pred_ref, mine_ref, theirs_ref,
    lse_ref, blank_ref, picked_ref,
    enc, pred, chosen, picks, columns_first, weight, hidden_a, hidden_b, logits_a, logits_b, top, total, top_a, top_b,
):
    mine, batch, core = lax.axis_index("label"), lax.axis_index("batch"), lax.rem(lax.axis_index("tm"), 2)
    frames, width = enc_ref.shape
    tiles, positions, _ = pred.shape
    share = weight.shape[0]
    chunk = share // CHUNKS
    enc[...] = enc_ref[...].astype(F32)
    blocks, half_rows, _ = own_ref.shape
    some = blocks // 2
    lane = lax.broadcasted_iota(jnp.int32, (half_rows, 128), 1)

    def put_rows(ref, start, count, source, first_pair):
        at = pl.multiple_of(source * 2 * half_rows, 8)
        for pair in range(count // 2):
            left = ref[start + 2 * pair].astype(F32)
            right = ref[start + 2 * pair + 1].astype(F32)
            columns_first[first_pair + pair, pl.ds(at, half_rows), :] = jnp.where(lane < 64, left, right)
            columns_first[first_pair + pair, pl.ds(at + half_rows, half_rows), :] = jnp.where(lane < 64, right, left)

    def put_positions(ref, start, count, source, first):
        at = pl.multiple_of(source * half_rows, 8)
        for index in range(count):
            pred[first + index, pl.ds(at, half_rows), :] = ref[start + index].astype(F32)

    def wrap(value, ways):
        return lax.rem(value + ways, ways)

    put_rows(own_ref, 0, blocks, batch, 0)
    put_positions(own_pred_ref, 0, tiles, mine, 0)
    for ref, side in ((mine_ref, core), (theirs_ref, 1 - core)):
        step = 2 * side - 1
        put_rows(ref, 0, blocks, wrap(batch + step, BATCH_WAYS), 0)
        put_rows(ref, blocks, some, wrap(batch + 2, BATCH_WAYS), side * (some // 2))
        put_positions(ref, blocks + some, tiles, wrap(mine + step, LABEL_WAYS), 0)
        put_positions(ref, blocks + some + tiles, tiles // 2, wrap(mine + 2, LABEL_WAYS), side * (tiles // 2))
    depth = lax.broadcasted_iota(jnp.int32, (128, width), 1)
    upper = lax.rem(depth, 2 * half_rows) < half_rows
    for tile in range(share // 128):
        turned = columns_first[tile].T
        swapped = jnp.concatenate([turned[64:], turned[:64]], axis=0)
        weight[128 * tile:128 * tile + 128, :] = jnp.where(upper, turned, swapped).astype(BF16)

    digits = pred[tiles - 1]
    high = digits[:, 0:1].astype(jnp.int32)
    low = digits[:, 1:2].astype(jnp.int32)
    spot = jnp.where((high & 3) == mine, (high >> 2) * 64 + low, -1)
    columns = lax.broadcasted_iota(jnp.int32, (positions, share), 1)
    one_hot = (columns == spot).astype(F32).astype(BF16)
    chosen[...] = jnp.dot(one_hot, weight[...], preferred_element_type=F32)
    picks[...] = jnp.zeros_like(picks)
    lanes = lax.broadcasted_iota(jnp.int32, picks.shape, 1)

    def make_hidden(frame, part, out):
        rows = slice(part * positions, (part + 1) * positions)
        picked = jnp.zeros((positions, 128), F32)
        frame_row = enc[pl.ds(frame, 1), :]
        for tile in range(tiles - 1):
            strip = slice(128 * tile, 128 * tile + 128)
            rounded = jnp.tanh(pred[tile] + frame_row[:, strip]).astype(BF16)
            out[rows, strip] = rounded
            picked = picked + rounded.astype(F32) * chosen[:, strip]
        picked = jnp.sum(picked, axis=1, keepdims=True)
        picks[...] = jnp.where(lanes == frame, picked, picks[...])

    def multiply(part, hidden, out, chunk_top):
        acc = lax.dot_general(
            weight[part * chunk:(part + 1) * chunk, :], hidden[...],
            (((1,), (1,)), ((), ())), preferred_element_type=F32,
        )
        out[...] = acc
        chunk_top[...] = jnp.max(acc, axis=0, keepdims=True)

    def gather_terms(part, group, logits, chunk_top):
        values = logits[...]
        high = chunk_top[...]
        if part == 0:
            blank_ref[pl.ds(group, 1), :] = logits[0:1, :]
            total[...] = jnp.sum(jnp.exp(values - high), axis=0, keepdims=True)
            top[...] = high
        else:
            high = jnp.maximum(high, top[...])
            total[...] = total[...] * jnp.exp(top[...] - high) + jnp.sum(
                jnp.exp(values - high), axis=0, keepdims=True
            )
            top[...] = high
        if part == CHUNKS - 1:
            lse_ref[pl.ds(group, 1), :] = top[...] + jnp.log(total[...])

    groups = frames // GROUP
    for part in range(GROUP):
        make_hidden(part, part, hidden_a)
    logits_b[...] = jnp.zeros_like(logits_b)
    top[...] = jnp.zeros_like(top)
    top_b[...] = jnp.zeros_like(top)
    total[...] = jnp.ones_like(total)
    each = GROUP // CHUNKS

    def half(group, now, later):
        for part in range(CHUNKS):
            fresh, old = (logits_a, logits_b) if part % 2 == 0 else (logits_b, logits_a)
            fresh_top, old_top = (top_a, top_b) if part % 2 == 0 else (top_b, top_a)
            multiply(part, now, fresh, fresh_top)
            for which in range(part * each, (part + 1) * each):
                make_hidden(jnp.minimum(group + 1, groups - 1) * GROUP + which, which, later)
            if part == 0:
                gather_terms(CHUNKS - 1, jnp.maximum(group - 1, 0), old, old_top)
            else:
                gather_terms(part - 1, group, old, old_top)

    def step(pair, carry):
        half(2 * pair, hidden_a, hidden_b)
        half(2 * pair + 1, hidden_b, hidden_a)
        return carry

    lax.fori_loop(0, groups // 2, step, 0)
    gather_terms(CHUNKS - 1, groups - 1, logits_b, top_b)
    picked_ref[...] = picks[...].T[:frames, :]


def joint_terms(enc, own, own_pred, mine, theirs):
    frames, width = enc.shape
    tiles = own_pred.shape[0]
    positions = LABEL_WAYS * own_pred.shape[1]
    share = 64 * own.shape[0]
    wide = GROUP * positions
    grouped = jax.ShapeDtypeStruct((frames // GROUP, wide), F32)
    vmem = pl.BlockSpec(memory_space=pltpu.VMEM)
    smem = pl.BlockSpec(memory_space=pltpu.SMEM)
    flops = 2 * frames * positions * width * share
    return pl.pallas_call(
        joint_kernel,
        out_shape=(grouped, grouped, jax.ShapeDtypeStruct((frames, positions), F32)),
        in_specs=[vmem] * 5,
        out_specs=(vmem,) * 3,
        scratch_shapes=[
            pltpu.VMEM((frames, width), F32),
            pltpu.VMEM((tiles, positions, 128), F32),
            pltpu.VMEM((positions, width), F32),
            pltpu.VMEM((positions, 128), F32),
            pltpu.VMEM((share // 128, width, 128), F32),
            pltpu.VMEM((share, width), BF16),
            pltpu.VMEM((wide, width), BF16),
            pltpu.VMEM((wide, width), BF16),
            pltpu.VMEM((share // CHUNKS, wide), F32),
            pltpu.VMEM((share // CHUNKS, wide), F32),
            pltpu.VMEM((1, wide), F32),
            pltpu.VMEM((1, wide), F32),
            pltpu.VMEM((1, wide), F32),
            pltpu.VMEM((1, wide), F32),
        ],
        compiler_params=pltpu.CompilerParams(vmem_limit_bytes=48 << 20),
        cost_estimate=pl.CostEstimate(flops=flops, bytes_accessed=2 << 20, transcendentals=0),
        name="joint",
    )(enc, own, own_pred, mine, theirs)


def tree(combine, terms):
    while len(terms) > 1:
        pairs = [combine(a, b) for a, b in zip(terms[::2], terms[1::2])]
        terms = pairs + terms[len(terms) - len(terms) % 2:]
    return terms[0]


def log_sum(terms):
    if len(terms) == 1:
        return terms[0]
    if len(terms) == 2:
        gap = jnp.minimum(*terms) - jnp.maximum(*terms)
        return jnp.maximum(*terms) + jnp.log(1.0 + jnp.exp(gap))
    top = tree(jnp.maximum, terms)
    return top + jnp.log(tree(jnp.add, [jnp.exp(term - top) for term in terms]))


def strips_of(values):
    return [values[:, start:start + 128] for start in range(0, values.shape[1], 128)]


def merge(strips, crossed, step):
    parts = [jnp.where(crossed, strips[(p - step) % len(strips)], strips[p]) for p in range(len(strips))]
    return jnp.concatenate(parts, axis=1)


def shift_lanes(values, by):
    if by == 0:
        return values
    lane = lax.broadcasted_iota(jnp.int32, (values.shape[0], 128), 1)
    turned = [pltpu.roll(strip, by % 128, 1) for strip in strips_of(values)]
    return merge(turned, lane < by, 1) if by > 0 else merge(turned, lane >= 128 + by, -1)


def compose(first, then):
    terms = []
    for count in range(len(first) + len(then) - 1):
        parts = [
            then[late] + shift_lanes(first[count - late], late)
            for late in range(len(then))
            if 0 <= count - late < len(first)
        ]
        terms.append(log_sum(parts))
    return terms


def shear(values, lead):
    rows = values.shape[0]
    lanes = lax.broadcasted_iota(jnp.int32, values.shape, 1)
    if lead:
        values = pltpu.roll(values, rows - lead, 0)
    for bit in (64, 32, 16, 8, 4, 2, 1):
        values = jnp.where((lanes & bit) != 0, pltpu.roll(values, bit, 0), values)
    return values


def lattice_kernel(
    frame_len_ref, label_len_ref, grid_ref, loss_ref, blank_ref, label_ref, stay, move, ahead, back, ahead_far, back_far
):
    blocks, _, frames_dev, positions = grid_ref.shape
    frames = blocks * frames_dev
    strips, diagonals, _ = stay.shape
    lanes_all = 128 * strips
    flen = frame_len_ref[0]
    ulen = label_len_ref[0]
    mine, held = lax.axis_index("label"), blank_ref.shape[1]
    for which, ref in enumerate((blank_ref, label_ref)):
        rows = grid_ref[lax.axis_index("tm"), which]
        own = rows[:, :held]
        for index in range(1, LABEL_WAYS):
            own = jnp.where(mine == index, rows[:, index * held:(index + 1) * held], own)
        ref[...] = own
    spare = jnp.full((frames, lanes_all - positions), NEG, F32)
    tall = frames + 128
    pad = jnp.full((tall - frames, 128), NEG, F32)

    def whole(which):
        rows = jnp.concatenate([grid_ref[block, which] for block in range(blocks)], axis=0)
        return jnp.concatenate([rows, spare], axis=1)

    blank = whole(0)
    label = shift_lanes(whole(1), 1)
    stay[...] = jnp.full(stay.shape, NEG, F32)
    move[...] = jnp.full(move.shape, NEG, F32)
    for part in range(strips):
        start = 128 * part
        rows = min(tall, diagonals - start)
        for source, out, lead in ((blank, stay, 0), (label, move, 1)):
            strip = jnp.concatenate([source[:, start:start + 128], pad], axis=0)
            out[part, start:start + rows, :] = shear(strip, lead)[:rows]

    depth = SIDE * SPAN
    for group in range(diagonals // depth):
        base = group * depth
        live = [p for p in range(strips) if 128 * p <= base + depth and base < 128 * p + 128 + frames]
        first, count_live = live[0], len(live)
        row = lax.broadcasted_iota(jnp.int32, (SIDE, 128 * count_live), 0)
        lane = lax.broadcasted_iota(jnp.int32, (SIDE, 128 * count_live), 1) + 128 * first
        in_row = lane < positions
        moves_in = in_row & (lane > 0)
        rest = jnp.where(lane == ulen, 0.0, NEG)
        steps = []
        for step in range(SPAN):
            time = base + row * SPAN + step - lane
            at = pl.ds(base + step, SIDE, stride=SPAN)
            held = jnp.concatenate([stay[part, at, :] for part in live], axis=1)
            moved = jnp.concatenate([move[part, at, :] for part in live], axis=1)
            held = jnp.where(in_row & (time < flen), held, rest)
            moved = jnp.where(moves_in & (time + 1 < flen), moved, NEG)
            steps.append([held, moved])
        while len(steps) > 1:
            steps = [compose(steps[i], steps[i + 1]) for i in range(0, len(steps), 2)]
        at = group * SIDE
        for count, values in enumerate(steps[0]):
            moved = shift_lanes(values, -count)
            for part in range(strips):
                if part in live:
                    strip = slice(128 * (part - first), 128 * (part - first) + 128)
                    forth, from_back = values[:, strip], moved[:, strip]
                else:
                    forth = jnp.full((SIDE, 128), NEG, F32)
                    if count == 0:
                        lane = lax.broadcasted_iota(jnp.int32, (SIDE, 128), 1) + 128 * part
                        forth = jnp.where(lane == ulen, 0.0, NEG)
                    from_back = forth
                if count < SPAN:
                    ahead[part, pl.ds(at * SPAN + count, SIDE, stride=SPAN), :] = forth
                    back[part, pl.ds(at * SPAN + SPAN - 1 - count, SIDE, stride=SPAN), :] = from_back
                else:
                    ahead_far[at:at + SIDE, 128 * part:128 * part + 128] = forth
                    back_far[at:at + SIDE, 128 * part:128 * part + 128] = from_back

    spans = diagonals // SPAN
    place = lax.broadcasted_iota(jnp.int32, (1, lanes_all), 1)

    def advance(state, step, table, far, block):
        rows = pl.ds(pl.multiple_of(block * SPAN, SPAN), SPAN)
        weights = jnp.concatenate([table[part, rows, :] for part in range(strips)], axis=1)
        first = 0 if step > 0 else 128 - SPAN + 1
        turned = [
            pltpu.roll(jnp.broadcast_to(strip, (SPAN, 128)), first, 1, stride=1, stride_axis=0)
            for strip in strips_of(state)
        ]
        lane = lax.broadcasted_iota(jnp.int32, (SPAN, 128), 1)
        row = lax.broadcasted_iota(jnp.int32, (SPAN, 128), 0)
        crossed = lane < row if step > 0 else lane >= first + row
        near = weights + merge(turned, crossed, step)
        last = far[pl.ds(block, 1), :] + shift_lanes(state, step * SPAN)
        top = jnp.maximum(jnp.max(near, axis=0, keepdims=True), last)
        total = jnp.sum(jnp.exp(near - top), axis=0, keepdims=True) + jnp.exp(last - top)
        return top + jnp.log(total)

    def sweep(index, carry):
        alpha, beta = carry
        alpha = advance(alpha, 1, ahead, ahead_far, index)
        beta = advance(beta, -1, back, back_far, spans - 1 - index)
        return alpha, beta

    alpha = jnp.where(place == 0, 0.0, NEG)
    beta = jnp.where(place == ulen, 0.0, NEG)
    alpha, beta = lax.fori_loop(0, spans // 2, sweep, (alpha, beta))
    both = alpha + beta
    top = jnp.max(both, axis=1, keepdims=True)
    value = top + jnp.log(jnp.sum(jnp.exp(both - top), axis=1, keepdims=True))
    loss_ref[...] = -value / jnp.full((1, 1), flen, jnp.int32).astype(F32)


def lattice_loss(frame_len, label_len, grid):
    blocks, _, frames_dev, positions = grid.shape
    lanes = -(-positions // 128) * 128
    diagonals = -(-(blocks * frames_dev + positions) // (SIDE * SPAN)) * SIDE * SPAN
    assert (diagonals // SPAN) % 2 == 0
    strip = pltpu.VMEM((lanes // 128, diagonals, 128), F32)
    block = jax.ShapeDtypeStruct((frames_dev, positions // LABEL_WAYS), F32)
    table = pltpu.VMEM((lanes // 128, diagonals, 128), F32)
    far = pltpu.VMEM((diagonals // SPAN, lanes), F32)
    vmem = pl.BlockSpec(memory_space=pltpu.VMEM)
    smem = pl.BlockSpec(memory_space=pltpu.SMEM)
    return pl.pallas_call(
        lattice_kernel,
        out_shape=(jax.ShapeDtypeStruct((1, 1), F32), block, block),
        in_specs=[smem, smem, vmem],
        out_specs=(vmem,) * 3,
        scratch_shapes=[
            strip,
            strip,
            table,
            table,
            far,
            far,
        ],
        compiler_params=pltpu.CompilerParams(vmem_limit_bytes=40 << 20),
        name="lattice",
    )(frame_len, label_len, grid)


def around(array, axis):
    size = lax.axis_size(axis)
    moved = [
        lax.ppermute(array, axis, [(i, (i + by) % size) for i in range(size)])
        for by in range(1, size)
    ]
    return [array] + moved


def both_ways(array, axis):
    ways, cores = lax.axis_size(axis), lax.axis_size("tm")
    axes = ("batch", "tm") if axis == "batch" else ("tm", "label")

    def device(way, at):
        return way % ways * cores + at if axis == "batch" else at * ways + way % ways

    near, opposite = [], []
    for way in range(ways):
        for at in range(cores):
            near.append((device(way, at), device(way + (1 if at % 2 == 0 else -1), at)))
            opposite.append((device(way, at), device(way + 2, at)))
    some = array.shape[0] // 2
    half = lax.dynamic_slice_in_dim(array, lax.axis_index("tm") % 2 * some, some, axis=0)
    return lax.ppermute(array, axes, near), lax.ppermute(half, axes, opposite)


def shards(enc_joint, pred_joint, out_weight, labels, frame_len, label_len):
    mine = lax.axis_index("label")
    own, own_pred = pack(out_weight, pred_joint[0], labels)
    with jax.named_scope("gather_weight"):
        own = lax.all_gather(own, "tm", axis=0, tiled=False)
    with jax.named_scope("fetch"):
        from_others = jnp.concatenate([*both_ways(own, "batch"), *both_ways(own_pred, "label")], axis=0)
        swap = [(i, i ^ 1) for i in range(lax.axis_size("tm"))]
        theirs = lax.ppermute(from_others, "tm", swap)
    lse, blank, picked = joint_terms(enc_joint[0], own, own_pred, from_others, theirs)
    with jax.named_scope("combine_vocab"):
        blank = jnp.where(mine == 0, blank, 0.0)
        parts = jnp.stack([lse.reshape(picked.shape), blank.reshape(picked.shape), picked])
        parts = around(parts, "label")
        norm, log_blank, log_label = parts[0]
        for part in parts[1:]:
            norm = jnp.logaddexp(norm, part[0])
            log_blank, log_label = log_blank + part[1], log_label + part[2]
            norm, log_blank, log_label = lax.optimization_barrier((norm, log_blank, log_label))
        log_blank, log_label = log_blank - norm, log_label - norm
    with jax.named_scope("gather_grid"):
        grid = lax.all_gather(jnp.stack([log_blank, log_label]), "tm", axis=0, tiled=False)
    loss, out_blank, out_label = lattice_loss(frame_len, label_len, grid)
    return out_blank[None], out_label[None], loss.reshape(1)


def solution(mesh):
    return jax.shard_map(
        shards,
        mesh=mesh,
        in_specs=(
            P("batch", "tm", None),
            P("batch", "label", None),
            P("batch", "tm"),
            P("batch", "label"),
            P("batch"),
            P("batch"),
        ),
        out_specs=(P("batch", "tm", "label"), P("batch", "tm", "label"), P("batch")),
        check_vma=False,
    )
```

```python
import functools

import jax
import jax.numpy as jnp
from jax import lax
from jax.experimental import pallas as pl
from jax.experimental.pallas import tpu as pltpu
from jax.sharding import PartitionSpec as P

NEG = -1e30
F32 = jnp.float32
BF16 = jnp.bfloat16
SPAN = 16
SIDE = 8
GROUP = 4
CHUNKS = 2
LABEL_WAYS = 4
BATCH_WAYS = 4


def pack_kernel(weight_ref, pred_ref, labels_ref, block_ref, packed_ref):
    mine, odd_block = lax.axis_index("label"), lax.rem(lax.axis_index("tm"), 2) == 1
    tiles, positions, _ = packed_ref.shape
    rows = block_ref.shape[0]
    lane = lax.broadcasted_iota(jnp.int32, (rows, 128), 1)
    values = jnp.where(mine < 2, weight_ref[:, :128].astype(F32), weight_ref[:, 128:].astype(F32))
    left = jnp.where(odd_block, values[rows:], values[:rows])
    right = jnp.where(odd_block, values[:rows], values[rows:])
    second = lax.rem(mine, 2) == 1
    left = jnp.where(second, pltpu.roll(left, 64, 1), left)
    right = jnp.where(second, right, pltpu.roll(right, 64, 1))
    block_ref[...] = jnp.where(lane < 64, left, right).astype(BF16)
    for tile in range(tiles - 1):
        packed_ref[tile] = pred_ref[:, 128 * tile:128 * tile + 128]
    labels = jnp.broadcast_to(labels_ref[...], (positions, positions))
    across = lax.broadcasted_iota(jnp.int32, (positions, positions), 0)
    along = lax.broadcasted_iota(jnp.int32, (positions, positions), 1)
    own = jnp.where(across == along, labels, 0)
    high = jnp.sum((own >> 6).astype(F32), axis=1, keepdims=True)
    low = jnp.sum((own & 63).astype(F32), axis=1, keepdims=True)
    lane = lax.broadcasted_iota(jnp.int32, (positions, 128), 1)
    packed_ref[tiles - 1] = jnp.where(lane == 0, high, jnp.where(lane == 1, low, 0.0)).astype(BF16)


def pack(weight, pred, labels):
    positions, width = pred.shape
    vmem = pl.BlockSpec(memory_space=pltpu.VMEM)
    return pl.pallas_call(
        pack_kernel,
        out_shape=(
            jax.ShapeDtypeStruct((weight.shape[0] // 2, 128), BF16),
            jax.ShapeDtypeStruct((width // 128 + 1, positions, 128), BF16),
        ),
        in_specs=[vmem] * 3,
        out_specs=(vmem, vmem),
        name="pack",
    )(weight, pred, labels)


def joint_kernel(
    enc_ref, own_ref, own_pred_ref, mine_ref, theirs_ref,
    lse_ref, blank_ref, picked_ref,
    enc, pred, chosen, picks, columns_first, weight, hidden_a, hidden_b, logits_a, logits_b, top, total, top_a, top_b,
):
    mine, batch, core = lax.axis_index("label"), lax.axis_index("batch"), lax.rem(lax.axis_index("tm"), 2)
    frames, width = enc_ref.shape
    tiles, positions, _ = pred.shape
    share = weight.shape[0]
    chunk = share // CHUNKS
    enc[...] = enc_ref[...].astype(F32)
    blocks, half_rows, _ = own_ref.shape
    some = blocks // 2
    lane = lax.broadcasted_iota(jnp.int32, (half_rows, 128), 1)

    def put_rows(ref, start, count, source, first_pair):
        at = pl.multiple_of(source * 2 * half_rows, 8)
        for pair in range(count // 2):
            left = ref[start + 2 * pair].astype(F32)
            right = ref[start + 2 * pair + 1].astype(F32)
            columns_first[first_pair + pair, pl.ds(at, half_rows), :] = jnp.where(lane < 64, left, right)
            columns_first[first_pair + pair, pl.ds(at + half_rows, half_rows), :] = jnp.where(lane < 64, right, left)

    def put_positions(ref, start, count, source, first):
        at = pl.multiple_of(source * half_rows, 8)
        for index in range(count):
            pred[first + index, pl.ds(at, half_rows), :] = ref[start + index].astype(F32)

    def wrap(value, ways):
        return lax.rem(value + ways, ways)

    put_rows(own_ref, 0, blocks, batch, 0)
    put_positions(own_pred_ref, 0, tiles, mine, 0)
    for ref, side in ((mine_ref, core), (theirs_ref, 1 - core)):
        step = 2 * side - 1
        put_rows(ref, 0, blocks, wrap(batch + step, BATCH_WAYS), 0)
        put_rows(ref, blocks, some, wrap(batch + 2, BATCH_WAYS), side * (some // 2))
        put_positions(ref, blocks + some, tiles, wrap(mine + step, LABEL_WAYS), 0)
        put_positions(ref, blocks + some + tiles, tiles // 2, wrap(mine + 2, LABEL_WAYS), side * (tiles // 2))
    depth = lax.broadcasted_iota(jnp.int32, (128, width), 1)
    upper = lax.rem(depth, 2 * half_rows) < half_rows
    for tile in range(share // 128):
        turned = columns_first[tile].T
        swapped = jnp.concatenate([turned[64:], turned[:64]], axis=0)
        weight[128 * tile:128 * tile + 128, :] = jnp.where(upper, turned, swapped).astype(BF16)

    digits = pred[tiles - 1]
    high = digits[:, 0:1].astype(jnp.int32)
    low = digits[:, 1:2].astype(jnp.int32)
    spot = jnp.where((high & 3) == mine, (high >> 2) * 64 + low, -1)
    columns = lax.broadcasted_iota(jnp.int32, (positions, share), 1)
    one_hot = (columns == spot).astype(F32).astype(BF16)
    chosen[...] = jnp.dot(one_hot, weight[...], preferred_element_type=F32)
    picks[...] = jnp.zeros_like(picks)
    lanes = lax.broadcasted_iota(jnp.int32, picks.shape, 1)

    def make_hidden(frame, part, out):
        rows = slice(part * positions, (part + 1) * positions)
        picked = jnp.zeros((positions, 128), F32)
        frame_row = enc[pl.ds(frame, 1), :]
        for tile in range(tiles - 1):
            strip = slice(128 * tile, 128 * tile + 128)
            rounded = jnp.tanh(pred[tile] + frame_row[:, strip]).astype(BF16)
            out[rows, strip] = rounded
            picked = picked + rounded.astype(F32) * chosen[:, strip]
        picked = jnp.sum(picked, axis=1, keepdims=True)
        picks[...] = jnp.where(lanes == frame, picked, picks[...])

    def multiply(part, hidden, out, chunk_top):
        acc = lax.dot_general(
            weight[part * chunk:(part + 1) * chunk, :], hidden[...],
            (((1,), (1,)), ((), ())), preferred_element_type=F32,
        )
        out[...] = acc
        chunk_top[...] = jnp.max(acc, axis=0, keepdims=True)

    def gather_terms(part, group, logits, chunk_top):
        values = logits[...]
        high = chunk_top[...]
        if part == 0:
            blank_ref[pl.ds(group, 1), :] = logits[0:1, :]
            total[...] = jnp.sum(jnp.exp(values - high), axis=0, keepdims=True)
            top[...] = high
        else:
            high = jnp.maximum(high, top[...])
            total[...] = total[...] * jnp.exp(top[...] - high) + jnp.sum(
                jnp.exp(values - high), axis=0, keepdims=True
            )
            top[...] = high
        if part == CHUNKS - 1:
            lse_ref[pl.ds(group, 1), :] = top[...] + jnp.log(total[...])

    groups = frames // GROUP
    for part in range(GROUP):
        make_hidden(part, part, hidden_a)
    logits_b[...] = jnp.zeros_like(logits_b)
    top[...] = jnp.zeros_like(top)
    top_b[...] = jnp.zeros_like(top)
    total[...] = jnp.ones_like(total)
    each = GROUP // CHUNKS

    def half(group, now, later):
        for part in range(CHUNKS):
            fresh, old = (logits_a, logits_b) if part % 2 == 0 else (logits_b, logits_a)
            fresh_top, old_top = (top_a, top_b) if part % 2 == 0 else (top_b, top_a)
            multiply(part, now, fresh, fresh_top)
            for which in range(part * each, (part + 1) * each):
                make_hidden(jnp.minimum(group + 1, groups - 1) * GROUP + which, which, later)
            if part == 0:
                gather_terms(CHUNKS - 1, jnp.maximum(group - 1, 0), old, old_top)
            else:
                gather_terms(part - 1, group, old, old_top)

    def step(pair, carry):
        half(2 * pair, hidden_a, hidden_b)
        half(2 * pair + 1, hidden_b, hidden_a)
        return carry

    lax.fori_loop(0, groups // 2, step, 0)
    gather_terms(CHUNKS - 1, groups - 1, logits_b, top_b)
    picked_ref[...] = picks[...].T[:frames, :]


def joint_terms(enc, own, own_pred, mine, theirs):
    frames, width = enc.shape
    tiles = own_pred.shape[0]
    positions = LABEL_WAYS * own_pred.shape[1]
    share = 64 * own.shape[0]
    wide = GROUP * positions
    grouped = jax.ShapeDtypeStruct((frames // GROUP, wide), F32)
    vmem = pl.BlockSpec(memory_space=pltpu.VMEM)
    smem = pl.BlockSpec(memory_space=pltpu.SMEM)
    flops = 2 * frames * positions * width * share
    return pl.pallas_call(
        joint_kernel,
        out_shape=(grouped, grouped, jax.ShapeDtypeStruct((frames, positions), F32)),
        in_specs=[vmem] * 5,
        out_specs=(vmem,) * 3,
        scratch_shapes=[
            pltpu.VMEM((frames, width), F32),
            pltpu.VMEM((tiles, positions, 128), F32),
            pltpu.VMEM((positions, width), F32),
            pltpu.VMEM((positions, 128), F32),
            pltpu.VMEM((share // 128, width, 128), F32),
            pltpu.VMEM((share, width), BF16),
            pltpu.VMEM((wide, width), BF16),
            pltpu.VMEM((wide, width), BF16),
            pltpu.VMEM((share // CHUNKS, wide), F32),
            pltpu.VMEM((share // CHUNKS, wide), F32),
            pltpu.VMEM((1, wide), F32),
            pltpu.VMEM((1, wide), F32),
            pltpu.VMEM((1, wide), F32),
            pltpu.VMEM((1, wide), F32),
        ],
        compiler_params=pltpu.CompilerParams(vmem_limit_bytes=48 << 20),
        cost_estimate=pl.CostEstimate(flops=flops, bytes_accessed=2 << 20, transcendentals=0),
        name="joint",
    )(enc, own, own_pred, mine, theirs)


def tree(combine, terms):
    while len(terms) > 1:
        pairs = [combine(a, b) for a, b in zip(terms[::2], terms[1::2])]
        terms = pairs + terms[len(terms) - len(terms) % 2:]
    return terms[0]


def log_sum(terms):
    if len(terms) == 1:
        return terms[0]
    if len(terms) == 2:
        gap = jnp.minimum(*terms) - jnp.maximum(*terms)
        return jnp.maximum(*terms) + jnp.log(1.0 + jnp.exp(gap))
    top = tree(jnp.maximum, terms)
    return top + jnp.log(tree(jnp.add, [jnp.exp(term - top) for term in terms]))


def strips_of(values):
    return [values[:, start:start + 128] for start in range(0, values.shape[1], 128)]


def merge(strips, crossed, step):
    parts = [jnp.where(crossed, strips[(p - step) % len(strips)], strips[p]) for p in range(len(strips))]
    return jnp.concatenate(parts, axis=1)


def shift_lanes(values, by):
    if by == 0:
        return values
    lane = lax.broadcasted_iota(jnp.int32, (values.shape[0], 128), 1)
    turned = [pltpu.roll(strip, by % 128, 1) for strip in strips_of(values)]
    return merge(turned, lane < by, 1) if by > 0 else merge(turned, lane >= 128 + by, -1)


def compose(first, then):
    terms = []
    for count in range(len(first) + len(then) - 1):
        parts = [
            then[late] + shift_lanes(first[count - late], late)
            for late in range(len(then))
            if 0 <= count - late < len(first)
        ]
        terms.append(log_sum(parts))
    return terms


def shear(values, lead):
    rows = values.shape[0]
    lanes = lax.broadcasted_iota(jnp.int32, values.shape, 1)
    if lead:
        values = pltpu.roll(values, rows - lead, 0)
    for bit in (64, 32, 16, 8, 4, 2, 1):
        values = jnp.where((lanes & bit) != 0, pltpu.roll(values, bit, 0), values)
    return values


def lattice_kernel(
    frame_len_ref, label_len_ref, grid_ref, loss_ref, blank_ref, label_ref, stay, move, ahead, back, ahead_far, back_far
):
    blocks, _, frames_dev, positions = grid_ref.shape
    frames = blocks * frames_dev
    strips, diagonals, _ = stay.shape
    lanes_all = 128 * strips
    flen = frame_len_ref[0]
    ulen = label_len_ref[0]
    mine, held = lax.axis_index("label"), blank_ref.shape[1]
    for which, ref in enumerate((blank_ref, label_ref)):
        rows = grid_ref[lax.axis_index("tm"), which]
        own = rows[:, :held]
        for index in range(1, LABEL_WAYS):
            own = jnp.where(mine == index, rows[:, index * held:(index + 1) * held], own)
        ref[...] = own
    spare = jnp.full((frames, lanes_all - positions), NEG, F32)
    tall = frames + 128
    pad = jnp.full((tall - frames, 128), NEG, F32)

    def whole(which):
        rows = jnp.concatenate([grid_ref[block, which] for block in range(blocks)], axis=0)
        return jnp.concatenate([rows, spare], axis=1)

    blank = whole(0)
    label = shift_lanes(whole(1), 1)
    stay[...] = jnp.full(stay.shape, NEG, F32)
    move[...] = jnp.full(move.shape, NEG, F32)
    for part in range(strips):
        start = 128 * part
        rows = min(tall, diagonals - start)
        for source, out, lead in ((blank, stay, 0), (label, move, 1)):
            strip = jnp.concatenate([source[:, start:start + 128], pad], axis=0)
            out[part, start:start + rows, :] = shear(strip, lead)[:rows]

    depth = SIDE * SPAN
    for group in range(diagonals // depth):
        base = group * depth
        live = [p for p in range(strips) if 128 * p <= base + depth and base < 128 * p + 128 + frames]
        first, count_live = live[0], len(live)
        row = lax.broadcasted_iota(jnp.int32, (SIDE, 128 * count_live), 0)
        lane = lax.broadcasted_iota(jnp.int32, (SIDE, 128 * count_live), 1) + 128 * first
        in_row = lane < positions
        moves_in = in_row & (lane > 0)
        rest = jnp.where(lane == ulen, 0.0, NEG)
        steps = []
        for step in range(SPAN):
            time = base + row * SPAN + step - lane
            at = pl.ds(base + step, SIDE, stride=SPAN)
            held = jnp.concatenate([stay[part, at, :] for part in live], axis=1)
            moved = jnp.concatenate([move[part, at, :] for part in live], axis=1)
            held = jnp.where(in_row & (time < flen), held, rest)
            moved = jnp.where(moves_in & (time + 1 < flen), moved, NEG)
            steps.append([held, moved])
        while len(steps) > 1:
            steps = [compose(steps[i], steps[i + 1]) for i in range(0, len(steps), 2)]
        at = group * SIDE
        for count, values in enumerate(steps[0]):
            moved = shift_lanes(values, -count)
            for part in range(strips):
                if part in live:
                    strip = slice(128 * (part - first), 128 * (part - first) + 128)
                    forth, from_back = values[:, strip], moved[:, strip]
                else:
                    forth = jnp.full((SIDE, 128), NEG, F32)
                    if count == 0:
                        lane = lax.broadcasted_iota(jnp.int32, (SIDE, 128), 1) + 128 * part
                        forth = jnp.where(lane == ulen, 0.0, NEG)
                    from_back = forth
                if count < SPAN:
                    ahead[part, pl.ds(at * SPAN + count, SIDE, stride=SPAN), :] = forth
                    back[part, pl.ds(at * SPAN + SPAN - 1 - count, SIDE, stride=SPAN), :] = from_back
                else:
                    ahead_far[at:at + SIDE, 128 * part:128 * part + 128] = forth
                    back_far[at:at + SIDE, 128 * part:128 * part + 128] = from_back

    spans = diagonals // SPAN
    place = lax.broadcasted_iota(jnp.int32, (1, lanes_all), 1)

    def advance(state, step, table, far, block):
        rows = pl.ds(pl.multiple_of(block * SPAN, SPAN), SPAN)
        weights = jnp.concatenate([table[part, rows, :] for part in range(strips)], axis=1)
        first = 0 if step > 0 else 128 - SPAN + 1
        turned = [
            pltpu.roll(jnp.broadcast_to(strip, (SPAN, 128)), first, 1, stride=1, stride_axis=0)
            for strip in strips_of(state)
        ]
        lane = lax.broadcasted_iota(jnp.int32, (SPAN, 128), 1)
        row = lax.broadcasted_iota(jnp.int32, (SPAN, 128), 0)
        crossed = lane < row if step > 0 else lane >= first + row
        near = weights + merge(turned, crossed, step)
        last = far[pl.ds(block, 1), :] + shift_lanes(state, step * SPAN)
        top = jnp.maximum(jnp.max(near, axis=0, keepdims=True), last)
        total = jnp.sum(jnp.exp(near - top), axis=0, keepdims=True) + jnp.exp(last - top)
        return top + jnp.log(total)

    def sweep(index, carry):
        alpha, beta = carry
        alpha = advance(alpha, 1, ahead, ahead_far, index)
        beta = advance(beta, -1, back, back_far, spans - 1 - index)
        return alpha, beta

    alpha = jnp.where(place == 0, 0.0, NEG)
    beta = jnp.where(place == ulen, 0.0, NEG)
    alpha, beta = lax.fori_loop(0, spans // 2, sweep, (alpha, beta))
    both = alpha + beta
    top = jnp.max(both, axis=1, keepdims=True)
    value = top + jnp.log(jnp.sum(jnp.exp(both - top), axis=1, keepdims=True))
    loss_ref[...] = -value / jnp.full((1, 1), flen, jnp.int32).astype(F32)


def lattice_loss(frame_len, label_len, grid):
    blocks, _, frames_dev, positions = grid.shape
    lanes = -(-positions // 128) * 128
    diagonals = -(-(blocks * frames_dev + positions) // (SIDE * SPAN)) * SIDE * SPAN
    assert (diagonals // SPAN) % 2 == 0
    strip = pltpu.VMEM((lanes // 128, diagonals, 128), F32)
    block = jax.ShapeDtypeStruct((frames_dev, positions // LABEL_WAYS), F32)
    table = pltpu.VMEM((lanes // 128, diagonals, 128), F32)
    far = pltpu.VMEM((diagonals // SPAN, lanes), F32)
    vmem = pl.BlockSpec(memory_space=pltpu.VMEM)
    smem = pl.BlockSpec(memory_space=pltpu.SMEM)
    return pl.pallas_call(
        lattice_kernel,
        out_shape=(jax.ShapeDtypeStruct((1, 1), F32), block, block),
        in_specs=[smem, smem, vmem],
        out_specs=(vmem,) * 3,
        scratch_shapes=[
            strip,
            strip,
            table,
            table,
            far,
            far,
        ],
        compiler_params=pltpu.CompilerParams(vmem_limit_bytes=40 << 20),
        name="lattice",
    )(frame_len, label_len, grid)


def around(array, axis):
    size = lax.axis_size(axis)
    moved = [
        lax.ppermute(array, axis, [(i, (i + by) % size) for i in range(size)])
        for by in range(1, size)
    ]
    return [array] + moved


def both_ways(array, axis):
    ways, cores = lax.axis_size(axis), lax.axis_size("tm")
    axes = ("batch", "tm") if axis == "batch" else ("tm", "label")

    def device(way, at):
        return way % ways * cores + at if axis == "batch" else at * ways + way % ways

    near, opposite = [], []
    for way in range(ways):
        for at in range(cores):
            near.append((device(way, at), device(way + (1 if at % 2 == 0 else -1), at)))
            opposite.append((device(way, at), device(way + 2, at)))
    some = array.shape[0] // 2
    half = lax.dynamic_slice_in_dim(array, lax.axis_index("tm") % 2 * some, some, axis=0)
    return lax.ppermute(array, axes, near), lax.ppermute(half, axes, opposite)


def shards(enc_joint, pred_joint, out_weight, labels, frame_len, label_len):
    mine = lax.axis_index("label")
    own, own_pred = pack(out_weight, pred_joint[0], labels)
    with jax.named_scope("gather_weight"):
        own = lax.all_gather(own, "tm", axis=0, tiled=False)
    with jax.named_scope("fetch"):
        from_others = jnp.concatenate([*both_ways(own, "batch"), *both_ways(own_pred, "label")], axis=0)
        swap = [(i, i ^ 1) for i in range(lax.axis_size("tm"))]
        theirs = lax.ppermute(from_others, "tm", swap)
    lse, blank, picked = joint_terms(enc_joint[0], own, own_pred, from_others, theirs)
    with jax.named_scope("combine_vocab"):
        blank = jnp.where(mine == 0, blank, 0.0)
        parts = jnp.stack([lse.reshape(picked.shape), blank.reshape(picked.shape), picked])
        parts = around(parts, "label")

        def merge_parts(one, two):
            return jnp.logaddexp(one[0], two[0]), one[1] + two[1], one[2] + two[2]

        here = lax.optimization_barrier(merge_parts(parts[0], parts[2]))
        norm, log_blank, log_label = merge_parts(here, merge_parts(parts[1], parts[3]))
        log_blank, log_label = log_blank - norm, log_label - norm
    with jax.named_scope("gather_grid"):
        grid = lax.all_gather(jnp.stack([log_blank, log_label]), "tm", axis=0, tiled=False)
    loss, out_blank, out_label = lattice_loss(frame_len, label_len, grid)
    return out_blank[None], out_label[None], loss.reshape(1)


def solution(mesh):
    return jax.shard_map(
        shards,
        mesh=mesh,
        in_specs=(
            P("batch", "tm", None),
            P("batch", "label", None),
            P("batch", "tm"),
            P("batch", "label"),
            P("batch"),
            P("batch"),
        ),
        out_specs=(P("batch", "tm", "label"), P("batch", "tm", "label"), P("batch")),
        check_vma=False,
    )
```

```python
import functools

import jax
import jax.numpy as jnp
from jax import lax
from jax.experimental import pallas as pl
from jax.experimental.pallas import tpu as pltpu
from jax.sharding import PartitionSpec as P

NEG = -1e30
F32 = jnp.float32
BF16 = jnp.bfloat16
SPAN = 16
SIDE = 8
GROUP = 4
CHUNKS = 2
LABEL_WAYS = 4
BATCH_WAYS = 4


def pack_kernel(weight_ref, pred_ref, labels_ref, block_ref, packed_ref):
    mine, odd_block = lax.axis_index("label"), lax.rem(lax.axis_index("tm"), 2) == 1
    tiles, positions, _ = packed_ref.shape
    rows = block_ref.shape[0]
    lane = lax.broadcasted_iota(jnp.int32, (rows, 128), 1)
    values = jnp.where(mine < 2, weight_ref[:, :128].astype(F32), weight_ref[:, 128:].astype(F32))
    left = jnp.where(odd_block, values[rows:], values[:rows])
    right = jnp.where(odd_block, values[:rows], values[rows:])
    second = lax.rem(mine, 2) == 1
    left = jnp.where(second, pltpu.roll(left, 64, 1), left)
    right = jnp.where(second, right, pltpu.roll(right, 64, 1))
    block_ref[...] = jnp.where(lane < 64, left, right).astype(BF16)
    for tile in range(tiles - 1):
        packed_ref[tile] = pred_ref[:, 128 * tile:128 * tile + 128]
    labels = jnp.broadcast_to(labels_ref[...], (positions, positions))
    across = lax.broadcasted_iota(jnp.int32, (positions, positions), 0)
    along = lax.broadcasted_iota(jnp.int32, (positions, positions), 1)
    own = jnp.where(across == along, labels, 0)
    high = jnp.sum((own >> 6).astype(F32), axis=1, keepdims=True)
    low = jnp.sum((own & 63).astype(F32), axis=1, keepdims=True)
    lane = lax.broadcasted_iota(jnp.int32, (positions, 128), 1)
    packed_ref[tiles - 1] = jnp.where(lane == 0, high, jnp.where(lane == 1, low, 0.0)).astype(BF16)


def pack(weight, pred, labels):
    positions, width = pred.shape
    vmem = pl.BlockSpec(memory_space=pltpu.VMEM)
    return pl.pallas_call(
        pack_kernel,
        out_shape=(
            jax.ShapeDtypeStruct((weight.shape[0] // 2, 128), BF16),
            jax.ShapeDtypeStruct((width // 128 + 1, positions, 128), BF16),
        ),
        in_specs=[vmem] * 3,
        out_specs=(vmem, vmem),
        name="pack",
    )(weight, pred, labels)


def joint_kernel(
    enc_ref, own_ref, own_pred_ref, near_mine_ref, mine_ref, near_theirs_ref, theirs_ref,
    lse_ref, blank_ref, picked_ref,
    enc, pred, chosen, picks, columns_first, weight, hidden_a, hidden_b, logits_a, logits_b, top, total, top_a, top_b,
):
    mine, batch, core = lax.axis_index("label"), lax.axis_index("batch"), lax.rem(lax.axis_index("tm"), 2)
    frames, width = enc_ref.shape
    tiles, positions, _ = pred.shape
    share = weight.shape[0]
    chunk = share // CHUNKS
    enc[...] = enc_ref[...].astype(F32)
    blocks, half_rows, _ = own_ref.shape
    some = blocks // 2
    lane = lax.broadcasted_iota(jnp.int32, (half_rows, 128), 1)

    def put_rows(ref, start, count, source, first_pair):
        at = pl.multiple_of(source * 2 * half_rows, 8)
        for pair in range(count // 2):
            left = ref[start + 2 * pair].astype(F32)
            right = ref[start + 2 * pair + 1].astype(F32)
            columns_first[first_pair + pair, pl.ds(at, half_rows), :] = jnp.where(lane < 64, left, right)
            columns_first[first_pair + pair, pl.ds(at + half_rows, half_rows), :] = jnp.where(lane < 64, right, left)

    def put_positions(ref, start, count, source, first):
        at = pl.multiple_of(source * half_rows, 8)
        for index in range(count):
            pred[first + index, pl.ds(at, half_rows), :] = ref[start + index].astype(F32)

    def wrap(value, ways):
        return lax.rem(value + ways, ways)

    put_rows(own_ref, 0, blocks, batch, 0)
    put_positions(own_pred_ref, 0, tiles, mine, 0)
    for near, ref, side in ((near_mine_ref, mine_ref, core), (near_theirs_ref, theirs_ref, 1 - core)):
        step = 2 * side - 1
        put_rows(near, 0, blocks, wrap(batch + step, BATCH_WAYS), 0)
        put_rows(ref, 0, some, wrap(batch + 2, BATCH_WAYS), side * (some // 2))
        put_positions(ref, some, tiles, wrap(mine + step, LABEL_WAYS), 0)
        put_positions(ref, some + tiles, tiles // 2, wrap(mine + 2, LABEL_WAYS), side * (tiles // 2))
    depth = lax.broadcasted_iota(jnp.int32, (128, width), 1)
    upper = lax.rem(depth, 2 * half_rows) < half_rows
    for tile in range(share // 128):
        turned = columns_first[tile].T
        swapped = jnp.concatenate([turned[64:], turned[:64]], axis=0)
        weight[128 * tile:128 * tile + 128, :] = jnp.where(upper, turned, swapped).astype(BF16)

    digits = pred[tiles - 1]
    high = digits[:, 0:1].astype(jnp.int32)
    low = digits[:, 1:2].astype(jnp.int32)
    spot = jnp.where((high & 3) == mine, (high >> 2) * 64 + low, -1)
    columns = lax.broadcasted_iota(jnp.int32, (positions, share), 1)
    one_hot = (columns == spot).astype(F32).astype(BF16)
    chosen[...] = jnp.dot(one_hot, weight[...], preferred_element_type=F32)
    picks[...] = jnp.zeros_like(picks)
    lanes = lax.broadcasted_iota(jnp.int32, picks.shape, 1)

    def make_hidden(frame, part, out):
        rows = slice(part * positions, (part + 1) * positions)
        picked = jnp.zeros((positions, 128), F32)
        frame_row = enc[pl.ds(frame, 1), :]
        for tile in range(tiles - 1):
            strip = slice(128 * tile, 128 * tile + 128)
            rounded = jnp.tanh(pred[tile] + frame_row[:, strip]).astype(BF16)
            out[rows, strip] = rounded
            picked = picked + rounded.astype(F32) * chosen[:, strip]
        picked = jnp.sum(picked, axis=1, keepdims=True)
        picks[...] = jnp.where(lanes == frame, picked, picks[...])

    def multiply(part, hidden, out, chunk_top):
        acc = lax.dot_general(
            weight[part * chunk:(part + 1) * chunk, :], hidden[...],
            (((1,), (1,)), ((), ())), preferred_element_type=F32,
        )
        out[...] = acc
        chunk_top[...] = jnp.max(acc, axis=0, keepdims=True)

    def gather_terms(part, group, logits, chunk_top):
        values = logits[...]
        high = chunk_top[...]
        if part == 0:
            blank_ref[pl.ds(group, 1), :] = logits[0:1, :]
            total[...] = jnp.sum(jnp.exp(values - high), axis=0, keepdims=True)
            top[...] = high
        else:
            high = jnp.maximum(high, top[...])
            total[...] = total[...] * jnp.exp(top[...] - high) + jnp.sum(
                jnp.exp(values - high), axis=0, keepdims=True
            )
            top[...] = high
        if part == CHUNKS - 1:
            lse_ref[pl.ds(group, 1), :] = top[...] + jnp.log(total[...])

    groups = frames // GROUP
    for part in range(GROUP):
        make_hidden(part, part, hidden_a)
    logits_b[...] = jnp.zeros_like(logits_b)
    top[...] = jnp.zeros_like(top)
    top_b[...] = jnp.zeros_like(top)
    total[...] = jnp.ones_like(total)
    each = GROUP // CHUNKS

    def half(group, now, later):
        for part in range(CHUNKS):
            fresh, old = (logits_a, logits_b) if part % 2 == 0 else (logits_b, logits_a)
            fresh_top, old_top = (top_a, top_b) if part % 2 == 0 else (top_b, top_a)
            multiply(part, now, fresh, fresh_top)
            for which in range(part * each, (part + 1) * each):
                make_hidden(jnp.minimum(group + 1, groups - 1) * GROUP + which, which, later)
            if part == 0:
                gather_terms(CHUNKS - 1, jnp.maximum(group - 1, 0), old, old_top)
            else:
                gather_terms(part - 1, group, old, old_top)

    def step(pair, carry):
        half(2 * pair, hidden_a, hidden_b)
        half(2 * pair + 1, hidden_b, hidden_a)
        return carry

    lax.fori_loop(0, groups // 2, step, 0)
    gather_terms(CHUNKS - 1, groups - 1, logits_b, top_b)
    picked_ref[...] = picks[...].T[:frames, :]


def joint_terms(enc, own, own_pred, near_mine, mine, near_theirs, theirs):
    frames, width = enc.shape
    tiles = own_pred.shape[0]
    positions = LABEL_WAYS * own_pred.shape[1]
    share = 64 * own.shape[0]
    wide = GROUP * positions
    grouped = jax.ShapeDtypeStruct((frames // GROUP, wide), F32)
    vmem = pl.BlockSpec(memory_space=pltpu.VMEM)
    smem = pl.BlockSpec(memory_space=pltpu.SMEM)
    flops = 2 * frames * positions * width * share
    return pl.pallas_call(
        joint_kernel,
        out_shape=(grouped, grouped, jax.ShapeDtypeStruct((frames, positions), F32)),
        in_specs=[vmem] * 7,
        out_specs=(vmem,) * 3,
        scratch_shapes=[
            pltpu.VMEM((frames, width), F32),
            pltpu.VMEM((tiles, positions, 128), F32),
            pltpu.VMEM((positions, width), F32),
            pltpu.VMEM((positions, 128), F32),
            pltpu.VMEM((share // 128, width, 128), F32),
            pltpu.VMEM((share, width), BF16),
            pltpu.VMEM((wide, width), BF16),
            pltpu.VMEM((wide, width), BF16),
            pltpu.VMEM((share // CHUNKS, wide), F32),
            pltpu.VMEM((share // CHUNKS, wide), F32),
            pltpu.VMEM((1, wide), F32),
            pltpu.VMEM((1, wide), F32),
            pltpu.VMEM((1, wide), F32),
            pltpu.VMEM((1, wide), F32),
        ],
        compiler_params=pltpu.CompilerParams(vmem_limit_bytes=48 << 20),
        cost_estimate=pl.CostEstimate(flops=flops, bytes_accessed=2 << 20, transcendentals=0),
        name="joint",
    )(enc, own, own_pred, near_mine, mine, near_theirs, theirs)


def tree(combine, terms):
    while len(terms) > 1:
        pairs = [combine(a, b) for a, b in zip(terms[::2], terms[1::2])]
        terms = pairs + terms[len(terms) - len(terms) % 2:]
    return terms[0]


def log_sum(terms):
    if len(terms) == 1:
        return terms[0]
    if len(terms) == 2:
        gap = jnp.minimum(*terms) - jnp.maximum(*terms)
        return jnp.maximum(*terms) + jnp.log(1.0 + jnp.exp(gap))
    top = tree(jnp.maximum, terms)
    return top + jnp.log(tree(jnp.add, [jnp.exp(term - top) for term in terms]))


def strips_of(values):
    return [values[:, start:start + 128] for start in range(0, values.shape[1], 128)]


def merge(strips, crossed, step):
    parts = [jnp.where(crossed, strips[(p - step) % len(strips)], strips[p]) for p in range(len(strips))]
    return jnp.concatenate(parts, axis=1)


def shift_lanes(values, by):
    if by == 0:
        return values
    lane = lax.broadcasted_iota(jnp.int32, (values.shape[0], 128), 1)
    turned = [pltpu.roll(strip, by % 128, 1) for strip in strips_of(values)]
    return merge(turned, lane < by, 1) if by > 0 else merge(turned, lane >= 128 + by, -1)


def compose(first, then):
    terms = []
    for count in range(len(first) + len(then) - 1):
        parts = [
            then[late] + shift_lanes(first[count - late], late)
            for late in range(len(then))
            if 0 <= count - late < len(first)
        ]
        terms.append(log_sum(parts))
    return terms


def shear(values, lead):
    rows = values.shape[0]
    lanes = lax.broadcasted_iota(jnp.int32, values.shape, 1)
    if lead:
        values = pltpu.roll(values, rows - lead, 0)
    for bit in (64, 32, 16, 8, 4, 2, 1):
        values = jnp.where((lanes & bit) != 0, pltpu.roll(values, bit, 0), values)
    return values


def lattice_kernel(
    frame_len_ref, label_len_ref, grid_ref, loss_ref, blank_ref, label_ref, stay, move, ahead, back, ahead_far, back_far
):
    blocks, _, frames_dev, positions = grid_ref.shape
    frames = blocks * frames_dev
    strips, diagonals, _ = stay.shape
    lanes_all = 128 * strips
    flen = frame_len_ref[0]
    ulen = label_len_ref[0]
    mine, held = lax.axis_index("label"), blank_ref.shape[1]
    for which, ref in enumerate((blank_ref, label_ref)):
        rows = grid_ref[lax.axis_index("tm"), which]
        own = rows[:, :held]
        for index in range(1, LABEL_WAYS):
            own = jnp.where(mine == index, rows[:, index * held:(index + 1) * held], own)
        ref[...] = own
    spare = jnp.full((frames, lanes_all - positions), NEG, F32)
    tall = frames + 128
    pad = jnp.full((tall - frames, 128), NEG, F32)

    def whole(which):
        rows = jnp.concatenate([grid_ref[block, which] for block in range(blocks)], axis=0)
        return jnp.concatenate([rows, spare], axis=1)

    blank = whole(0)
    label = shift_lanes(whole(1), 1)
    stay[...] = jnp.full(stay.shape, NEG, F32)
    move[...] = jnp.full(move.shape, NEG, F32)
    for part in range(strips):
        start = 128 * part
        rows = min(tall, diagonals - start)
        for source, out, lead in ((blank, stay, 0), (label, move, 1)):
            strip = jnp.concatenate([source[:, start:start + 128], pad], axis=0)
            out[part, start:start + rows, :] = shear(strip, lead)[:rows]

    depth = SIDE * SPAN
    for group in range(diagonals // depth):
        base = group * depth
        live = [p for p in range(strips) if 128 * p <= base + depth and base < 128 * p + 128 + frames]
        first, count_live = live[0], len(live)
        row = lax.broadcasted_iota(jnp.int32, (SIDE, 128 * count_live), 0)
        lane = lax.broadcasted_iota(jnp.int32, (SIDE, 128 * count_live), 1) + 128 * first
        in_row = lane < positions
        moves_in = in_row & (lane > 0)
        rest = jnp.where(lane == ulen, 0.0, NEG)
        steps = []
        for step in range(SPAN):
            time = base + row * SPAN + step - lane
            at = pl.ds(base + step, SIDE, stride=SPAN)
            held = jnp.concatenate([stay[part, at, :] for part in live], axis=1)
            moved = jnp.concatenate([move[part, at, :] for part in live], axis=1)
            held = jnp.where(in_row & (time < flen), held, rest)
            moved = jnp.where(moves_in & (time + 1 < flen), moved, NEG)
            steps.append([held, moved])
        while len(steps) > 1:
            steps = [compose(steps[i], steps[i + 1]) for i in range(0, len(steps), 2)]
        at = group * SIDE
        for count, values in enumerate(steps[0]):
            moved = shift_lanes(values, -count)
            for part in range(strips):
                if part in live:
                    strip = slice(128 * (part - first), 128 * (part - first) + 128)
                    forth, from_back = values[:, strip], moved[:, strip]
                else:
                    forth = jnp.full((SIDE, 128), NEG, F32)
                    if count == 0:
                        lane = lax.broadcasted_iota(jnp.int32, (SIDE, 128), 1) + 128 * part
                        forth = jnp.where(lane == ulen, 0.0, NEG)
                    from_back = forth
                if count < SPAN:
                    ahead[part, pl.ds(at * SPAN + count, SIDE, stride=SPAN), :] = forth
                    back[part, pl.ds(at * SPAN + SPAN - 1 - count, SIDE, stride=SPAN), :] = from_back
                else:
                    ahead_far[at:at + SIDE, 128 * part:128 * part + 128] = forth
                    back_far[at:at + SIDE, 128 * part:128 * part + 128] = from_back

    spans = diagonals // SPAN
    place = lax.broadcasted_iota(jnp.int32, (1, lanes_all), 1)

    def advance(state, step, table, far, block):
        rows = pl.ds(pl.multiple_of(block * SPAN, SPAN), SPAN)
        weights = jnp.concatenate([table[part, rows, :] for part in range(strips)], axis=1)
        first = 0 if step > 0 else 128 - SPAN + 1
        turned = [
            pltpu.roll(jnp.broadcast_to(strip, (SPAN, 128)), first, 1, stride=1, stride_axis=0)
            for strip in strips_of(state)
        ]
        lane = lax.broadcasted_iota(jnp.int32, (SPAN, 128), 1)
        row = lax.broadcasted_iota(jnp.int32, (SPAN, 128), 0)
        crossed = lane < row if step > 0 else lane >= first + row
        near = weights + merge(turned, crossed, step)
        last = far[pl.ds(block, 1), :] + shift_lanes(state, step * SPAN)
        top = jnp.maximum(jnp.max(near, axis=0, keepdims=True), last)
        total = jnp.sum(jnp.exp(near - top), axis=0, keepdims=True) + jnp.exp(last - top)
        return top + jnp.log(total)

    def sweep(index, carry):
        alpha, beta = carry
        alpha = advance(alpha, 1, ahead, ahead_far, index)
        beta = advance(beta, -1, back, back_far, spans - 1 - index)
        return alpha, beta

    alpha = jnp.where(place == 0, 0.0, NEG)
    beta = jnp.where(place == ulen, 0.0, NEG)
    alpha, beta = lax.fori_loop(0, spans // 2, sweep, (alpha, beta))
    both = alpha + beta
    top = jnp.max(both, axis=1, keepdims=True)
    value = top + jnp.log(jnp.sum(jnp.exp(both - top), axis=1, keepdims=True))
    loss_ref[...] = -value / jnp.full((1, 1), flen, jnp.int32).astype(F32)


def lattice_loss(frame_len, label_len, grid):
    blocks, _, frames_dev, positions = grid.shape
    lanes = -(-positions // 128) * 128
    diagonals = -(-(blocks * frames_dev + positions) // (SIDE * SPAN)) * SIDE * SPAN
    assert (diagonals // SPAN) % 2 == 0
    strip = pltpu.VMEM((lanes // 128, diagonals, 128), F32)
    block = jax.ShapeDtypeStruct((frames_dev, positions // LABEL_WAYS), F32)
    table = pltpu.VMEM((lanes // 128, diagonals, 128), F32)
    far = pltpu.VMEM((diagonals // SPAN, lanes), F32)
    vmem = pl.BlockSpec(memory_space=pltpu.VMEM)
    smem = pl.BlockSpec(memory_space=pltpu.SMEM)
    return pl.pallas_call(
        lattice_kernel,
        out_shape=(jax.ShapeDtypeStruct((1, 1), F32), block, block),
        in_specs=[smem, smem, vmem],
        out_specs=(vmem,) * 3,
        scratch_shapes=[
            strip,
            strip,
            table,
            table,
            far,
            far,
        ],
        compiler_params=pltpu.CompilerParams(vmem_limit_bytes=40 << 20),
        name="lattice",
    )(frame_len, label_len, grid)


def around(array, axis):
    size = lax.axis_size(axis)
    moved = [
        lax.ppermute(array, axis, [(i, (i + by) % size) for i in range(size)])
        for by in range(1, size)
    ]
    return [array] + moved


def both_ways(array, axis):
    ways, cores = lax.axis_size(axis), lax.axis_size("tm")
    axes = ("batch", "tm") if axis == "batch" else ("tm", "label")

    def device(way, at):
        return way % ways * cores + at if axis == "batch" else at * ways + way % ways

    near, opposite = [], []
    for way in range(ways):
        for at in range(cores):
            near.append((device(way, at), device(way + (1 if at % 2 == 0 else -1), at)))
            opposite.append((device(way, at), device(way + 2, at)))
    some = array.shape[0] // 2
    half = lax.dynamic_slice_in_dim(array, lax.axis_index("tm") % 2 * some, some, axis=0)
    return lax.ppermute(array, axes, near), lax.ppermute(half, axes, opposite)


def shards(enc_joint, pred_joint, out_weight, labels, frame_len, label_len):
    mine = lax.axis_index("label")
    own, own_pred = pack(out_weight, pred_joint[0], labels)
    with jax.named_scope("gather_weight"):
        own = lax.all_gather(own, "tm", axis=0, tiled=False)
    with jax.named_scope("fetch"):
        near, opposite = both_ways(own, "batch")
        rest = jnp.concatenate([opposite, *both_ways(own_pred, "label")], axis=0)
        swap = [(i, i ^ 1) for i in range(lax.axis_size("tm"))]
        near_theirs = lax.ppermute(near, "tm", swap)
        theirs = lax.ppermute(rest, "tm", swap)
    lse, blank, picked = joint_terms(enc_joint[0], own, own_pred, near, rest, near_theirs, theirs)
    with jax.named_scope("combine_vocab"):
        blank = jnp.where(mine == 0, blank, 0.0)
        parts = jnp.stack([lse.reshape(picked.shape), blank.reshape(picked.shape), picked])
        parts = around(parts, "label")

        def merge_parts(one, two):
            return jnp.logaddexp(one[0], two[0]), one[1] + two[1], one[2] + two[2]

        here = lax.optimization_barrier(merge_parts(parts[0], parts[2]))
        norm, log_blank, log_label = merge_parts(here, merge_parts(parts[1], parts[3]))
        log_blank, log_label = log_blank - norm, log_label - norm
    with jax.named_scope("gather_grid"):
        grid = lax.all_gather(jnp.stack([log_blank, log_label]), "tm", axis=0, tiled=False)
    loss, out_blank, out_label = lattice_loss(frame_len, label_len, grid)
    return out_blank[None], out_label[None], loss.reshape(1)


def solution(mesh):
    return jax.shard_map(
        shards,
        mesh=mesh,
        in_specs=(
            P("batch", "tm", None),
            P("batch", "label", None),
            P("batch", "tm"),
            P("batch", "label"),
            P("batch"),
            P("batch"),
        ),
        out_specs=(P("batch", "tm", "label"), P("batch", "tm", "label"), P("batch")),
        check_vma=False,
    )
```

```python
import functools

import jax
import jax.numpy as jnp
from jax import lax
from jax.experimental import pallas as pl
from jax.experimental.pallas import tpu as pltpu
from jax.sharding import PartitionSpec as P

NEG = -1e30
F32 = jnp.float32
BF16 = jnp.bfloat16
SPAN = 16
SIDE = 8
GROUP = 4
CHUNKS = 2
LABEL_WAYS = 4
BATCH_WAYS = 4


def pack_kernel(weight_ref, pred_ref, labels_ref, block_ref, packed_ref, half_ref):
    mine, odd_block = lax.axis_index("label"), lax.rem(lax.axis_index("tm"), 2) == 1
    tiles, positions, _ = packed_ref.shape
    rows = block_ref.shape[0]
    lane = lax.broadcasted_iota(jnp.int32, (rows, 128), 1)
    values = jnp.where(mine < 2, weight_ref[:, :128].astype(F32), weight_ref[:, 128:].astype(F32))
    left = jnp.where(odd_block, values[rows:], values[:rows])
    right = jnp.where(odd_block, values[:rows], values[rows:])
    second = lax.rem(mine, 2) == 1
    left = jnp.where(second, pltpu.roll(left, 64, 1), left)
    right = jnp.where(second, right, pltpu.roll(right, 64, 1))
    block_ref[...] = jnp.where(lane < 64, left, right).astype(BF16)
    for tile in range(tiles - 1):
        packed_ref[tile] = pred_ref[:, 128 * tile:128 * tile + 128]
    labels = jnp.broadcast_to(labels_ref[...], (positions, positions))
    across = lax.broadcasted_iota(jnp.int32, (positions, positions), 0)
    along = lax.broadcasted_iota(jnp.int32, (positions, positions), 1)
    own = jnp.where(across == along, labels, 0)
    high = jnp.sum((own >> 6).astype(F32), axis=1, keepdims=True)
    low = jnp.sum((own & 63).astype(F32), axis=1, keepdims=True)
    lane = lax.broadcasted_iota(jnp.int32, (positions, 128), 1)
    packed_ref[tiles - 1] = jnp.where(lane == 0, high, jnp.where(lane == 1, low, 0.0)).astype(BF16)
    some = tiles // 2
    for tile in range(some):
        early, late = packed_ref[tile].astype(F32), packed_ref[some + tile].astype(F32)
        half_ref[tile] = jnp.where(odd_block, late, early).astype(BF16)


def pack(weight, pred, labels):
    positions, width = pred.shape
    vmem = pl.BlockSpec(memory_space=pltpu.VMEM)
    return pl.pallas_call(
        pack_kernel,
        out_shape=(
            jax.ShapeDtypeStruct((weight.shape[0] // 2, 128), BF16),
            jax.ShapeDtypeStruct((width // 128 + 1, positions, 128), BF16),
            jax.ShapeDtypeStruct(((width // 128 + 1) // 2, positions, 128), BF16),
        ),
        in_specs=[vmem] * 3,
        out_specs=(vmem,) * 3,
        name="pack",
    )(weight, pred, labels)


def joint_kernel(
    enc_ref, own_ref, own_pred_ref, near_mine_ref, mine_ref, near_theirs_ref, theirs_ref,
    lse_ref, blank_ref, picked_ref,
    enc, pred, chosen, picks, columns_first, weight, hidden_a, hidden_b, logits_a, logits_b, top, total, top_a, top_b,
):
    mine, batch, core = lax.axis_index("label"), lax.axis_index("batch"), lax.rem(lax.axis_index("tm"), 2)
    frames, width = enc_ref.shape
    tiles, positions, _ = pred.shape
    share = weight.shape[0]
    chunk = share // CHUNKS
    enc[...] = enc_ref[...].astype(F32)
    blocks, half_rows, _ = own_ref.shape
    some = blocks // 2
    lane = lax.broadcasted_iota(jnp.int32, (half_rows, 128), 1)

    def put_rows(ref, start, count, source, first_pair):
        at = pl.multiple_of(source * 2 * half_rows, 8)
        for pair in range(count // 2):
            left = ref[start + 2 * pair].astype(F32)
            right = ref[start + 2 * pair + 1].astype(F32)
            columns_first[first_pair + pair, pl.ds(at, half_rows), :] = jnp.where(lane < 64, left, right)
            columns_first[first_pair + pair, pl.ds(at + half_rows, half_rows), :] = jnp.where(lane < 64, right, left)

    def put_positions(ref, start, count, source, first):
        at = pl.multiple_of(source * half_rows, 8)
        for index in range(count):
            pred[first + index, pl.ds(at, half_rows), :] = ref[start + index].astype(F32)

    def wrap(value, ways):
        return lax.rem(value + ways, ways)

    put_rows(own_ref, 0, blocks, batch, 0)
    put_positions(own_pred_ref, 0, tiles, mine, 0)
    for near, ref, side in ((near_mine_ref, mine_ref, core), (near_theirs_ref, theirs_ref, 1 - core)):
        step = 2 * side - 1
        put_rows(near, 0, blocks, wrap(batch + step, BATCH_WAYS), 0)
        put_rows(ref, 0, some, wrap(batch + 2, BATCH_WAYS), side * (some // 2))
        put_positions(ref, some, tiles, wrap(mine + step, LABEL_WAYS), 0)
        put_positions(ref, some + tiles, tiles // 2, wrap(mine + 2, LABEL_WAYS), side * (tiles // 2))
    depth = lax.broadcasted_iota(jnp.int32, (128, width), 1)
    upper = lax.rem(depth, 2 * half_rows) < half_rows
    for tile in range(share // 128):
        turned = columns_first[tile].T
        swapped = jnp.concatenate([turned[64:], turned[:64]], axis=0)
        weight[128 * tile:128 * tile + 128, :] = jnp.where(upper, turned, swapped).astype(BF16)

    digits = pred[tiles - 1]
    high = digits[:, 0:1].astype(jnp.int32)
    low = digits[:, 1:2].astype(jnp.int32)
    spot = jnp.where((high & 3) == mine, (high >> 2) * 64 + low, -1)
    columns = lax.broadcasted_iota(jnp.int32, (positions, share), 1)
    one_hot = (columns == spot).astype(F32).astype(BF16)
    chosen[...] = jnp.dot(one_hot, weight[...], preferred_element_type=F32)
    picks[...] = jnp.zeros_like(picks)
    lanes = lax.broadcasted_iota(jnp.int32, picks.shape, 1)

    def make_hidden(frame, part, out):
        rows = slice(part * positions, (part + 1) * positions)
        picked = jnp.zeros((positions, 128), F32)
        frame_row = enc[pl.ds(frame, 1), :]
        for tile in range(tiles - 1):
            strip = slice(128 * tile, 128 * tile + 128)
            rounded = jnp.tanh(pred[tile] + frame_row[:, strip]).astype(BF16)
            out[rows, strip] = rounded
            picked = picked + rounded.astype(F32) * chosen[:, strip]
        picked = jnp.sum(picked, axis=1, keepdims=True)
        picks[...] = jnp.where(lanes == frame, picked, picks[...])

    def multiply(part, hidden, out, chunk_top):
        acc = lax.dot_general(
            weight[part * chunk:(part + 1) * chunk, :], hidden[...],
            (((1,), (1,)), ((), ())), preferred_element_type=F32,
        )
        out[...] = acc
        chunk_top[...] = jnp.max(acc, axis=0, keepdims=True)

    def gather_terms(part, group, logits, chunk_top):
        values = logits[...]
        high = chunk_top[...]
        if part == 0:
            blank_ref[pl.ds(group, 1), :] = logits[0:1, :]
            total[...] = jnp.sum(jnp.exp(values - high), axis=0, keepdims=True)
            top[...] = high
        else:
            high = jnp.maximum(high, top[...])
            total[...] = total[...] * jnp.exp(top[...] - high) + jnp.sum(
                jnp.exp(values - high), axis=0, keepdims=True
            )
            top[...] = high
        if part == CHUNKS - 1:
            lse_ref[pl.ds(group, 1), :] = top[...] + jnp.log(total[...])

    groups = frames // GROUP
    for part in range(GROUP):
        make_hidden(part, part, hidden_a)
    logits_b[...] = jnp.zeros_like(logits_b)
    top[...] = jnp.zeros_like(top)
    top_b[...] = jnp.zeros_like(top)
    total[...] = jnp.ones_like(total)
    each = GROUP // CHUNKS

    def half(group, now, later):
        for part in range(CHUNKS):
            fresh, old = (logits_a, logits_b) if part % 2 == 0 else (logits_b, logits_a)
            fresh_top, old_top = (top_a, top_b) if part % 2 == 0 else (top_b, top_a)
            multiply(part, now, fresh, fresh_top)
            for which in range(part * each, (part + 1) * each):
                make_hidden(jnp.minimum(group + 1, groups - 1) * GROUP + which, which, later)
            if part == 0:
                gather_terms(CHUNKS - 1, jnp.maximum(group - 1, 0), old, old_top)
            else:
                gather_terms(part - 1, group, old, old_top)

    def step(pair, carry):
        half(2 * pair, hidden_a, hidden_b)
        half(2 * pair + 1, hidden_b, hidden_a)
        return carry

    lax.fori_loop(0, groups // 2, step, 0)
    gather_terms(CHUNKS - 1, groups - 1, logits_b, top_b)
    picked_ref[...] = picks[...].T[:frames, :]


def joint_terms(enc, own, own_pred, near_mine, mine, near_theirs, theirs):
    frames, width = enc.shape
    tiles = own_pred.shape[0]
    positions = LABEL_WAYS * own_pred.shape[1]
    share = 64 * own.shape[0]
    wide = GROUP * positions
    grouped = jax.ShapeDtypeStruct((frames // GROUP, wide), F32)
    vmem = pl.BlockSpec(memory_space=pltpu.VMEM)
    smem = pl.BlockSpec(memory_space=pltpu.SMEM)
    flops = 2 * frames * positions * width * share
    return pl.pallas_call(
        joint_kernel,
        out_shape=(grouped, grouped, jax.ShapeDtypeStruct((frames, positions), F32)),
        in_specs=[vmem] * 7,
        out_specs=(vmem,) * 3,
        scratch_shapes=[
            pltpu.VMEM((frames, width), F32),
            pltpu.VMEM((tiles, positions, 128), F32),
            pltpu.VMEM((positions, width), F32),
            pltpu.VMEM((positions, 128), F32),
            pltpu.VMEM((share // 128, width, 128), F32),
            pltpu.VMEM((share, width), BF16),
            pltpu.VMEM((wide, width), BF16),
            pltpu.VMEM((wide, width), BF16),
            pltpu.VMEM((share // CHUNKS, wide), F32),
            pltpu.VMEM((share // CHUNKS, wide), F32),
            pltpu.VMEM((1, wide), F32),
            pltpu.VMEM((1, wide), F32),
            pltpu.VMEM((1, wide), F32),
            pltpu.VMEM((1, wide), F32),
        ],
        compiler_params=pltpu.CompilerParams(vmem_limit_bytes=48 << 20),
        cost_estimate=pl.CostEstimate(flops=flops, bytes_accessed=2 << 20, transcendentals=0),
        name="joint",
    )(enc, own, own_pred, near_mine, mine, near_theirs, theirs)


def tree(combine, terms):
    while len(terms) > 1:
        pairs = [combine(a, b) for a, b in zip(terms[::2], terms[1::2])]
        terms = pairs + terms[len(terms) - len(terms) % 2:]
    return terms[0]


def log_sum(terms):
    if len(terms) == 1:
        return terms[0]
    if len(terms) == 2:
        gap = jnp.minimum(*terms) - jnp.maximum(*terms)
        return jnp.maximum(*terms) + jnp.log(1.0 + jnp.exp(gap))
    top = tree(jnp.maximum, terms)
    return top + jnp.log(tree(jnp.add, [jnp.exp(term - top) for term in terms]))


def strips_of(values):
    return [values[:, start:start + 128] for start in range(0, values.shape[1], 128)]


def merge(strips, crossed, step):
    parts = [jnp.where(crossed, strips[(p - step) % len(strips)], strips[p]) for p in range(len(strips))]
    return jnp.concatenate(parts, axis=1)


def shift_lanes(values, by):
    if by == 0:
        return values
    lane = lax.broadcasted_iota(jnp.int32, (values.shape[0], 128), 1)
    turned = [pltpu.roll(strip, by % 128, 1) for strip in strips_of(values)]
    return merge(turned, lane < by, 1) if by > 0 else merge(turned, lane >= 128 + by, -1)


def compose(first, then):
    terms = []
    for count in range(len(first) + len(then) - 1):
        parts = [
            then[late] + shift_lanes(first[count - late], late)
            for late in range(len(then))
            if 0 <= count - late < len(first)
        ]
        terms.append(log_sum(parts))
    return terms


def shear(values, lead):
    rows = values.shape[0]
    lanes = lax.broadcasted_iota(jnp.int32, values.shape, 1)
    if lead:
        values = pltpu.roll(values, rows - lead, 0)
    for bit in (64, 32, 16, 8, 4, 2, 1):
        values = jnp.where((lanes & bit) != 0, pltpu.roll(values, bit, 0), values)
    return values


def lattice_kernel(
    frame_len_ref, label_len_ref, grid_ref, loss_ref, blank_ref, label_ref, stay, move, ahead, back, ahead_far, back_far
):
    blocks, _, frames_dev, positions = grid_ref.shape
    frames = blocks * frames_dev
    strips, diagonals, _ = stay.shape
    lanes_all = 128 * strips
    flen = frame_len_ref[0]
    ulen = label_len_ref[0]
    mine, held = lax.axis_index("label"), blank_ref.shape[1]
    for which, ref in enumerate((blank_ref, label_ref)):
        rows = grid_ref[lax.axis_index("tm"), which]
        own = rows[:, :held]
        for index in range(1, LABEL_WAYS):
            own = jnp.where(mine == index, rows[:, index * held:(index + 1) * held], own)
        ref[...] = own
    spare = jnp.full((frames, lanes_all - positions), NEG, F32)
    tall = frames + 128
    pad = jnp.full((tall - frames, 128), NEG, F32)

    def whole(which):
        rows = jnp.concatenate([grid_ref[block, which] for block in range(blocks)], axis=0)
        return jnp.concatenate([rows, spare], axis=1)

    blank = whole(0)
    label = shift_lanes(whole(1), 1)
    stay[...] = jnp.full(stay.shape, NEG, F32)
    move[...] = jnp.full(move.shape, NEG, F32)
    for part in range(strips):
        start = 128 * part
        rows = min(tall, diagonals - start)
        for source, out, lead in ((blank, stay, 0), (label, move, 1)):
            strip = jnp.concatenate([source[:, start:start + 128], pad], axis=0)
            out[part, start:start + rows, :] = shear(strip, lead)[:rows]

    depth = SIDE * SPAN
    for group in range(diagonals // depth):
        base = group * depth
        live = [p for p in range(strips) if 128 * p <= base + depth and base < 128 * p + 128 + frames]
        first, count_live = live[0], len(live)
        row = lax.broadcasted_iota(jnp.int32, (SIDE, 128 * count_live), 0)
        lane = lax.broadcasted_iota(jnp.int32, (SIDE, 128 * count_live), 1) + 128 * first
        in_row = lane < positions
        moves_in = in_row & (lane > 0)
        rest = jnp.where(lane == ulen, 0.0, NEG)
        steps = []
        for step in range(SPAN):
            time = base + row * SPAN + step - lane
            at = pl.ds(base + step, SIDE, stride=SPAN)
            held = jnp.concatenate([stay[part, at, :] for part in live], axis=1)
            moved = jnp.concatenate([move[part, at, :] for part in live], axis=1)
            held = jnp.where(in_row & (time < flen), held, rest)
            moved = jnp.where(moves_in & (time + 1 < flen), moved, NEG)
            steps.append([held, moved])
        while len(steps) > 1:
            steps = [compose(steps[i], steps[i + 1]) for i in range(0, len(steps), 2)]
        at = group * SIDE
        for count, values in enumerate(steps[0]):
            moved = shift_lanes(values, -count)
            for part in range(strips):
                if part in live:
                    strip = slice(128 * (part - first), 128 * (part - first) + 128)
                    forth, from_back = values[:, strip], moved[:, strip]
                else:
                    forth = jnp.full((SIDE, 128), NEG, F32)
                    if count == 0:
                        lane = lax.broadcasted_iota(jnp.int32, (SIDE, 128), 1) + 128 * part
                        forth = jnp.where(lane == ulen, 0.0, NEG)
                    from_back = forth
                if count < SPAN:
                    ahead[part, pl.ds(at * SPAN + count, SIDE, stride=SPAN), :] = forth
                    back[part, pl.ds(at * SPAN + SPAN - 1 - count, SIDE, stride=SPAN), :] = from_back
                else:
                    ahead_far[at:at + SIDE, 128 * part:128 * part + 128] = forth
                    back_far[at:at + SIDE, 128 * part:128 * part + 128] = from_back

    spans = diagonals // SPAN
    place = lax.broadcasted_iota(jnp.int32, (1, lanes_all), 1)

    def advance(state, step, table, far, block):
        rows = pl.ds(pl.multiple_of(block * SPAN, SPAN), SPAN)
        weights = jnp.concatenate([table[part, rows, :] for part in range(strips)], axis=1)
        first = 0 if step > 0 else 128 - SPAN + 1
        turned = [
            pltpu.roll(jnp.broadcast_to(strip, (SPAN, 128)), first, 1, stride=1, stride_axis=0)
            for strip in strips_of(state)
        ]
        lane = lax.broadcasted_iota(jnp.int32, (SPAN, 128), 1)
        row = lax.broadcasted_iota(jnp.int32, (SPAN, 128), 0)
        crossed = lane < row if step > 0 else lane >= first + row
        near = weights + merge(turned, crossed, step)
        last = far[pl.ds(block, 1), :] + shift_lanes(state, step * SPAN)
        top = jnp.maximum(jnp.max(near, axis=0, keepdims=True), last)
        total = jnp.sum(jnp.exp(near - top), axis=0, keepdims=True) + jnp.exp(last - top)
        return top + jnp.log(total)

    def sweep(index, carry):
        alpha, beta = carry
        alpha = advance(alpha, 1, ahead, ahead_far, index)
        beta = advance(beta, -1, back, back_far, spans - 1 - index)
        return alpha, beta

    alpha = jnp.where(place == 0, 0.0, NEG)
    beta = jnp.where(place == ulen, 0.0, NEG)
    alpha, beta = lax.fori_loop(0, spans // 2, sweep, (alpha, beta))
    both = alpha + beta
    top = jnp.max(both, axis=1, keepdims=True)
    value = top + jnp.log(jnp.sum(jnp.exp(both - top), axis=1, keepdims=True))
    loss_ref[...] = -value / jnp.full((1, 1), flen, jnp.int32).astype(F32)


def lattice_loss(frame_len, label_len, grid):
    blocks, _, frames_dev, positions = grid.shape
    lanes = -(-positions // 128) * 128
    diagonals = -(-(blocks * frames_dev + positions) // (SIDE * SPAN)) * SIDE * SPAN
    assert (diagonals // SPAN) % 2 == 0
    strip = pltpu.VMEM((lanes // 128, diagonals, 128), F32)
    block = jax.ShapeDtypeStruct((frames_dev, positions // LABEL_WAYS), F32)
    table = pltpu.VMEM((lanes // 128, diagonals, 128), F32)
    far = pltpu.VMEM((diagonals // SPAN, lanes), F32)
    vmem = pl.BlockSpec(memory_space=pltpu.VMEM)
    smem = pl.BlockSpec(memory_space=pltpu.SMEM)
    return pl.pallas_call(
        lattice_kernel,
        out_shape=(jax.ShapeDtypeStruct((1, 1), F32), block, block),
        in_specs=[smem, smem, vmem],
        out_specs=(vmem,) * 3,
        scratch_shapes=[
            strip,
            strip,
            table,
            table,
            far,
            far,
        ],
        compiler_params=pltpu.CompilerParams(vmem_limit_bytes=40 << 20),
        name="lattice",
    )(frame_len, label_len, grid)


def around(array, axis):
    size = lax.axis_size(axis)
    moved = [
        lax.ppermute(array, axis, [(i, (i + by) % size) for i in range(size)])
        for by in range(1, size)
    ]
    return [array] + moved


def both_ways(array, axis, half=None):
    ways, cores = lax.axis_size(axis), lax.axis_size("tm")
    axes = ("batch", "tm") if axis == "batch" else ("tm", "label")

    def device(way, at):
        return way % ways * cores + at if axis == "batch" else at * ways + way % ways

    near, opposite = [], []
    for way in range(ways):
        for at in range(cores):
            near.append((device(way, at), device(way + (1 if at % 2 == 0 else -1), at)))
            opposite.append((device(way, at), device(way + 2, at)))
    if half is None:
        some = array.shape[0] // 2
        half = lax.dynamic_slice_in_dim(array, lax.axis_index("tm") % 2 * some, some, axis=0)
    return lax.ppermute(array, axes, near), lax.ppermute(half, axes, opposite)


def shards(enc_joint, pred_joint, out_weight, labels, frame_len, label_len):
    mine = lax.axis_index("label")
    own, own_pred, half_pred = pack(out_weight, pred_joint[0], labels)
    with jax.named_scope("gather_weight"):
        own = lax.all_gather(own, "tm", axis=0, tiled=False)
    with jax.named_scope("fetch"):
        near, opposite = both_ways(own, "batch")
        rest = jnp.concatenate([opposite, *both_ways(own_pred, "label", half_pred)], axis=0)
        swap = [(i, i ^ 1) for i in range(lax.axis_size("tm"))]
        near_theirs = lax.ppermute(near, "tm", swap)
        theirs = lax.ppermute(rest, "tm", swap)
    lse, blank, picked = joint_terms(enc_joint[0], own, own_pred, near, rest, near_theirs, theirs)
    with jax.named_scope("combine_vocab"):
        blank = jnp.where(mine == 0, blank, 0.0)
        parts = jnp.stack([lse.reshape(picked.shape), blank.reshape(picked.shape), picked])
        parts = around(parts, "label")

        def merge_parts(one, two):
            return jnp.logaddexp(one[0], two[0]), one[1] + two[1], one[2] + two[2]

        here = lax.optimization_barrier(merge_parts(parts[0], parts[2]))
        norm, log_blank, log_label = merge_parts(here, merge_parts(parts[1], parts[3]))
        log_blank, log_label = log_blank - norm, log_label - norm
    with jax.named_scope("gather_grid"):
        grid = lax.all_gather(jnp.stack([log_blank, log_label]), "tm", axis=0, tiled=False)
    loss, out_blank, out_label = lattice_loss(frame_len, label_len, grid)
    return out_blank[None], out_label[None], loss.reshape(1)


def solution(mesh):
    return jax.shard_map(
        shards,
        mesh=mesh,
        in_specs=(
            P("batch", "tm", None),
            P("batch", "label", None),
            P("batch", "tm"),
            P("batch", "label"),
            P("batch"),
            P("batch"),
        ),
        out_specs=(P("batch", "tm", "label"), P("batch", "tm", "label"), P("batch")),
        check_vma=False,
    )
```
